32 devices in a mesh: ctx: 2 (over core), exp: 4 (over z), tp: 4 (over y, x).
Axes of the slice: x: 2, y: 2, z: 4, core: 2. Of those that a mesh axis runs over, the one named last changes fastest.
Arguments:
- conv_in: bfloat16 [4, 256, 4096], P('exp', 'ctx', 'tp'), may hold values from -6 to 6
- gate_in: bfloat16 [4, 256, 4096], P('exp', 'ctx', 'tp'), may hold values from -6 to 6
- residual: bfloat16 [4, 256, 2048], P('exp', 'ctx'), may hold values from -6 to 6
- conv_weight: float32 [4, 4096], P(None, 'tp'), may hold values from -3 to 3
- conv_bias: float32 [4096], P('tp'), may hold values from -3 to 3
- proj_weight: bfloat16 [4096, 288], P('tp'), may hold values from -0.09375 to 0.09375
- step_weight: bfloat16 [256, 4096], P(None, 'tp'), may hold values from -0.375 to 0.375
- step_bias: float32 [4096], P('tp'), may hold values from -6 to -2
- decay_log: float32 [16, 4096], P(None, 'tp'), may hold values from -3 to 2
- skip_gain: float32 [4096], P('tp'), may hold values from 0.5 to 1.5
- out_weight: bfloat16 [4096, 2048], P('tp'), may hold values from -0.09375 to 0.09375
- norm_gain: float32 [2048], replicated, may hold values from 0.5 to 1.5
- expert_ids: int32 [4, 256, 2], P('exp', 'ctx'), may hold values from 0 to 3, all different within a row; in each aligned block of 128 rows (0 to 127, 128 to 255, ..., all dimensions but the last counted through in order) at most 64 rows name the same one
- route_gates: float32 [4, 256, 2], P('exp', 'ctx'), may hold values from 0.2 to 1
- expert_weight: bfloat16 [4, 3, 2048, 14336], P('exp', None, None, ('ctx', 'tp')), may hold values from -0.125 to 0.125
Outputs:
- layer_out: bfloat16 [4, 256, 2048], P('exp', 'ctx', 'tp')
The draws below stay inside these ranges and needn't reach their ends.
Inputs may be any that keep to these rules, and one draw needn't show every extreme that they name: `expert_ids`: the 2 picks of a token differ. Among the picks of the 128 tokens of one sequence block, no expert is named more than 64 times, and in some block one expert is named exactly 64 times.
All inputs are finite; a program needn't handle non-finite values.
Results may differ from the reference program's by a relative error of at most 0.015.
Values may be sent and summed in bfloat16 or wider, within the bound.
No kernel may reach another device: no remote copies, remote signals or barrier semaphores. Data moves between devices by JAX's collectives and lax.ppermute only.
A program may use at most 128 MiB of HBM per device.

```python
import math
import jax
import jax.numpy as jnp
import numpy as np
from jax import lax

D = 2048
INNER = 4096
STATE = 16
DT_RANK = 256
CONV = 4
FF = 14336
TOP = 2
TOK_DEV = 128
CAP = 64
EXPERTS = 4
SEQS = 4
LEN = 256


def block_levels(own_key, dims, pieces, smallest, top_value):
    def one(axis_at, blocks):
        heights = jax.random.uniform(jax.random.fold_in(jax.random.fold_in(own_key, 6), axis_at), (blocks,), jnp.float32, smallest / len(pieces), top_value / len(pieces))
        return jnp.repeat(jnp.exp(heights), dims[axis_at] // blocks).reshape((-1,) + (1,) * (len(dims) - axis_at - 1))

    loudness = one(*pieces[0])
    for cut in pieces[1:]:
        loudness = loudness * one(*cut)
    return loudness


def assign_block(own_key, own, number, rows, count, top, bound, lean):
    sequence = jax.random.permutation(own_key, count)
    crowded, usual = portions_of(count, rows * top, bound, lean, True), portions_of(count, rows * top, bound, lean, False)
    places = jnp.arange(count)

    def named(lengths, turn):
        used = int((lengths > 0).sum())
        fixed = max(1, used // 4)
        moved = fixed + (places - fixed + turn * (used - fixed)) % max(1, count - fixed)
        return jnp.zeros((count,), jnp.int32).at[sequence[jnp.where(places < fixed, places, moved)]].set(jnp.asarray(lengths, jnp.int32))

    lengths = jnp.where(number % 4 == 0, named(crowded, number // 4), named(usual, number - number // 4 - 1))
    mixed = jax.random.permutation(jax.random.fold_in(own, 3), count)
    source_of, sink = mixed[0:count // 2 * 2:2], mixed[1:count // 2 * 2:2]
    room = jnp.minimum(lengths[source_of] - 1, bound - lengths[sink]) // 2
    room = jnp.where((source_of == sequence[0]) | (sink == sequence[0]) | (lengths[sink] == 0), 0, jnp.maximum(room, 0))
    moved = jax.random.randint(jax.random.fold_in(own, 4), (count // 2,), 0, 1 << 20) % (room + 1)
    lengths = lengths.at[source_of].add(-moved).at[sink].add(moved)
    members = jnp.searchsorted(jnp.cumsum(lengths), jnp.arange(rows * top), side="right").astype(jnp.int32)
    grid = members.reshape(top, rows).T
    grid = grid[jax.random.permutation(jax.random.fold_in(own, 1), rows)]
    turn = jax.random.randint(jax.random.fold_in(own, 2), (rows, 1), 0, top)
    return jnp.take_along_axis(grid, (jnp.arange(top)[None, :] + turn) % top, axis=1)


def portions_of(amount, total, limit, skew, full):
    portions = [(1 << 20) // math.isqrt(grade ** skew) + 1 for grade in range(1, amount + 1)]
    largest = limit if full else min(limit, max(-(-total // amount), total * portions[0] // sum(portions)))
    least = 1 if total - largest >= amount - 1 else 0
    given, surplus = [largest] + [least] * (amount - 1), total - largest - least * (amount - 1)
    while surplus > 0:
        movable = [i for i in range(1, amount) if given[i] < largest] or [i for i in range(1, amount) if given[i] < limit]
        pool, left = sum([portions[i] for i in movable]), surplus
        for i in movable:
            extra = min(limit - given[i], max(1, left * portions[i] // pool), surplus)
            given[i] = given[i] + extra
            surplus = surplus - extra
    return np.array(given)


def centred(own_key, shape, width, limit, pieces=(), kind=jnp.bfloat16):
    level = block_levels(own_key, shape, pieces, -0.22, 0.18) if pieces else 1.0
    array = jax.random.normal(own_key, shape, jnp.float32) * width * level
    return jnp.minimum(jnp.maximum(array, -limit), limit).astype(kind)


def setup_inputs(seed: int = 0) -> dict:
    streams_of = jax.random.split(jax.random.key(seed), 16)
    conv_in = centred(streams_of[0], (SEQS, LEN, INNER), 1.0, 6.0, ((0, 4), (1, 2), (2, 4)))
    gate_in = centred(streams_of[1], (SEQS, LEN, INNER), 1.0, 6.0, ((0, 4), (1, 2), (2, 4)))
    residual = centred(streams_of[2], (SEQS, LEN, D), 1.0, 6.0, ((0, 4), (1, 2)))
    conv_weight = centred(streams_of[3], (CONV, INNER), CONV ** -0.5, 3.0, ((1, 4),), jnp.float32)
    conv_bias = centred(streams_of[4], (INNER,), 0.5, 3.0, ((0, 4),), jnp.float32)
    proj_weight = centred(streams_of[5], (INNER, DT_RANK + 2 * STATE), INNER ** -0.5, 0.09375, ((0, 4),))
    step_weight = centred(streams_of[6], (DT_RANK, INNER), DT_RANK ** -0.5, 0.375, ((1, 4),))
    step_bias = jnp.clip(-6.0 + 4.0 * jax.random.uniform(streams_of[7], (INNER,), jnp.float32) ** block_levels(streams_of[7], (INNER,), ((0, 4),), -0.2, 0.2), -6.0, -2.0)
    decay_log = jnp.clip(-3.0 + 5.0 * jax.random.uniform(streams_of[8], (STATE, INNER), jnp.float32) ** block_levels(streams_of[8], (STATE, INNER), ((1, 4),), -0.2, 0.2), -3.0, 2.0)
    skip_gain = jnp.clip(0.5 + 1.0 * jax.random.uniform(streams_of[9], (INNER,), jnp.float32) ** block_levels(streams_of[9], (INNER,), ((0, 4),), -0.2, 0.2), 0.5, 1.5)
    out_weight = centred(streams_of[10], (INNER, D), INNER ** -0.5, 0.09375, ((0, 4),))
    norm_gain = jnp.clip(1.0 + 0.1 * jax.random.normal(streams_of[11], (D,), jnp.float32), 0.5, 1.5)
    expert_ids_keys = jax.random.split(jax.random.fold_in(streams_of[12], 1), SEQS * LEN // TOK_DEV)
    expert_ids_turns = jax.random.permutation(jax.random.fold_in(streams_of[12], 3), SEQS * LEN // TOK_DEV)
    expert_ids = jax.vmap(lambda own, number: assign_block(jax.random.fold_in(streams_of[12], 2), own, number, TOK_DEV, EXPERTS, TOP, CAP, 2))(expert_ids_keys, expert_ids_turns).reshape((SEQS, LEN, TOP))
    route_gates = jnp.clip(0.2 + 0.8 * jax.random.uniform(streams_of[13], (SEQS, LEN, TOP), jnp.float32) ** block_levels(streams_of[13], (SEQS, LEN, TOP), ((0, 4), (1, 2)), -0.2, 0.2), 0.2, 1.0)
    expert_weight = centred(streams_of[14], (EXPERTS, 3, D, FF), D ** -0.5, 0.125, ((0, 4), (3, 8)))
    return dict(conv_in=conv_in, gate_in=gate_in, residual=residual, conv_weight=conv_weight, conv_bias=conv_bias, proj_weight=proj_weight, step_weight=step_weight, step_bias=step_bias, decay_log=decay_log, skip_gain=skip_gain, out_weight=out_weight, norm_gain=norm_gain, expert_ids=expert_ids, route_gates=route_gates, expert_weight=expert_weight)


def reference(conv_in, gate_in, residual, conv_weight, conv_bias, proj_weight, step_weight, step_bias, decay_log, skip_gain, out_weight, norm_gain, expert_ids, route_gates, expert_weight):
    highest = lax.Precision.HIGHEST
    seq_count = conv_in.shape[0]
    seq_length = conv_in.shape[1]
    padded = jnp.pad(conv_in.astype(jnp.float32), ((0, 0), (CONV - 1, 0), (0, 0)))
    convolved = conv_bias[None, None, :] + sum((conv_weight[k][None, None, :] * padded[:, k:k + seq_length] for k in range(CONV)))
    xconv = jax.nn.silu(convolved).astype(jnp.bfloat16)
    projected = jnp.dot(xconv.reshape(seq_count * seq_length, INNER), proj_weight, preferred_element_type=jnp.float32)
    projected = projected.reshape(seq_count, seq_length, DT_RANK + 2 * STATE)
    rank_part = projected[..., :DT_RANK].astype(jnp.bfloat16)
    input_map = projected[..., DT_RANK:DT_RANK + STATE]
    output_map = projected[..., DT_RANK + STATE:]
    step_sizes = jnp.dot(rank_part.reshape(seq_count * seq_length, DT_RANK), step_weight, preferred_element_type=jnp.float32)
    step_sizes = jax.nn.softplus(step_sizes.reshape(seq_count, seq_length, INNER) + step_bias)
    decay_rates = -jnp.exp(decay_log)
    xfloat = xconv.astype(jnp.float32)

    def advance(state, inputs):
        step_now, value_now, in_now, out_now = inputs
        state = jnp.exp(step_now[:, None, :] * decay_rates[None]) * state + (step_now * value_now)[:, None, :] * in_now[:, :, None]
        return (state, jnp.einsum('sn,snc->sc', out_now, state, precision=highest))
    initial = jnp.zeros((seq_count, STATE, INNER), jnp.float32)
    _, scanned = lax.scan(advance, initial, (jnp.swapaxes(step_sizes, 0, 1), jnp.swapaxes(xfloat, 0, 1), jnp.swapaxes(input_map, 0, 1), jnp.swapaxes(output_map, 0, 1)))
    outputs = jnp.swapaxes(scanned, 0, 1) + skip_gain * xfloat
    gated = (outputs * jax.nn.silu(gate_in.astype(jnp.float32))).astype(jnp.bfloat16)
    mixed = jnp.dot(gated.reshape(seq_count * seq_length, INNER), out_weight, preferred_element_type=jnp.float32)
    stream = (residual.reshape(seq_count * seq_length, D).astype(jnp.float32) + mixed).astype(jnp.bfloat16)
    sfloat = stream.astype(jnp.float32)
    meansq = lax.optimization_barrier(jnp.mean(sfloat * sfloat, axis=1, keepdims=True))
    normed = (sfloat * lax.rsqrt(meansq + 1e-06) * norm_gain).astype(jnp.bfloat16)
    block_count = seq_count * seq_length // TOK_DEV
    picks = expert_ids.reshape(block_count, TOK_DEV, TOP)
    onehot = (picks[..., None] == jnp.arange(EXPERTS, dtype=jnp.int32)).astype(jnp.int32)
    flat_hot = onehot.reshape(block_count, TOK_DEV * TOP, EXPERTS)
    ranks = jnp.cumsum(flat_hot, axis=1) - 1
    within = lax.optimization_barrier(jnp.sum(ranks * flat_hot, axis=2)).reshape(block_count, TOK_DEV, TOP)
    places = picks * CAP + within
    table = (places[..., None] == jnp.arange(EXPERTS * CAP, dtype=jnp.int32)).astype(jnp.float32)
    chooser = lax.optimization_barrier(jnp.sum(table, axis=2))
    blender = lax.optimization_barrier(jnp.sum(table * route_gates.reshape(block_count, TOK_DEV, TOP)[..., None], axis=2))
    buffers = jnp.einsum('btm,btd->bmd', chooser, normed.reshape(block_count, TOK_DEV, D).astype(jnp.float32), precision=highest).astype(jnp.bfloat16)
    grouped = jnp.swapaxes(buffers.reshape(block_count, EXPERTS, CAP, D), 0, 1).reshape(EXPERTS, block_count * CAP, D)

    def expert(inputs):
        rows_in, weights = inputs
        gate_part = jnp.dot(rows_in, weights[0], preferred_element_type=jnp.float32)
        up_part = jnp.dot(rows_in, weights[1], preferred_element_type=jnp.float32)
        hidden = (jax.nn.silu(gate_part) * up_part).astype(jnp.bfloat16)
        return lax.dot_general(hidden, weights[2], (((1,), (1,)), ((), ())), preferred_element_type=jnp.float32).astype(jnp.bfloat16)
    results = lax.map(expert, (grouped, expert_weight))
    back = jnp.swapaxes(results.reshape(EXPERTS, block_count, CAP, D), 0, 1).reshape(block_count, EXPERTS * CAP, D)
    moe = jnp.einsum('btm,bmd->btd', blender, back.astype(jnp.float32), precision=highest)
    final = (sfloat.reshape(block_count, TOK_DEV, D) + moe).astype(jnp.bfloat16)
    return final.reshape(seq_count, seq_length, D)
```

```python
import functools
import math

import jax
import jax.numpy as jnp
from jax import lax
from jax.experimental import pallas as pl
from jax.experimental.pallas import tpu as pltpu
from jax.sharding import PartitionSpec as P

STATE = 16
DT_RANK = 256
CAP = 64
LOG2E = math.log2(math.e)
VMEM_LIMIT = 50 * 1024 * 1024
F32 = jnp.float32
BF16 = jnp.bfloat16


def params():
    return pltpu.CompilerParams(vmem_limit_bytes=VMEM_LIMIT)


def whole():
    return pl.BlockSpec(memory_space=pltpu.VMEM)


def shaped(shape, dtype):
    return jax.ShapeDtypeStruct(shape, dtype)


def swap(block, axis, k):
    return lax.ppermute(block, axis, [(i, i ^ k) for i in range(lax.axis_size(axis))])


def sigmoid(x):
    return 1.0 / (1.0 + jnp.exp2(x * -LOG2E))


def route_kernel(ids_ref, first_ref, second_ref, chooser_ref):
    rows, slots = first_ref.shape
    own = lax.axis_index("exp")
    ids = ids_ref[...]
    lanes = lax.broadcasted_iota(jnp.int32, (rows, 128), 1)
    hot = [(ids[:, i : i + 1] == lanes).astype(F32) for i in range(2)]
    earlier = lax.broadcasted_iota(jnp.int32, (rows, rows), 1) < lax.broadcasted_iota(
        jnp.int32, (rows, rows), 0
    )
    ranks = jnp.dot(
        earlier.astype(F32).astype(BF16), (hot[0] + hot[1]).astype(BF16), preferred_element_type=F32
    )
    places = lax.broadcasted_iota(jnp.int32, (rows, slots), 1)
    tables = []
    for i in range(2):
        slot = jnp.sum(ranks * hot[i], axis=1, keepdims=True).astype(jnp.int32)
        place = jnp.bitwise_xor(ids[:, i : i + 1], own) * CAP + slot
        tables.append((place == places).astype(F32))
    first_ref[...] = tables[0].astype(BF16)
    second_ref[...] = tables[1].astype(BF16)
    chooser_ref[...] = jnp.transpose(tables[0] + tables[1]).astype(BF16)


def route(ids, expert_count):
    rows, slots = ids.shape[0], expert_count * CAP
    return pl.pallas_call(
        route_kernel,
        out_shape=(
            shaped((rows, slots), BF16),
            shaped((rows, slots), BF16),
            shaped((slots, rows), BF16),
        ),
        in_specs=[whole()],
        out_specs=[whole()] * 3,
        compiler_params=params(),
        name="route",
    )(ids)


def conv_kernel(halo_ref, x_ref, taps_ref, bias_ref, weight_ref, xconv_ref, part_ref, ext_ref):
    rows = x_ref.shape[0]
    halo = halo_ref.shape[0]
    count = taps_ref.shape[0]
    ext_ref[:halo, :] = halo_ref[...].astype(F32)
    ext_ref[halo:, :] = x_ref[...].astype(F32)
    total = bias_ref[...] + taps_ref[count - 1 : count, :] * ext_ref[halo:, :]
    for k in range(count - 1):
        start = halo - (count - 1) + k
        total = total + taps_ref[k : k + 1, :] * ext_ref[start : start + rows, :]
    xconv = (total * sigmoid(total)).astype(BF16)
    xconv_ref[...] = xconv
    part_ref[...] = jnp.dot(xconv, weight_ref[...], preferred_element_type=F32).astype(BF16)


def conv(halo, x, taps, bias, weight):
    rows, channels = x.shape
    return pl.pallas_call(
        conv_kernel,
        out_shape=(shaped((rows, channels), BF16), shaped((rows, weight.shape[1]), BF16)),
        in_specs=[whole()] * 5,
        out_specs=[whole()] * 2,
        scratch_shapes=[pltpu.VMEM((halo.shape[0] + rows, channels), F32)],
        compiler_params=params(),
        name="conv",
    )(halo, x, taps, bias, weight)


def scan_kernel(parts, *refs):
    part_refs = refs[:parts]
    xconv_ref, weight_ref, bias_ref, decay_ref, skip_ref = refs[parts : parts + 5]
    y_ref, elapsed_ref, rates_ref, maps_ref, state_ref = refs[parts + 5 : parts + 10]
    steps_ref, x_ref, tall_ref, scalars, sem = refs[parts + 10 :]
    rows, channels = xconv_ref.shape
    tiles = channels // 128
    proj = part_refs[0][...].astype(F32)
    for ref in part_refs[1:]:
        proj = proj + ref[...].astype(F32)
    maps_ref[...] = proj[:, DT_RANK:]
    copy = pltpu.make_async_copy(maps_ref, scalars, sem)
    copy.start()
    rank = proj[:, :DT_RANK].astype(BF16)
    raw = jnp.dot(rank, weight_ref[...], preferred_element_type=F32) + bias_ref[...]
    steps = jnp.maximum(raw, 0.0) + jnp.log1p(jnp.exp(-jnp.abs(raw)))
    xfloat = xconv_ref[...].astype(F32)
    rates = -LOG2E * jnp.exp(decay_ref[...])
    skip = skip_ref[...]
    for j in range(tiles):
        cut = slice(j * 128, (j + 1) * 128)
        steps_ref[:, j, :] = steps[:, cut]
        x_ref[:, j, :] = xfloat[:, cut]
        rates_ref[:, j, :] = rates[:, cut]
        tall_ref[j : j + 1, :] = skip[:, cut]
    copy.wait()
    gain = tall_ref[...]

    def step(t, carry):
        elapsed, states = carry
        now = steps_ref[t]
        x = x_ref[t]
        driven = now * x
        sums = [gain * x, None]
        new = []
        for n in range(STATE):
            state = jnp.exp2(now * rates_ref[n]) * states[n] + driven * scalars[t, n]
            new.append(state)
            term = state * scalars[t, STATE + n]
            sums[n % 2] = term if sums[n % 2] is None else sums[n % 2] + term
        elapsed = elapsed + now
        y_ref[t] = sums[0] + sums[1]
        elapsed_ref[t] = elapsed
        return elapsed, tuple(new)

    zero = jnp.zeros((tiles, 128), F32)
    _, states = lax.fori_loop(0, rows, step, (zero, (zero,) * STATE), unroll=4)
    for n in range(STATE):
        state_ref[n] = states[n]


def scan(pieces, xconv, weight, bias, decay_log, skip):
    rows, channels = xconv.shape
    tiles = channels // 128
    return pl.pallas_call(
        functools.partial(scan_kernel, len(pieces)),
        out_shape=(
            shaped((rows, tiles, 128), F32),
            shaped((rows, tiles, 128), F32),
            shaped((STATE, tiles, 128), F32),
            shaped((rows, 2 * STATE), F32),
            shaped((STATE, tiles, 128), F32),
        ),
        in_specs=[whole()] * (len(pieces) + 5),
        out_specs=[whole()] * 5,
        scratch_shapes=[
            pltpu.VMEM((rows, tiles, 128), F32),
            pltpu.VMEM((rows, tiles, 128), F32),
            pltpu.VMEM((tiles, 128), F32),
            pltpu.SMEM((rows, 2 * STATE), F32),
            pltpu.SemaphoreType.DMA,
        ],
        compiler_params=params(),
        name="scan",
    )(*pieces, xconv, weight, bias, decay_log, skip)


def mix_kernel(parts, *refs):
    maps, y_ref, elapsed_ref, rates_ref, state_ref, gate_ref, residual_ref, weight_hbm = refs[:8]
    own_ref, sent = refs[8], refs[9 : 8 + parts]
    sum_ref, gated_ref, weight_ref, sem = refs[8 + parts :]
    copy = pltpu.make_async_copy(weight_hbm, weight_ref, sem)
    copy.start()
    rows, tiles, _ = y_ref.shape

    def step(t, carry):
        elapsed = elapsed_ref[t]
        sums = [y_ref[t], None]
        for n in range(STATE):
            term = jnp.exp2(elapsed * rates_ref[n]) * state_ref[n] * maps[t, STATE + n]
            sums[n % 2] = term if sums[n % 2] is None else sums[n % 2] + term
        sum_ref[t] = sums[0] + sums[1]
        return carry

    lax.fori_loop(0, rows, step, 0, unroll=4)
    for j in range(tiles):
        cut = slice(j * 128, (j + 1) * 128)
        gate = gate_ref[:, cut].astype(F32)
        gated_ref[:, cut] = (sum_ref[:, j, :] * (gate * sigmoid(gate))).astype(BF16)
    copy.wait()
    own = lax.axis_index("tp")
    width = own_ref.shape[1]
    for k in range(parts):
        start = pl.multiple_of(jnp.bitwise_xor(own, k) * width, 128)
        product = jnp.dot(
            gated_ref[...], weight_ref[:, pl.ds(start, width)], preferred_element_type=F32
        )
        if k == 0:
            own_ref[...] = product + residual_ref[:, pl.ds(start, width)].astype(F32)
        else:
            sent[k - 1][...] = product.astype(BF16)


def mix(parts, maps, y, elapsed, rates, state, gate, residual, weight):
    rows, tiles, _ = y.shape
    width = weight.shape[1] // parts
    return pl.pallas_call(
        functools.partial(mix_kernel, parts),
        out_shape=[shaped((rows, width), F32)] + [shaped((rows, width), BF16)] * (parts - 1),
        in_specs=[pl.BlockSpec(memory_space=pltpu.SMEM)]
        + [whole()] * 6
        + [pl.BlockSpec(memory_space=pl.ANY)],
        out_specs=[whole()] * parts,
        scratch_shapes=[
            pltpu.VMEM((rows, tiles, 128), F32),
            pltpu.VMEM((rows, tiles * 128), BF16),
            pltpu.VMEM(weight.shape, BF16),
            pltpu.SemaphoreType.DMA,
        ],
        compiler_params=params(),
        name="mix",
    )(maps, y, elapsed, rates, state, gate, residual, weight)


def pick_kernel(parts, *refs):
    own_ref, arrived, chooser_ref = refs[0], refs[1:parts], refs[parts]
    stream_ref, out_refs = refs[parts + 1], refs[parts + 2 :]
    total = own_ref[...]
    for ref in arrived:
        total = total + ref[...].astype(F32)
    stream = total.astype(BF16)
    stream_ref[...] = stream
    picked = jnp.dot(chooser_ref[...], stream, preferred_element_type=F32).astype(BF16)
    for j, ref in enumerate(out_refs):
        ref[...] = picked[j * CAP : (j + 1) * CAP, :]


def pick(own, arrived, chooser):
    rows, width = own.shape
    experts = chooser.shape[0] // CAP
    return pl.pallas_call(
        functools.partial(pick_kernel, 1 + len(arrived)),
        out_shape=[shaped((rows, width), BF16)] + [shaped((CAP, width), BF16)] * experts,
        in_specs=[whole()] * (2 + len(arrived)),
        out_specs=[whole()] * (1 + experts),
        compiler_params=params(),
        name="pick",
    )(own, *arrived, chooser)


def expert_kernel(parts, *refs):
    x_refs = refs[: 2 * parts]
    gain_ref, gate_ref, up_ref, down_ref = refs[2 * parts : 2 * parts + 4]
    own_refs = refs[2 * parts + 4 : 3 * parts + 4]
    other_refs = refs[3 * parts + 4 : 4 * parts + 4]
    x_ref, acc_ref = refs[4 * parts + 4 :]
    half, width = x_refs[0].shape
    own = lax.axis_index("tp")
    block = pl.program_id(0)
    starts = [pl.multiple_of(jnp.bitwise_xor(own, k) * width, 128) for k in range(parts)]

    @pl.when(block == 0)
    def _():
        for core in range(2):
            pieces = [ref[...].astype(F32) for ref in x_refs[core * parts : (core + 1) * parts]]
            total = sum(jnp.sum(piece * piece, axis=1, keepdims=True) for piece in pieces)
            scale = lax.rsqrt(total / (width * parts) + 1e-6)
            for piece, start in zip(pieces, starts):
                gain = gain_ref[:, pl.ds(start, width)]
                x_ref[core * half : (core + 1) * half, pl.ds(start, width)] = (
                    piece * scale * gain
                ).astype(BF16)

    x = x_ref[...]
    gate = jnp.dot(x, gate_ref[0, 0], preferred_element_type=F32)
    up = jnp.dot(x, up_ref[0, 0], preferred_element_type=F32)
    hidden = (gate * sigmoid(gate) * up).astype(BF16)
    product = lax.dot_general(
        hidden, down_ref[0, 0], (((1,), (1,)), ((), ())), preferred_element_type=F32
    )

    @pl.when(block == 0)
    def _():
        acc_ref[...] = product

    @pl.when(block > 0)
    def _():
        acc_ref[...] += product

    @pl.when(block == pl.num_programs(0) - 1)
    def _():
        for k, start in enumerate(starts):
            own_refs[k][...] = acc_ref[:half, pl.ds(start, width)].astype(own_refs[k].dtype)
            other_refs[k][...] = acc_ref[half:, pl.ds(start, width)].astype(BF16)


def expert(own_rows, other_rows, gain, weights):
    parts = len(own_rows)
    half, width = own_rows[0].shape
    model, hidden = weights.shape[2:]
    size = 256 if hidden % 256 == 0 else hidden
    fixed = pl.BlockSpec((half, width), lambda b: (0, 0))

    def weight_spec(which):
        return pl.BlockSpec((1, 1, model, size), lambda b: (0, which, 0, b))

    return pl.pallas_call(
        functools.partial(expert_kernel, parts),
        grid=(hidden // size,),
        out_shape=[shaped((half, width), F32)] * parts + [shaped((half, width), BF16)] * parts,
        in_specs=[fixed] * (2 * parts)
        + [pl.BlockSpec((1, model), lambda b: (0, 0))]
        + [weight_spec(i) for i in range(3)],
        out_specs=[fixed] * (2 * parts),
        scratch_shapes=[pltpu.VMEM((2 * half, model), BF16), pltpu.VMEM((2 * half, model), F32)],
        compiler_params=params(),
        name="expert",
    )(*own_rows, *other_rows, gain, weights, weights, weights)


def total_kernel(parts, *refs):
    total = refs[0][...].astype(F32)
    for ref in refs[1:parts]:
        total = total + ref[...].astype(F32)
    total = total.astype(BF16)
    for j, ref in enumerate(refs[parts:]):
        ref[...] = total[j * CAP : (j + 1) * CAP, :]


def totals(pieces):
    rows, width = pieces[0].shape
    experts = rows // CAP
    return pl.pallas_call(
        functools.partial(total_kernel, len(pieces)),
        out_shape=[shaped((CAP, width), BF16)] * experts,
        in_specs=[whole()] * len(pieces),
        out_specs=[whole()] * experts,
        compiler_params=params(),
        name="totals",
    )(*pieces)


def blend_kernel(experts, *refs):
    back = refs[:experts]
    stream_ref, first_ref, second_ref, gates_ref, out_ref, rows_ref = refs[experts:]
    for j, ref in enumerate(back):
        rows_ref[j * CAP : (j + 1) * CAP, :] = ref[...]
    rows = rows_ref[...]
    gates = gates_ref[...]
    moe = gates[:, 0:1] * jnp.dot(first_ref[...], rows, preferred_element_type=F32)
    moe = moe + gates[:, 1:2] * jnp.dot(second_ref[...], rows, preferred_element_type=F32)
    out_ref[...] = (stream_ref[...].astype(F32) + moe).astype(BF16)


def blend(back, stream, first, second, gates):
    experts, width = len(back), stream.shape[1]
    return pl.pallas_call(
        functools.partial(blend_kernel, experts),
        out_shape=shaped(stream.shape, BF16),
        in_specs=[whole()] * (experts + 4),
        out_specs=whole(),
        scratch_shapes=[pltpu.VMEM((experts * CAP, width), BF16)],
        compiler_params=params(),
        name="blend",
    )(*back, stream, first, second, gates)


def body(
    conv_in,
    gate_in,
    residual,
    conv_weight,
    conv_bias,
    proj_weight,
    step_weight,
    step_bias,
    decay_log,
    skip_gain,
    out_weight,
    norm_gain,
    expert_ids,
    route_gates,
    expert_weight,
):
    tp, experts = lax.axis_size("tp"), lax.axis_size("exp")
    local = conv_in[0]
    halo = lax.ppermute(local[-16:], "ctx", [(0, 1)])
    first, second, chooser = route(expert_ids[0], experts)
    xconv, part = conv(halo, local, conv_weight, conv_bias[None], proj_weight)
    parts = [part] + [swap(part, "tp", k) for k in range(1, tp)]
    y, elapsed, rates, maps, state = scan(
        parts, xconv, step_weight, step_bias[None], decay_log, skip_gain[None]
    )
    before = lax.ppermute(state, "ctx", [(0, 1)])
    own, *sent = mix(tp, maps, y, elapsed, rates, before, gate_in[0], residual[0], out_weight)
    arrived = [swap(piece, "tp", k) for k, piece in enumerate(sent, 1)]
    stream, *picked = pick(own, arrived, chooser)
    rows = jnp.concatenate(
        [picked[0]] + [swap(picked[j], "exp", j) for j in range(1, experts)], axis=0
    )
    own_rows = [rows] + [swap(rows, "tp", k) for k in range(1, tp)]
    other_rows = [swap(piece, "ctx", 1) for piece in own_rows]
    made = expert(own_rows, other_rows, norm_gain[None], expert_weight)
    summed = []
    for k in range(tp):
        piece = made[k] + swap(made[tp + k], "ctx", 1).astype(F32)
        summed.append(piece if k == 0 else swap(piece.astype(BF16), "tp", k))
    results = totals(summed)
    back = [results[0]] + [swap(results[j], "exp", j) for j in range(1, experts)]
    return blend(back, stream, first, second, route_gates[0])[None]


def solution(mesh):
    placed = (
        P("exp", "ctx", "tp"),
        P("exp", "ctx", "tp"),
        P("exp", "ctx", None),
        P(None, "tp"),
        P("tp"),
        P("tp", None),
        P(None, "tp"),
        P("tp"),
        P(None, "tp"),
        P("tp"),
        P("tp", None),
        P(),
        P("exp", "ctx", None),
        P("exp", "ctx", None),
        P("exp", None, None, ("ctx", "tp")),
    )
    return jax.shard_map(
        body, mesh=mesh, in_specs=placed, out_specs=P("exp", "ctx", "tp"), check_vma=False
    )
```

```python
import functools
import math

import jax
import jax.numpy as jnp
from jax import lax
from jax.experimental import pallas as pl
from jax.experimental.pallas import tpu as pltpu
from jax.sharding import PartitionSpec as P

STATE = 16
DT_RANK = 256
CAP = 64
LOG2E = math.log2(math.e)
VMEM_LIMIT = 20 * 1024 * 1024
F32 = jnp.float32
BF16 = jnp.bfloat16


def params():
    return pltpu.CompilerParams(vmem_limit_bytes=VMEM_LIMIT)


def whole():
    return pl.BlockSpec(memory_space=pltpu.VMEM)


def shaped(shape, dtype):
    return jax.ShapeDtypeStruct(shape, dtype)


def swap(block, axis, k):
    return lax.ppermute(block, axis, [(i, i ^ k) for i in range(lax.axis_size(axis))])


def sigmoid(x):
    return 1.0 / (1.0 + jnp.exp2(x * -LOG2E))


def stay(array):
    return pltpu.with_memory_space_constraint(array, pltpu.HBM)


def hbm():
    return pl.BlockSpec(memory_space=pltpu.HBM)


def unread(arrays):
    return [pl.BlockSpec(memory_space=pl.ANY)] * len(arrays)


def stack_kernel(count, *refs):
    for j, ref in enumerate(refs[:count]):
        rows = ref.shape[0]
        refs[-1][j * rows : (j + 1) * rows, :] = ref[...]


def stack(pieces, after):
    rows, width = pieces[0].shape
    return pl.pallas_call(
        functools.partial(stack_kernel, len(pieces)),
        out_shape=shaped((rows * len(pieces), width), pieces[0].dtype),
        in_specs=[whole()] * len(pieces) + unread(after),
        out_specs=whole(),
        compiler_params=params(),
        cost_estimate=cost(1e6, 0),
        name="stack",
    )(*pieces, *after)


def order_kernel(*refs):
    refs[-1][...] = jnp.zeros_like(refs[-1])


def order(after):
    return pl.pallas_call(
        order_kernel,
        out_shape=shaped((8, 128), F32),
        in_specs=unread(after),
        out_specs=whole(),
        compiler_params=params(),
        cost_estimate=cost(2e10, 0),
        name="order",
    )(*after)


def cost(flops, loaded=0):
    return pl.CostEstimate(flops=int(flops), bytes_accessed=int(loaded), transcendentals=0)


def route_kernel(ids_ref, first_ref, second_ref, chooser_ref):
    rows, slots = first_ref.shape
    own = lax.axis_index("exp")
    ids = jnp.transpose(ids_ref[...].astype(F32)).astype(jnp.int32)
    lanes = lax.broadcasted_iota(jnp.int32, (rows, 128), 1)
    hot = [(ids[:, i : i + 1] == lanes).astype(F32) for i in range(2)]
    earlier = lax.broadcasted_iota(jnp.int32, (rows, rows), 1) < lax.broadcasted_iota(
        jnp.int32, (rows, rows), 0
    )
    ranks = jnp.dot(
        earlier.astype(F32).astype(BF16), (hot[0] + hot[1]).astype(BF16), preferred_element_type=F32
    )
    places = lax.broadcasted_iota(jnp.int32, (rows, slots), 1)
    tables = []
    for i in range(2):
        slot = jnp.sum(ranks * hot[i], axis=1, keepdims=True).astype(jnp.int32)
        place = jnp.bitwise_xor(ids[:, i : i + 1], own) * CAP + slot
        tables.append((place == places).astype(F32))
    first_ref[...] = tables[0].astype(BF16)
    second_ref[...] = tables[1].astype(BF16)
    chooser_ref[...] = jnp.transpose(tables[0] + tables[1]).astype(BF16)


def route(ids, expert_count):
    rows, slots = ids.shape[1], expert_count * CAP
    return pl.pallas_call(
        route_kernel,
        out_shape=(
            shaped((rows, slots), BF16),
            shaped((rows, slots), BF16),
            shaped((slots, rows), BF16),
        ),
        in_specs=[whole()],
        out_specs=[whole()] * 3,
        compiler_params=params(),
        cost_estimate=cost(1e6, 1e6),
        name="route",
    )(ids)


def conv_kernel(
    halo_hbm, x_hbm, taps_hbm, bias_hbm, weight_hbm, xconv_ref, part_ref,
    ext_ref, halo_ref, x_ref, taps_ref, bias_ref, weight_ref, sems,
):
    rows = x_ref.shape[0]
    halo = halo_ref.shape[0]
    count = taps_ref.shape[0]
    copies = [
        pltpu.make_async_copy(source, target, sems.at[i])
        for i, (source, target) in enumerate(
            (
                (halo_hbm.at[rows - halo :], halo_ref),
                (x_hbm, x_ref),
                (taps_hbm, taps_ref),
                (bias_hbm, bias_ref),
                (weight_hbm, weight_ref),
            )
        )
    ]
    for copy in copies:
        copy.start()
    for copy in copies[:4]:
        copy.wait()
    ext_ref[:halo, :] = halo_ref[...].astype(F32)
    ext_ref[halo:, :] = x_ref[...].astype(F32)
    total = bias_ref[...] + taps_ref[count - 1 : count, :] * ext_ref[halo:, :]
    for k in range(count - 1):
        start = halo - (count - 1) + k
        total = total + taps_ref[k : k + 1, :] * ext_ref[start : start + rows, :]
    xconv = (total * sigmoid(total)).astype(BF16)
    xconv_ref[...] = xconv
    copies[4].wait()
    part_ref[...] = lax.dot_general(
        xconv, weight_ref[...], (((1,), (1,)), ((), ())), preferred_element_type=F32
    ).astype(BF16)


def conv(before, x, taps, bias, weight):
    rows, channels = x.shape
    return pl.pallas_call(
        conv_kernel,
        out_shape=(shaped((rows, channels), BF16), shaped((rows, weight.shape[0]), BF16)),
        in_specs=[hbm()] * 5,
        out_specs=[whole()] * 2,
        scratch_shapes=[
            pltpu.VMEM((16 + rows, channels), F32),
            pltpu.VMEM((16, channels), BF16),
            pltpu.VMEM((rows, channels), BF16),
            pltpu.VMEM(taps.shape, F32),
            pltpu.VMEM(bias.shape, F32),
            pltpu.VMEM(weight.shape, BF16),
            pltpu.SemaphoreType.DMA((5,)),
        ],
        compiler_params=params(),
        name="conv",
    )(before, x, taps, bias, weight)


def prepare_kernel(
    xconv_ref, gate_hbm, decay_hbm, skip_hbm, bias_hbm, step_hbm, out_hbm, residual_hbm, gain_hbm, expert_hbm,
    x_ref, silu_ref, rates_ref, skip_ref, bias_ref, step_ref, out_ref, quarter_ref, gain_ref, first_ref,
    gate_ref, decay_ref, flat_ref, residual_ref, sems,
):
    copies = [
        pltpu.make_async_copy(source, target, sems.at[i])
        for i, (source, target) in enumerate(
            (
                (gate_hbm, gate_ref),
                (decay_hbm, decay_ref),
                (skip_hbm, flat_ref),
                (residual_hbm, residual_ref),
                (bias_hbm, bias_ref),
                (gain_hbm, gain_ref),
                (step_hbm, step_ref),
                (out_hbm, out_ref),
                (expert_hbm.at[0, 0], first_ref),
            )
        )
    ]
    for copy in copies:
        copy.start()
    tiles = x_ref.shape[1]
    xfloat = xconv_ref[...].astype(F32)
    for j in range(tiles):
        x_ref[:, j, :] = xfloat[:, j * 128 : (j + 1) * 128]
    for copy in copies[:4]:
        copy.wait()
    gate = gate_ref[...].astype(F32)
    silu_ref[...] = gate * sigmoid(gate)
    rates = -LOG2E * jnp.exp(decay_ref[...])
    for j in range(tiles):
        cut = slice(j * 128, (j + 1) * 128)
        rates_ref[:, j, :] = rates[:, cut]
        skip_ref[j : j + 1, :] = flat_ref[:, cut]
    width = quarter_ref.shape[1]
    start = pl.multiple_of(lax.axis_index("tp") * width, 128)
    quarter_ref[...] = residual_ref[:, pl.ds(start, width)].astype(F32)
    for copy in copies[4:]:
        copy.wait()


def prepare(parts, xconv, gate, decay_log, skip, bias, step_weight, out_weight, residual, gain, experts):
    rows, channels = xconv.shape
    tiles = channels // 128
    return pl.pallas_call(
        prepare_kernel,
        out_shape=(
            shaped((rows, tiles, 128), F32),
            shaped((rows, channels), F32),
            shaped((STATE, tiles, 128), F32),
            shaped((tiles, 128), F32),
            shaped(bias.shape, F32),
            shaped(step_weight.shape, BF16),
            shaped(out_weight.shape, BF16),
            shaped((rows, residual.shape[1] // parts), F32),
            shaped(gain.shape, F32),
            shaped(experts.shape[2:], BF16),
        ),
        in_specs=[whole()] + [hbm()] * 9,
        out_specs=[whole()] * 10,
        scratch_shapes=[
            pltpu.VMEM((rows, channels), BF16),
            pltpu.VMEM(decay_log.shape, F32),
            pltpu.VMEM(skip.shape, F32),
            pltpu.VMEM(residual.shape, BF16),
            pltpu.SemaphoreType.DMA((9,)),
        ],
        compiler_params=params(),
        cost_estimate=cost(1e6, 14e6),
        name="prepare",
    )(xconv, gate, decay_log, skip, bias, step_weight, out_weight, residual, gain, experts)


def scan_kernel(parts, *refs):
    part_refs = refs[:parts]
    x_ref, rates_ref, gain_ref, bias_ref, weight_ref, expert_hbm = refs[parts : parts + 6]
    y_ref, elapsed_ref, maps_ref, state_ref, second_ref = refs[parts + 6 : parts + 11]
    steps_ref, scalars, sem, expert_sem = refs[parts + 11 :]
    rows, tiles, _ = x_ref.shape
    expert_copy = pltpu.make_async_copy(expert_hbm.at[0, 1], second_ref, expert_sem)
    expert_copy.start()
    proj = part_refs[0][...].astype(F32)
    for ref in part_refs[1:]:
        proj = proj + ref[...].astype(F32)
    maps_ref[...] = proj[:, DT_RANK:]
    copy = pltpu.make_async_copy(maps_ref, scalars, sem)
    copy.start()
    rank = proj[:, :DT_RANK].astype(BF16)
    raw = jnp.dot(rank, weight_ref[...], preferred_element_type=F32) + bias_ref[...]
    steps = jnp.maximum(raw, 0.0) + jnp.log1p(jnp.exp(-jnp.abs(raw)))
    for j in range(tiles):
        steps_ref[:, j, :] = steps[:, j * 128 : (j + 1) * 128]
    copy.wait()
    gain = gain_ref[...]

    def step(t, carry):
        elapsed, states = carry
        now = steps_ref[t]
        x = x_ref[t]
        driven = now * x
        sums = [gain * x, None]
        new = []
        for n in range(STATE):
            state = jnp.exp2(now * rates_ref[n]) * states[n] + driven * scalars[t, n]
            new.append(state)
            term = state * scalars[t, STATE + n]
            sums[n % 2] = term if sums[n % 2] is None else sums[n % 2] + term
        elapsed = elapsed + now
        y_ref[t] = sums[0] + sums[1]
        elapsed_ref[t] = elapsed
        return elapsed, tuple(new)

    zero = jnp.zeros((tiles, 128), F32)
    _, states = lax.fori_loop(0, rows, step, (zero, (zero,) * STATE), unroll=4)
    for n in range(STATE):
        state_ref[n] = states[n]
    expert_copy.wait()


def scan(pieces, x, rates, gain, bias, weight, experts):
    rows, tiles, _ = x.shape
    return pl.pallas_call(
        functools.partial(scan_kernel, len(pieces)),
        out_shape=(
            shaped((rows, tiles, 128), F32),
            shaped((rows, tiles, 128), F32),
            shaped((rows, 2 * STATE), F32),
            shaped((STATE, tiles, 128), F32),
            shaped(experts.shape[2:], BF16),
        ),
        in_specs=[whole()] * (len(pieces) + 5) + [hbm()],
        out_specs=[whole()] * 5,
        scratch_shapes=[
            pltpu.VMEM((rows, tiles, 128), F32),
            pltpu.SMEM((rows, 2 * STATE), F32),
            pltpu.SemaphoreType.DMA,
            pltpu.SemaphoreType.DMA,
        ],
        compiler_params=params(),
        cost_estimate=cost(1e6, 14e6),
        name="scan",
    )(*pieces, x, rates, gain, bias, weight, experts)


def mix_kernel(parts, *refs):
    maps_ref, y_ref, elapsed_ref, rates_ref, state_ref, silu_ref, quarter_ref, weight_ref, expert_hbm = refs[:9]
    own_ref, sent, third_ref = refs[9], refs[10 : 9 + parts], refs[9 + parts]
    sum_ref, gated_ref, scalars, sem, expert_sem = refs[10 + parts :]
    copy = pltpu.make_async_copy(maps_ref, scalars, sem)
    copy.start()
    expert_copy = pltpu.make_async_copy(expert_hbm.at[0, 2], third_ref, expert_sem)
    expert_copy.start()
    rows, tiles, _ = y_ref.shape
    copy.wait()

    def step(t, carry):
        elapsed = elapsed_ref[t]
        sums = [y_ref[t], None]
        for n in range(STATE):
            term = jnp.exp2(elapsed * rates_ref[n]) * state_ref[n] * scalars[t, STATE + n]
            sums[n % 2] = term if sums[n % 2] is None else sums[n % 2] + term
        sum_ref[t] = sums[0] + sums[1]
        return carry

    lax.fori_loop(0, rows, step, 0, unroll=4)
    for j in range(tiles):
        cut = slice(j * 128, (j + 1) * 128)
        gated_ref[:, cut] = (sum_ref[:, j, :] * silu_ref[:, cut]).astype(BF16)
    own = lax.axis_index("tp")
    width = own_ref.shape[1]
    for k in range(parts):
        start = pl.multiple_of(jnp.bitwise_xor(own, k) * width, 128)
        product = jnp.dot(
            gated_ref[...], weight_ref[:, pl.ds(start, width)], preferred_element_type=F32
        )
        if k == 0:
            own_ref[...] = product + quarter_ref[...]
        else:
            sent[k - 1][...] = product.astype(BF16)
    expert_copy.wait()


def mix(parts, maps, y, elapsed, rates, state, silu, quarter, weight, experts):
    rows, tiles, _ = y.shape
    width = weight.shape[1] // parts
    return pl.pallas_call(
        functools.partial(mix_kernel, parts),
        out_shape=[shaped((rows, width), F32)]
        + [shaped((rows, width), BF16)] * (parts - 1)
        + [shaped(experts.shape[2:], BF16)],
        in_specs=[whole()] * 8 + [hbm()],
        out_specs=[whole()] * (parts + 1),
        scratch_shapes=[
            pltpu.VMEM((rows, tiles, 128), F32),
            pltpu.VMEM((rows, tiles * 128), BF16),
            pltpu.SMEM(maps.shape, F32),
            pltpu.SemaphoreType.DMA,
            pltpu.SemaphoreType.DMA,
        ],
        compiler_params=params(),
        cost_estimate=cost(1e6, 12e6),
        name="mix",
    )(maps, y, elapsed, rates, state, silu, quarter, weight, experts)


def pick_kernel(parts, *refs):
    own_ref, arrived, chooser_ref = refs[0], refs[1:parts], refs[parts]
    stream_ref, out_refs = refs[parts + 1], refs[parts + 2 :]
    total = own_ref[...]
    for ref in arrived:
        total = total + ref[...].astype(F32)
    stream = total.astype(BF16)
    stream_ref[...] = stream
    picked = jnp.dot(chooser_ref[...], stream, preferred_element_type=F32).astype(BF16)
    for j, ref in enumerate(out_refs):
        ref[...] = picked[j * CAP : (j + 1) * CAP, :]


def pick(own, arrived, chooser):
    rows, width = own.shape
    experts = chooser.shape[0] // CAP
    return pl.pallas_call(
        functools.partial(pick_kernel, 1 + len(arrived)),
        out_shape=[shaped((rows, width), BF16)] + [shaped((CAP, width), BF16)] * experts,
        in_specs=[whole()] * (2 + len(arrived)),
        out_specs=[whole()] * (1 + experts),
        compiler_params=params(),
        cost_estimate=cost(1e6, 1e6),
        name="pick",
    )(own, *arrived, chooser)


def norm_kernel(parts, *refs):
    x_refs, gain_ref, out_ref = refs[:parts], refs[parts], refs[-1]
    width = x_refs[0].shape[1]
    own = lax.axis_index("tp")
    pieces = [ref[...].astype(F32) for ref in x_refs]
    total = sum(jnp.sum(piece * piece, axis=1, keepdims=True) for piece in pieces)
    scale = lax.rsqrt(total / (width * parts) + 1e-6)
    for k, piece in enumerate(pieces):
        start = pl.multiple_of(jnp.bitwise_xor(own, k) * width, 128)
        out_ref[:, pl.ds(start, width)] = (
            piece * scale * gain_ref[:, pl.ds(start, width)]
        ).astype(BF16)


def norm(pieces, gain, after):
    rows, width = pieces[0].shape
    return pl.pallas_call(
        functools.partial(norm_kernel, len(pieces)),
        out_shape=shaped((rows, width * len(pieces)), BF16),
        in_specs=[whole()] * (len(pieces) + 1) + unread(after),
        out_specs=whole(),
        compiler_params=params(),
        cost_estimate=cost(1e6, 1e6),
        name="norm",
    )(*pieces, gain, *after)


def hidden_kernel(x_ref, gate_ref, up_ref, *refs):
    hidden_ref = refs[-1]
    width = gate_ref.shape[1]
    size = 256 if width % 256 == 0 else width
    for i in range(width // size):
        cut = slice(i * size, (i + 1) * size)
        gate = jnp.dot(x_ref[...], gate_ref[:, cut], preferred_element_type=F32)
        up = jnp.dot(x_ref[...], up_ref[:, cut], preferred_element_type=F32)
        hidden_ref[:, cut] = (gate * sigmoid(gate) * up).astype(BF16)


def hidden_units(x, gate, up, after):
    rows, width = x.shape[0], gate.shape[1]
    return pl.pallas_call(
        hidden_kernel,
        out_shape=shaped((rows, width), BF16),
        in_specs=[whole()] * 3 + unread(after),
        out_specs=whole(),
        compiler_params=params(),
        cost_estimate=cost(1e6, 0),
        name="hidden",
    )(x, gate, up, *after)


def down_kernel(hidden_own_ref, hidden_other_ref, down_ref, *refs):
    own_ref, other_ref, hidden_ref = refs[-3:]
    rows = hidden_own_ref.shape[0]
    hidden_ref[:rows, :] = hidden_own_ref[...]
    hidden_ref[rows:, :] = hidden_other_ref[...]
    size = 256
    for i in range(down_ref.shape[0] // size):
        cut = slice(i * size, (i + 1) * size)
        product = lax.dot_general(
            hidden_ref[...], down_ref[cut, :], (((1,), (1,)), ((), ())), preferred_element_type=F32
        )
        own_ref[:, cut] = product[:rows]
        other_ref[:, cut] = product[rows:].astype(BF16)


def down_sums(hidden_own, hidden_other, down, after):
    rows, width = hidden_own.shape
    model = down.shape[0]
    return pl.pallas_call(
        down_kernel,
        out_shape=(shaped((rows, model), F32), shaped((rows, model), BF16)),
        in_specs=[whole()] * 3 + unread(after),
        out_specs=[whole()] * 2,
        scratch_shapes=[pltpu.VMEM((2 * rows, width), BF16)],
        compiler_params=params(),
        cost_estimate=cost(1e6, 0),
        name="down",
    )(hidden_own, hidden_other, down, *after)


def join_kernel(parts, own_ref, other_ref, *refs):
    out_refs = refs[-parts:]
    width = out_refs[0].shape[1]
    own = lax.axis_index("tp")
    for k, ref in enumerate(out_refs):
        cut = pl.ds(pl.multiple_of(jnp.bitwise_xor(own, k) * width, 128), width)
        ref[...] = (own_ref[:, cut] + other_ref[:, cut].astype(F32)).astype(ref.dtype)


def join(parts, own, other, after):
    rows, model = own.shape
    return pl.pallas_call(
        functools.partial(join_kernel, parts),
        out_shape=[shaped((rows, model // parts), BF16 if k else F32) for k in range(parts)],
        in_specs=[whole()] * 2 + unread(after),
        out_specs=[whole()] * parts,
        compiler_params=params(),
        cost_estimate=cost(1e6, 1e6),
        name="join",
    )(own, other, *after)


def total_kernel(parts, *refs):
    total = refs[0][...].astype(F32)
    for ref in refs[1:parts]:
        total = total + ref[...].astype(F32)
    total = total.astype(BF16)
    for j, ref in enumerate(refs[parts:]):
        ref[...] = total[j * CAP : (j + 1) * CAP, :]


def totals(pieces):
    rows, width = pieces[0].shape
    count = rows // CAP
    return pl.pallas_call(
        functools.partial(total_kernel, len(pieces)),
        out_shape=[shaped((CAP, width), BF16)] * count,
        in_specs=[whole()] * len(pieces),
        out_specs=[whole()] * count,
        compiler_params=params(),
        cost_estimate=cost(1e6, 1e6),
        name="totals",
    )(*pieces)


def blend_kernel(experts, *refs):
    back = refs[:experts]
    stream_ref, first_ref, second_ref, gates_ref, out_ref, rows_ref = refs[experts:]
    for j, ref in enumerate(back):
        rows_ref[j * CAP : (j + 1) * CAP, :] = ref[...]
    rows = rows_ref[...]
    gates = jnp.transpose(gates_ref[...])
    moe = gates[:, 0:1] * jnp.dot(first_ref[...], rows, preferred_element_type=F32)
    moe = moe + gates[:, 1:2] * jnp.dot(second_ref[...], rows, preferred_element_type=F32)
    out_ref[...] = (stream_ref[...].astype(F32) + moe).astype(BF16)


def blend(back, stream, first, second, gates):
    experts, width = len(back), stream.shape[1]
    return pl.pallas_call(
        functools.partial(blend_kernel, experts),
        out_shape=shaped(stream.shape, BF16),
        in_specs=[whole()] * (experts + 4),
        out_specs=whole(),
        scratch_shapes=[pltpu.VMEM((experts * CAP, width), BF16)],
        compiler_params=params(),
        name="blend",
    )(*back, stream, first, second, gates)


def expert(tp, x_own, gate, up, down, after_start, after_sums):
    x_other = swap(x_own, "ctx", 1)
    hidden_own = hidden_units(x_own, gate, up, after_start)
    hidden_other = hidden_units(x_other, gate, up, [hidden_own])
    sum_own, sum_other = down_sums(hidden_own, hidden_other, down, [])
    after_sums = [order([sum_other, *after_sums])] if after_sums else []
    joined = join(tp, sum_own, swap(sum_other, "ctx", 1), after_sums)
    return sum_own, joined


def body(
    conv_in,
    gate_in,
    residual,
    conv_weight,
    conv_bias,
    proj_weight,
    step_weight,
    step_bias,
    decay_log,
    skip_gain,
    out_weight,
    norm_gain,
    expert_ids,
    route_gates,
    expert_weight,
):
    tp, experts = lax.axis_size("tp"), lax.axis_size("exp")
    local = conv_in[0]
    before = lax.ppermute(local, "ctx", [(0, 1)])
    expert_weight = stay(expert_weight)
    xconv, part = conv(
        stay(before), stay(local), stay(conv_weight), stay(conv_bias[None]), stay(proj_weight.T)
    )
    parts = [part] + [swap(part, "tp", k) for k in range(1, tp)]
    x, silu, rates, skip, bias, step_w, out_w, quarter, gain, gate_w = prepare(
        tp, xconv, stay(gate_in[0]), stay(decay_log), stay(skip_gain[None]), stay(step_bias[None]),
        stay(step_weight), stay(out_weight), stay(residual[0]), stay(norm_gain[None]), expert_weight,
    )
    y, elapsed, maps, state, up_w = scan(parts, x, rates, skip, bias, step_w, expert_weight)
    before = lax.ppermute(state, "ctx", [(0, 1)])
    own, *sent, down_w = mix(
        tp, maps, y, elapsed, rates, before, silu, quarter, out_w, expert_weight
    )
    arrived = [swap(piece, "tp", k) for k, piece in enumerate(sent, 1)]
    first, second, chooser = route(expert_ids[0].T, experts)
    stream, *picked = pick(own, arrived, chooser)
    rows = [picked[0]] + [swap(picked[j], "exp", j) for j in range(1, experts)]
    piece_a = stack(rows[: experts // 2], [])
    piece_b = stack(rows[experts // 2 :], [piece_a])
    rows_a, rows_b = [piece_a], [piece_b]
    both = order([piece_a, piece_b])
    for k in range(1, tp):
        top = 1 << (k.bit_length() - 1)
        passed = rows_a[k ^ top]
        rows_a.append(swap(passed if k == top else stack([passed], [both]), "tp", top))
        rows_b.append(swap(piece_b, "tp", k))
    x_a = norm(rows_a, gain, [piece_b])
    own_a, joined_a = expert(tp, x_a, gate_w, up_w, down_w, [], [])
    summed_a = [joined_a[0]] + [swap(joined_a[k], "tp", k) for k in range(1, tp)]
    back = totals(summed_a)
    x_b = norm(rows_b, gain, [own_a])
    _, joined_b = expert(tp, x_b, gate_w, up_w, down_w, [joined_a[0]], [back[0]])
    back += totals([joined_b[0]] + [swap(joined_b[k], "tp", k) for k in range(1, tp)])
    back = [back[0]] + [swap(back[j], "exp", j) for j in range(1, experts)]
    return blend(back, stream, first, second, route_gates[0].T)[None]


def solution(mesh):
    placed = (
        P("exp", "ctx", "tp"),
        P("exp", "ctx", "tp"),
        P("exp", "ctx", None),
        P(None, "tp"),
        P("tp"),
        P("tp", None),
        P(None, "tp"),
        P("tp"),
        P(None, "tp"),
        P("tp"),
        P("tp", None),
        P(),
        P("exp", "ctx", None),
        P("exp", "ctx", None),
        P("exp", None, None, ("ctx", "tp")),
    )
    return jax.shard_map(
        body, mesh=mesh, in_specs=placed, out_specs=P("exp", "ctx", "tp"), check_vma=False
    )
```

```python
import functools
import math

import jax
import jax.numpy as jnp
from jax import lax
from jax.experimental import pallas as pl
from jax.experimental.pallas import tpu as pltpu
from jax.sharding import PartitionSpec as P

STATE = 16
DT_RANK = 256
CAP = 64
LOG2E = math.log2(math.e)
VMEM_LIMIT = 20 * 1024 * 1024
F32 = jnp.float32
BF16 = jnp.bfloat16


def params():
    return pltpu.CompilerParams(vmem_limit_bytes=VMEM_LIMIT)


def whole():
    return pl.BlockSpec(memory_space=pltpu.VMEM)


def shaped(shape, dtype):
    return jax.ShapeDtypeStruct(shape, dtype)


def swap(block, axis, k):
    return lax.ppermute(block, axis, [(i, i ^ k) for i in range(lax.axis_size(axis))])


def sigmoid(x):
    return 1.0 / (1.0 + jnp.exp2(x * -LOG2E))


def stay(array):
    return pltpu.with_memory_space_constraint(array, pltpu.HBM)


def hbm():
    return pl.BlockSpec(memory_space=pltpu.HBM)


def unread(arrays):
    return [pl.BlockSpec(memory_space=pl.ANY)] * len(arrays)


def stack_kernel(count, *refs):
    for j, ref in enumerate(refs[:count]):
        rows = ref.shape[0]
        refs[-1][j * rows : (j + 1) * rows, :] = ref[...]


def stack(pieces, after):
    rows, width = pieces[0].shape
    return pl.pallas_call(
        functools.partial(stack_kernel, len(pieces)),
        out_shape=shaped((rows * len(pieces), width), pieces[0].dtype),
        in_specs=[whole()] * len(pieces) + unread(after),
        out_specs=whole(),
        compiler_params=params(),
        cost_estimate=cost(1e6, 0),
        name="stack",
    )(*pieces, *after)


def order_kernel(*refs):
    refs[-1][...] = jnp.zeros_like(refs[-1])


def order(after):
    return pl.pallas_call(
        order_kernel,
        out_shape=shaped((8, 128), F32),
        in_specs=unread(after),
        out_specs=whole(),
        compiler_params=params(),
        cost_estimate=cost(2e10, 0),
        name="order",
    )(*after)


def cost(flops, loaded=0):
    return pl.CostEstimate(flops=int(flops), bytes_accessed=int(loaded), transcendentals=0)


def route_kernel(ids_ref, expert_hbm, first_ref, second_ref, chooser_ref, weight_ref, sem):
    copy = pltpu.make_async_copy(expert_hbm.at[0, 0], weight_ref, sem)
    copy.start()
    rows, slots = first_ref.shape
    own = lax.axis_index("exp")
    ids = jnp.transpose(ids_ref[...].astype(F32)).astype(jnp.int32)
    lanes = lax.broadcasted_iota(jnp.int32, (rows, 128), 1)
    hot = [(ids[:, i : i + 1] == lanes).astype(F32) for i in range(2)]
    earlier = lax.broadcasted_iota(jnp.int32, (rows, rows), 1) < lax.broadcasted_iota(
        jnp.int32, (rows, rows), 0
    )
    ranks = jnp.dot(
        earlier.astype(F32).astype(BF16), (hot[0] + hot[1]).astype(BF16), preferred_element_type=F32
    )
    places = lax.broadcasted_iota(jnp.int32, (rows, slots), 1)
    tables = []
    for i in range(2):
        slot = jnp.sum(ranks * hot[i], axis=1, keepdims=True).astype(jnp.int32)
        place = jnp.bitwise_xor(ids[:, i : i + 1], own) * CAP + slot
        tables.append((place == places).astype(F32))
    first_ref[...] = tables[0].astype(BF16)
    second_ref[...] = tables[1].astype(BF16)
    chooser_ref[...] = jnp.transpose(tables[0] + tables[1]).astype(BF16)
    copy.wait()


def route(ids, expert_count, experts):
    rows, slots = ids.shape[1], expert_count * CAP
    return pl.pallas_call(
        route_kernel,
        out_shape=(
            shaped((rows, slots), BF16),
            shaped((rows, slots), BF16),
            shaped((slots, rows), BF16),
            shaped(experts.shape[2:], BF16),
        ),
        in_specs=[whole(), hbm()],
        out_specs=[whole()] * 4,
        scratch_shapes=[pltpu.SemaphoreType.DMA],
        compiler_params=params(),
        cost_estimate=cost(1e6, 8e6),
        name="route",
    )(ids, experts)


def conv_kernel(
    before_ref, x_hbm, taps_hbm, bias_hbm, weight_hbm, xconv_ref, part_ref,
    ext_ref, x_ref, taps_ref, bias_ref, weight_ref, sems,
):
    rows = x_ref.shape[0]
    halo = 16
    count = taps_ref.shape[0]
    copies = [
        pltpu.make_async_copy(source, target, sems.at[i])
        for i, (source, target) in enumerate(
            (
                (x_hbm, x_ref),
                (taps_hbm, taps_ref),
                (bias_hbm, bias_ref),
                (weight_hbm, weight_ref),
            )
        )
    ]
    for copy in copies:
        copy.start()
    for copy in copies[:3]:
        copy.wait()
    ext_ref[:halo, :] = before_ref[rows - halo :, :].astype(F32)
    ext_ref[halo:, :] = x_ref[...].astype(F32)
    total = bias_ref[...] + taps_ref[count - 1 : count, :] * ext_ref[halo:, :]
    for k in range(count - 1):
        start = halo - (count - 1) + k
        total = total + taps_ref[k : k + 1, :] * ext_ref[start : start + rows, :]
    xconv = (total * sigmoid(total)).astype(BF16)
    xconv_ref[...] = xconv
    copies[3].wait()
    across = (((1,), (1,)), ((), ()))
    part_ref[:rows, :] = lax.dot_general(
        xconv, weight_ref[:DT_RANK, :], across, preferred_element_type=F32
    ).astype(BF16)
    maps = lax.dot_general(
        weight_ref[DT_RANK:, :], xconv, across, preferred_element_type=F32
    ).astype(BF16)
    part_ref[rows:, :rows] = maps[:STATE]
    part_ref[rows:, rows:] = maps[STATE:]


def conv(before, x, taps, bias, weight):
    rows, channels = x.shape
    return pl.pallas_call(
        conv_kernel,
        out_shape=(shaped((rows, channels), BF16), shaped((rows + STATE, DT_RANK), BF16)),
        in_specs=[whole()] + [hbm()] * 4,
        out_specs=[whole()] * 2,
        scratch_shapes=[
            pltpu.VMEM((16 + rows, channels), F32),
            pltpu.VMEM((rows, channels), BF16),
            pltpu.VMEM(taps.shape, F32),
            pltpu.VMEM(bias.shape, F32),
            pltpu.VMEM(weight.shape, BF16),
            pltpu.SemaphoreType.DMA((4,)),
        ],
        compiler_params=params(),
        name="conv",
    )(before, x, taps, bias, weight)


def prepare_kernel(
    gate_hbm, decay_hbm, residual_hbm, skip_hbm, bias_hbm, step_hbm, out_hbm, gain_hbm,
    silu_ref, rates_ref, skip_ref, bias_ref, step_ref, out_ref, quarter_ref, gain_ref,
    gate_ref, decay_ref, residual_ref, sems,
):
    copies = [
        pltpu.make_async_copy(source, target, sems.at[i])
        for i, (source, target) in enumerate(
            (
                (gate_hbm, gate_ref),
                (decay_hbm, decay_ref),
                (residual_hbm, residual_ref),
                (skip_hbm, skip_ref),
                (bias_hbm, bias_ref),
                (gain_hbm, gain_ref),
                (step_hbm, step_ref),
                (out_hbm, out_ref),
            )
        )
    ]
    for copy in copies:
        copy.start()
    for copy in copies[:3]:
        copy.wait()
    gate = gate_ref[...].astype(F32)
    silu_ref[...] = gate * sigmoid(gate)
    rates_ref[...] = -LOG2E * jnp.exp(decay_ref[...])
    width = quarter_ref.shape[1]
    start = pl.multiple_of(lax.axis_index("tp") * width, 128)
    quarter_ref[...] = residual_ref[:, pl.ds(start, width)].astype(F32)
    for copy in copies[3:]:
        copy.wait()


def prepare(parts, gate, decay_log, residual, skip, bias, step_weight, out_weight, gain):
    rows, channels = gate.shape
    return pl.pallas_call(
        prepare_kernel,
        out_shape=(
            shaped((rows, channels), F32),
            shaped(decay_log.shape, F32),
            shaped(skip.shape, F32),
            shaped(bias.shape, F32),
            shaped(step_weight.shape, BF16),
            shaped(out_weight.shape, BF16),
            shaped((rows, residual.shape[1] // parts), F32),
            shaped(gain.shape, F32),
        ),
        in_specs=[hbm()] * 8,
        out_specs=[whole()] * 8,
        scratch_shapes=[
            pltpu.VMEM((rows, channels), BF16),
            pltpu.VMEM(decay_log.shape, F32),
            pltpu.VMEM(residual.shape, BF16),
            pltpu.SemaphoreType.DMA((8,)),
        ],
        compiler_params=params(),
        cost_estimate=cost(1e6, 6e6),
        name="prepare",
    )(gate, decay_log, residual, skip, bias, step_weight, out_weight, gain)


def over_states(sum_ref):
    total = sum_ref[:, 0, :]
    for i in range(1, 8):
        total = total + sum_ref[:, i, :]
    return total


def scan_kernel(parts, *refs):
    part_refs = refs[:parts]
    xconv_ref, rates_ref, gain_ref, bias_ref, weight_ref, expert_hbm = refs[parts : parts + 6]
    y_ref, elapsed_ref, maps_ref, state_ref, second_ref = refs[parts + 6 : parts + 11]
    steps_ref, driven_ref, sum_ref, expert_sem = refs[parts + 11 :]
    rows, channels = xconv_ref.shape
    expert_copy = pltpu.make_async_copy(expert_hbm.at[0, 1], second_ref, expert_sem)
    expert_copy.start()
    proj = part_refs[0][...].astype(F32)
    for ref in part_refs[1:]:
        proj = proj + ref[...].astype(F32)
    maps = proj[rows:]
    maps_ref[...] = maps
    rank = proj[:rows].astype(BF16)
    raw = jnp.dot(rank, weight_ref[...], preferred_element_type=F32) + bias_ref[...]
    steps = jnp.maximum(raw, 0.0) + jnp.log1p(jnp.exp(-jnp.abs(raw)))
    xfloat = xconv_ref[...].astype(F32)
    steps_ref[...] = steps
    driven_ref[...] = steps * xfloat
    y_ref[...] = gain_ref[...] * xfloat
    high = steps.astype(BF16)
    low = (steps - high.astype(F32)).astype(BF16)
    until = lax.broadcasted_iota(jnp.int32, (rows, rows), 1) <= lax.broadcasted_iota(
        jnp.int32, (rows, rows), 0
    )
    until = until.astype(F32).astype(BF16)
    elapsed_ref[...] = jnp.dot(until, high, preferred_element_type=F32) + jnp.dot(
        until, low, preferred_element_type=F32
    )

    def block(i, carry):
        state, into, out = carry
        begin = pl.multiple_of(i * 8, 8)
        for r in range(8):
            now = steps_ref[pl.ds(begin + r, 1), :]
            driven = driven_ref[pl.ds(begin + r, 1), :]
            state = jnp.exp2(now * rates_ref[...]) * state + driven * into[:, r : r + 1]
            seen = state * out[:, r : r + 1]
            sum_ref[r] = seen[:8] + seen[8:]
        y_ref[pl.ds(begin, 8), :] += over_states(sum_ref)
        return state, pltpu.roll(into, rows - 8, 1), pltpu.roll(out, rows - 8, 1)

    start = jnp.zeros((STATE, channels), F32)
    state_ref[...] = lax.fori_loop(0, rows // 8, block, (start, maps[:, :rows], maps[:, rows:]))[0]
    expert_copy.wait()


def scan(pieces, xconv, rates, gain, bias, weight, experts):
    rows, channels = xconv.shape
    return pl.pallas_call(
        functools.partial(scan_kernel, len(pieces)),
        out_shape=(
            shaped((rows, channels), F32),
            shaped((rows, channels), F32),
            shaped((STATE, DT_RANK), F32),
            shaped((STATE, channels), F32),
            shaped(experts.shape[2:], BF16),
        ),
        in_specs=[whole()] * (len(pieces) + 5) + [hbm()],
        out_specs=[whole()] * 5,
        scratch_shapes=[
            pltpu.VMEM((rows, channels), F32),
            pltpu.VMEM((rows, channels), F32),
            pltpu.VMEM((8, 8, channels), F32),
            pltpu.SemaphoreType.DMA,
        ],
        compiler_params=params(),
        cost_estimate=cost(1e6, 14e6),
        name="scan",
    )(*pieces, xconv, rates, gain, bias, weight, experts)


def mix_kernel(parts, *refs):
    maps_ref, y_ref, elapsed_ref, rates_ref, state_ref, silu_ref, quarter_ref, weight_ref, expert_hbm = refs[:9]
    own_ref, sent, third_ref = refs[9], refs[10 : 9 + parts], refs[9 + parts]
    sum_ref, gated_ref, expert_sem = refs[10 + parts :]
    expert_copy = pltpu.make_async_copy(expert_hbm.at[0, 2], third_ref, expert_sem)
    expert_copy.start()
    rows = y_ref.shape[0]

    def block(i, out):
        begin = pl.multiple_of(i * 16, 16)
        for r in range(16):
            decay = jnp.exp2(elapsed_ref[pl.ds(begin + r, 1), :] * rates_ref[...])
            seen = decay * (state_ref[...] * out[:, r : r + 1])
            sum_ref[r] = seen[:8] + seen[8:]
        cut = pl.ds(begin, 16)
        gated_ref[cut, :] = ((y_ref[cut, :] + over_states(sum_ref)) * silu_ref[cut, :]).astype(BF16)
        return pltpu.roll(out, rows - 16, 1)

    lax.fori_loop(0, rows // 16, block, maps_ref[:, rows:])
    own = lax.axis_index("tp")
    width = own_ref.shape[1]
    for k in range(parts):
        start = pl.multiple_of(jnp.bitwise_xor(own, k) * width, 128)
        product = jnp.dot(
            gated_ref[...], weight_ref[:, pl.ds(start, width)], preferred_element_type=F32
        )
        if k == 0:
            own_ref[...] = product + quarter_ref[...]
        else:
            sent[k - 1][...] = product.astype(BF16)
    expert_copy.wait()


def mix(parts, maps, y, elapsed, rates, state, silu, quarter, weight, experts):
    rows, channels = y.shape
    width = weight.shape[1] // parts
    return pl.pallas_call(
        functools.partial(mix_kernel, parts),
        out_shape=[shaped((rows, width), F32)]
        + [shaped((rows, width), BF16)] * (parts - 1)
        + [shaped(experts.shape[2:], BF16)],
        in_specs=[whole()] * 8 + [hbm()],
        out_specs=[whole()] * (parts + 1),
        scratch_shapes=[
            pltpu.VMEM((16, 8, channels), F32),
            pltpu.VMEM((rows, channels), BF16),
            pltpu.SemaphoreType.DMA,
        ],
        compiler_params=params(),
        cost_estimate=cost(1e6, 12e6),
        name="mix",
    )(maps, y, elapsed, rates, state, silu, quarter, weight, experts)


def pick_kernel(parts, *refs):
    own_ref, arrived, chooser_ref = refs[0], refs[1:parts], refs[parts]
    stream_ref, out_refs = refs[parts + 1], refs[parts + 2 :]
    total = own_ref[...]
    for ref in arrived:
        total = total + ref[...].astype(F32)
    stream = total.astype(BF16)
    stream_ref[...] = stream
    picked = jnp.dot(chooser_ref[...], stream, preferred_element_type=F32).astype(BF16)
    for j, ref in enumerate(out_refs):
        ref[...] = picked[j * CAP : (j + 1) * CAP, :]


def pick(own, arrived, chooser):
    rows, width = own.shape
    experts = chooser.shape[0] // CAP
    return pl.pallas_call(
        functools.partial(pick_kernel, 1 + len(arrived)),
        out_shape=[shaped((rows, width), BF16)] + [shaped((CAP, width), BF16)] * experts,
        in_specs=[whole()] * (2 + len(arrived)),
        out_specs=[whole()] * (1 + experts),
        compiler_params=params(),
        cost_estimate=cost(1e6, 1e6),
        name="pick",
    )(own, *arrived, chooser)


def norm_kernel(parts, count, *refs):
    gain_ref, out_ref = refs[parts * count], refs[-1]
    own = lax.axis_index("tp")
    begin = 0
    for i in range(count):
        pieces = [ref[...].astype(F32) for ref in refs[i * parts : (i + 1) * parts]]
        rows, width = pieces[0].shape
        total = sum(jnp.sum(piece * piece, axis=1, keepdims=True) for piece in pieces)
        scale = lax.rsqrt(total / (width * parts) + 1e-6)
        for k, piece in enumerate(pieces):
            start = pl.multiple_of(jnp.bitwise_xor(own, k) * width, 128)
            out_ref[begin : begin + rows, pl.ds(start, width)] = (
                piece * scale * gain_ref[:, pl.ds(start, width)]
            ).astype(BF16)
        begin += rows


def norm(sets, gain, after):
    parts = len(sets[0])
    rows, width = sum(pieces[0].shape[0] for pieces in sets), sets[0][0].shape[1]
    return pl.pallas_call(
        functools.partial(norm_kernel, parts, len(sets)),
        out_shape=shaped((rows, width * parts), BF16),
        in_specs=[whole()] * (parts * len(sets) + 1) + unread(after),
        out_specs=whole(),
        compiler_params=params(),
        cost_estimate=cost(1e6, 1e6),
        name="norm",
    )(*sum(sets, []), gain, *after)


def hidden_kernel(x_ref, gate_ref, up_ref, *refs):
    hidden_ref = refs[-1]
    width = gate_ref.shape[1]
    size = 256 if width % 256 == 0 else width
    for i in range(width // size):
        cut = slice(i * size, (i + 1) * size)
        gate = jnp.dot(x_ref[...], gate_ref[:, cut], preferred_element_type=F32)
        up = jnp.dot(x_ref[...], up_ref[:, cut], preferred_element_type=F32)
        hidden_ref[:, cut] = (gate * sigmoid(gate) * up).astype(BF16)


def hidden_units(x, gate, up, after):
    rows, width = x.shape[0], gate.shape[1]
    return pl.pallas_call(
        hidden_kernel,
        out_shape=shaped((rows, width), BF16),
        in_specs=[whole()] * 3 + unread(after),
        out_specs=whole(),
        compiler_params=params(),
        cost_estimate=cost(1e6, 0),
        name="hidden",
    )(x, gate, up, *after)


def down_kernel(hidden_own_ref, hidden_other_ref, down_ref, *refs):
    own_ref, other_ref, hidden_ref = refs[-3:]
    rows = hidden_own_ref.shape[0]
    hidden_ref[:rows, :] = hidden_own_ref[...]
    hidden_ref[rows:, :] = hidden_other_ref[...]
    size = 256
    for i in range(down_ref.shape[0] // size):
        cut = slice(i * size, (i + 1) * size)
        product = lax.dot_general(
            hidden_ref[...], down_ref[cut, :], (((1,), (1,)), ((), ())), preferred_element_type=F32
        )
        own_ref[:, cut] = product[:rows]
        other_ref[:, cut] = product[rows:].astype(BF16)


def down_sums(hidden_own, hidden_other, down, after):
    rows, width = hidden_own.shape
    model = down.shape[0]
    return pl.pallas_call(
        down_kernel,
        out_shape=(shaped((rows, model), F32), shaped((rows, model), BF16)),
        in_specs=[whole()] * 3 + unread(after),
        out_specs=[whole()] * 2,
        scratch_shapes=[pltpu.VMEM((2 * rows, width), BF16)],
        compiler_params=params(),
        cost_estimate=cost(1e6, 0),
        name="down",
    )(hidden_own, hidden_other, down, *after)


def join_kernel(parts, own_ref, other_ref, *refs):
    out_refs = refs[-parts:]
    width = out_refs[0].shape[1]
    own = lax.axis_index("tp")
    for k, ref in enumerate(out_refs):
        cut = pl.ds(pl.multiple_of(jnp.bitwise_xor(own, k) * width, 128), width)
        ref[...] = (own_ref[:, cut] + other_ref[:, cut].astype(F32)).astype(ref.dtype)


def join(parts, own, other, after):
    rows, model = own.shape
    return pl.pallas_call(
        functools.partial(join_kernel, parts),
        out_shape=[shaped((rows, model // parts), BF16 if k else F32) for k in range(parts)],
        in_specs=[whole()] * 2 + unread(after),
        out_specs=[whole()] * parts,
        compiler_params=params(),
        cost_estimate=cost(1e6, 1e6),
        name="join",
    )(own, other, *after)


def total_kernel(parts, *refs):
    total = refs[0][...].astype(F32)
    for ref in refs[1:parts]:
        total = total + ref[...].astype(F32)
    total = total.astype(BF16)
    for j, ref in enumerate(refs[parts:]):
        ref[...] = total[j * CAP : (j + 1) * CAP, :]


def totals(pieces):
    rows, width = pieces[0].shape
    count = rows // CAP
    return pl.pallas_call(
        functools.partial(total_kernel, len(pieces)),
        out_shape=[shaped((CAP, width), BF16)] * count,
        in_specs=[whole()] * len(pieces),
        out_specs=[whole()] * count,
        compiler_params=params(),
        cost_estimate=cost(1e6, 1e6),
        name="totals",
    )(*pieces)


def blend_kernel(experts, *refs):
    back = refs[:experts]
    stream_ref, first_ref, second_ref, gates_ref, out_ref, rows_ref = refs[experts:]
    for j, ref in enumerate(back):
        rows_ref[j * CAP : (j + 1) * CAP, :] = ref[...]
    rows = rows_ref[...]
    gates = jnp.transpose(gates_ref[...])
    moe = gates[:, 0:1] * jnp.dot(first_ref[...], rows, preferred_element_type=F32)
    moe = moe + gates[:, 1:2] * jnp.dot(second_ref[...], rows, preferred_element_type=F32)
    out_ref[...] = (stream_ref[...].astype(F32) + moe).astype(BF16)


def blend(back, stream, first, second, gates):
    experts, width = len(back), stream.shape[1]
    return pl.pallas_call(
        functools.partial(blend_kernel, experts),
        out_shape=shaped(stream.shape, BF16),
        in_specs=[whole()] * (experts + 4),
        out_specs=whole(),
        scratch_shapes=[pltpu.VMEM((experts * CAP, width), BF16)],
        compiler_params=params(),
        name="blend",
    )(*back, stream, first, second, gates)


def expert(tp, x_own, gate, up, down, after_start, after_sums):
    x_other = swap(x_own, "ctx", 1)
    hidden_own = hidden_units(x_own, gate, up, after_start)
    hidden_other = hidden_units(x_other, gate, up, [hidden_own])
    sum_own, sum_other = down_sums(hidden_own, hidden_other, down, [])
    after_sums = [order([sum_other, *after_sums])] if after_sums else []
    joined = join(tp, sum_own, swap(sum_other, "ctx", 1), after_sums)
    return sum_own, joined


def body(
    conv_in,
    gate_in,
    residual,
    conv_weight,
    conv_bias,
    proj_weight,
    step_weight,
    step_bias,
    decay_log,
    skip_gain,
    out_weight,
    norm_gain,
    expert_ids,
    route_gates,
    expert_weight,
):
    tp, experts = lax.axis_size("tp"), lax.axis_size("exp")
    local = conv_in[0]
    before = lax.ppermute(local, "ctx", [(0, 1)])
    expert_weight = stay(expert_weight)
    xconv, part = conv(
        before, stay(local), stay(conv_weight), stay(conv_bias[None]), stay(proj_weight.T)
    )
    parts = [part] + [swap(part, "tp", k) for k in range(1, tp)]
    silu, rates, skip, bias, step_w, out_w, quarter, gain = prepare(
        tp, stay(gate_in[0]), stay(decay_log), stay(residual[0]), stay(skip_gain[None]),
        stay(step_bias[None]), stay(step_weight), stay(out_weight), stay(norm_gain[None]),
    )
    y, elapsed, maps, state, up_w = scan(parts, xconv, rates, skip, bias, step_w, expert_weight)
    before = lax.ppermute(state, "ctx", [(0, 1)])
    own, *sent, down_w = mix(
        tp, maps, y, elapsed, rates, before, silu, quarter, out_w, expert_weight
    )
    arrived = [swap(piece, "tp", k) for k, piece in enumerate(sent, 1)]
    first, second, chooser, gate_w = route(expert_ids[0].T, experts, expert_weight)
    stream, *picked = pick(own, arrived, chooser)
    rows = [picked[0]] + [swap(picked[j], "exp", j) for j in range(1, experts)]
    half = experts // 2
    piece_a = rows[1] if half == 2 else stack(rows[1:half], [])
    piece_b = stack(rows[half:], [rows[1]])
    both = order([rows[1], piece_b])
    sets = [
        [piece] + [swap(piece, "tp", k) for k in range(1, tp)]
        for piece in (rows[0], piece_a, piece_b)
    ]
    x_a = norm(sets[:2], gain, [both])
    own_a, joined_a = expert(tp, x_a, gate_w, up_w, down_w, [], [])
    summed_a = [joined_a[0]] + [swap(joined_a[k], "tp", k) for k in range(1, tp)]
    back = totals(summed_a)
    x_b = norm(sets[2:], gain, [own_a])
    _, joined_b = expert(tp, x_b, gate_w, up_w, down_w, [joined_a[0]], [back[0]])
    back += totals([joined_b[0]] + [swap(joined_b[k], "tp", k) for k in range(1, tp)])
    back = [back[0]] + [swap(back[j], "exp", j) for j in range(1, experts)]
    return blend(back, stream, first, second, route_gates[0].T)[None]


def solution(mesh):
    placed = (
        P("exp", "ctx", "tp"),
        P("exp", "ctx", "tp"),
        P("exp", "ctx", None),
        P(None, "tp"),
        P("tp"),
        P("tp", None),
        P(None, "tp"),
        P("tp"),
        P(None, "tp"),
        P("tp"),
        P("tp", None),
        P(),
        P("exp", "ctx", None),
        P("exp", "ctx", None),
        P("exp", None, None, ("ctx", "tp")),
    )
    return jax.shard_map(
        body, mesh=mesh, in_specs=placed, out_specs=P("exp", "ctx", "tp"), check_vma=False
    )
```

```python
import functools
import math

import jax
import jax.numpy as jnp
from jax import lax
from jax.experimental import pallas as pl
from jax.experimental.pallas import tpu as pltpu
from jax.sharding import PartitionSpec as P

STATE = 16
DT_RANK = 256
CAP = 64
LOG2E = math.log2(math.e)
VMEM_LIMIT = 20 * 1024 * 1024
F32 = jnp.float32
BF16 = jnp.bfloat16


def params():
    return pltpu.CompilerParams(vmem_limit_bytes=VMEM_LIMIT)


def whole():
    return pl.BlockSpec(memory_space=pltpu.VMEM)


def shaped(shape, dtype):
    return jax.ShapeDtypeStruct(shape, dtype)


def swap(block, axis, k):
    return lax.ppermute(block, axis, [(i, i ^ k) for i in range(lax.axis_size(axis))])


def swaps(blocks):
    got = {k: swap(blocks[k - 1], "tp", k) for k in range(len(blocks), 0, -1)}
    return [got[k] for k in sorted(got)]


def sigmoid(x):
    return 1.0 / (1.0 + jnp.exp2(x * -LOG2E))


def stay(array):
    return pltpu.with_memory_space_constraint(array, pltpu.HBM)


def hbm():
    return pl.BlockSpec(memory_space=pltpu.HBM)


def unread(arrays):
    return [pl.BlockSpec(memory_space=pl.ANY)] * len(arrays)


def stack_kernel(count, *refs):
    for j, ref in enumerate(refs[:count]):
        rows = ref.shape[0]
        refs[-1][j * rows : (j + 1) * rows, :] = ref[...]


def stack(pieces, after):
    rows, width = pieces[0].shape
    return pl.pallas_call(
        functools.partial(stack_kernel, len(pieces)),
        out_shape=shaped((rows * len(pieces), width), pieces[0].dtype),
        in_specs=[whole()] * len(pieces) + unread(after),
        out_specs=whole(),
        compiler_params=params(),
        cost_estimate=cost(1e6, 0),
        name="stack",
    )(*pieces, *after)


def order_kernel(*refs):
    refs[-1][...] = jnp.zeros_like(refs[-1])


def order(after):
    return pl.pallas_call(
        order_kernel,
        out_shape=shaped((8, 128), F32),
        in_specs=unread(after),
        out_specs=whole(),
        compiler_params=params(),
        cost_estimate=cost(2e10, 0),
        name="order",
    )(*after)


def cost(flops, loaded=0):
    return pl.CostEstimate(flops=int(flops), bytes_accessed=int(loaded), transcendentals=0)


def route_kernel(ids_ref, expert_hbm, first_ref, second_ref, chooser_ref, weight_ref, sem):
    copy = pltpu.make_async_copy(expert_hbm.at[0, 0], weight_ref, sem)
    copy.start()
    rows, slots = first_ref.shape
    own = lax.axis_index("exp")
    ids = jnp.transpose(ids_ref[...].astype(F32)).astype(jnp.int32)
    lanes = lax.broadcasted_iota(jnp.int32, (rows, 128), 1)
    hot = [(ids[:, i : i + 1] == lanes).astype(F32) for i in range(2)]
    earlier = lax.broadcasted_iota(jnp.int32, (rows, rows), 1) < lax.broadcasted_iota(
        jnp.int32, (rows, rows), 0
    )
    ranks = jnp.dot(
        earlier.astype(F32).astype(BF16), (hot[0] + hot[1]).astype(BF16), preferred_element_type=F32
    )
    places = lax.broadcasted_iota(jnp.int32, (rows, slots), 1)
    tables = []
    for i in range(2):
        slot = jnp.sum(ranks * hot[i], axis=1, keepdims=True).astype(jnp.int32)
        place = jnp.bitwise_xor(ids[:, i : i + 1], own) * CAP + slot
        tables.append((place == places).astype(F32))
    first_ref[...] = tables[0].astype(BF16)
    second_ref[...] = tables[1].astype(BF16)
    chooser_ref[...] = jnp.transpose(tables[0] + tables[1]).astype(BF16)
    copy.wait()


def route(ids, expert_count, experts):
    rows, slots = ids.shape[1], expert_count * CAP
    return pl.pallas_call(
        route_kernel,
        out_shape=(
            shaped((rows, slots), BF16),
            shaped((rows, slots), BF16),
            shaped((slots, rows), BF16),
            shaped(experts.shape[2:], BF16),
        ),
        in_specs=[whole(), hbm()],
        out_specs=[whole()] * 4,
        scratch_shapes=[pltpu.SemaphoreType.DMA],
        compiler_params=params(),
        cost_estimate=cost(1e6, 8e6),
        name="route",
    )(ids, experts)


def conv_kernel(before_ref, x_ref, taps_ref, bias_ref, weight_ref, xconv_ref, part_ref, ext_ref):
    rows = x_ref.shape[0]
    halo = 16
    count = taps_ref.shape[0]
    ext_ref[:halo, :] = before_ref[rows - halo :, :].astype(F32)
    ext_ref[halo:, :] = x_ref[...].astype(F32)
    total = bias_ref[...] + taps_ref[count - 1 : count, :] * ext_ref[halo:, :]
    for k in range(count - 1):
        start = halo - (count - 1) + k
        total = total + taps_ref[k : k + 1, :] * ext_ref[start : start + rows, :]
    xconv = (total * sigmoid(total)).astype(BF16)
    xconv_ref[...] = xconv
    across = (((1,), (1,)), ((), ()))
    part_ref[:rows, :] = lax.dot_general(
        xconv, weight_ref[:DT_RANK, :], across, preferred_element_type=F32
    ).astype(BF16)
    maps = lax.dot_general(
        weight_ref[DT_RANK:, :], xconv, across, preferred_element_type=F32
    ).astype(BF16)
    part_ref[rows:, :rows] = maps[:STATE]
    part_ref[rows:, rows:] = maps[STATE:]


def conv(before, x, taps, bias, weight):
    rows, channels = x.shape
    return pl.pallas_call(
        conv_kernel,
        out_shape=(shaped((rows, channels), BF16), shaped((rows + STATE, DT_RANK), BF16)),
        in_specs=[whole()] * 5,
        out_specs=[whole()] * 2,
        scratch_shapes=[pltpu.VMEM((16 + rows, channels), F32)],
        compiler_params=params(),
        cost_estimate=cost(1e6, 1e6),
        name="conv",
    )(before, x, taps, bias, weight)


def load_kernel(count, *refs):
    copies = [
        pltpu.make_async_copy(refs[i], refs[count + i], refs[-1].at[i]) for i in range(count)
    ]
    for copy in copies:
        copy.start()
    for copy in copies:
        copy.wait()


def load(*arrays):
    count = len(arrays)
    return pl.pallas_call(
        functools.partial(load_kernel, count),
        out_shape=[shaped(array.shape, array.dtype) for array in arrays],
        in_specs=[hbm()] * count,
        out_specs=[whole()] * count,
        scratch_shapes=[pltpu.SemaphoreType.DMA((count,))],
        compiler_params=params(),
        cost_estimate=cost(1e6, 2e6),
        name="load",
    )(*arrays)


def prepare_kernel(
    gate_hbm, decay_hbm, residual_hbm, skip_hbm, bias_hbm, step_hbm, out_hbm, gain_hbm,
    silu_ref, rates_ref, skip_ref, bias_ref, step_ref, out_ref, quarter_ref, gain_ref,
    gate_ref, decay_ref, residual_ref, sems,
):
    copies = [
        pltpu.make_async_copy(source, target, sems.at[i])
        for i, (source, target) in enumerate(
            (
                (gate_hbm, gate_ref),
                (decay_hbm, decay_ref),
                (residual_hbm, residual_ref),
                (skip_hbm, skip_ref),
                (bias_hbm, bias_ref),
                (gain_hbm, gain_ref),
                (step_hbm, step_ref),
                (out_hbm, out_ref),
            )
        )
    ]
    for copy in copies:
        copy.start()
    for copy in copies[:3]:
        copy.wait()
    gate = gate_ref[...].astype(F32)
    silu_ref[...] = gate * sigmoid(gate)
    rates_ref[...] = -LOG2E * jnp.exp(decay_ref[...])
    width = quarter_ref.shape[1]
    start = pl.multiple_of(lax.axis_index("tp") * width, 128)
    quarter_ref[...] = residual_ref[:, pl.ds(start, width)].astype(F32)
    for copy in copies[3:]:
        copy.wait()


def prepare(parts, gate, decay_log, residual, skip, bias, step_weight, out_weight, gain):
    rows, channels = gate.shape
    return pl.pallas_call(
        prepare_kernel,
        out_shape=(
            shaped((rows, channels), F32),
            shaped(decay_log.shape, F32),
            shaped(skip.shape, F32),
            shaped(bias.shape, F32),
            shaped(step_weight.shape, BF16),
            shaped(out_weight.shape, BF16),
            shaped((rows, residual.shape[1] // parts), F32),
            shaped(gain.shape, F32),
        ),
        in_specs=[hbm()] * 8,
        out_specs=[whole()] * 8,
        scratch_shapes=[
            pltpu.VMEM((rows, channels), BF16),
            pltpu.VMEM(decay_log.shape, F32),
            pltpu.VMEM(residual.shape, BF16),
            pltpu.SemaphoreType.DMA((8,)),
        ],
        compiler_params=params(),
        cost_estimate=cost(1e6, 6e6),
        name="prepare",
    )(gate, decay_log, residual, skip, bias, step_weight, out_weight, gain)


def over_states(sum_ref):
    total = sum_ref[:, 0, :]
    for i in range(1, 8):
        total = total + sum_ref[:, i, :]
    return total


def scan_kernel(parts, *refs):
    part_refs = refs[:parts]
    xconv_ref, rates_ref, gain_ref, bias_ref, weight_ref, expert_hbm = refs[parts : parts + 6]
    y_ref, elapsed_ref, maps_ref, state_ref, second_ref = refs[parts + 6 : parts + 11]
    steps_ref, driven_ref, sum_ref, expert_sem = refs[parts + 11 :]
    rows, channels = xconv_ref.shape
    expert_copy = pltpu.make_async_copy(expert_hbm.at[0, 1], second_ref, expert_sem)
    expert_copy.start()
    proj = part_refs[0][...].astype(F32)
    for ref in part_refs[1:]:
        proj = proj + ref[...].astype(F32)
    maps = proj[rows:]
    maps_ref[...] = maps
    rank = proj[:rows].astype(BF16)
    raw = jnp.dot(rank, weight_ref[...], preferred_element_type=F32) + bias_ref[...]
    steps = jnp.maximum(raw, 0.0) + jnp.log1p(jnp.exp(-jnp.abs(raw)))
    xfloat = xconv_ref[...].astype(F32)
    steps_ref[...] = steps
    driven_ref[...] = steps * xfloat
    y_ref[...] = gain_ref[...] * xfloat
    high = steps.astype(BF16)
    low = (steps - high.astype(F32)).astype(BF16)
    until = lax.broadcasted_iota(jnp.int32, (rows, rows), 1) <= lax.broadcasted_iota(
        jnp.int32, (rows, rows), 0
    )
    until = until.astype(F32).astype(BF16)
    elapsed_ref[...] = jnp.dot(until, high, preferred_element_type=F32) + jnp.dot(
        until, low, preferred_element_type=F32
    )

    def block(i, carry):
        state, into, out = carry
        begin = pl.multiple_of(i * 8, 8)
        for r in range(8):
            now = steps_ref[pl.ds(begin + r, 1), :]
            driven = driven_ref[pl.ds(begin + r, 1), :]
            state = jnp.exp2(now * rates_ref[...]) * state + driven * into[:, r : r + 1]
            seen = state * out[:, r : r + 1]
            sum_ref[r] = seen[:8] + seen[8:]
        y_ref[pl.ds(begin, 8), :] += over_states(sum_ref)
        return state, pltpu.roll(into, rows - 8, 1), pltpu.roll(out, rows - 8, 1)

    start = jnp.zeros((STATE, channels), F32)
    state_ref[...] = lax.fori_loop(0, rows // 8, block, (start, maps[:, :rows], maps[:, rows:]))[0]
    expert_copy.wait()


def scan(pieces, xconv, rates, gain, bias, weight, experts):
    rows, channels = xconv.shape
    return pl.pallas_call(
        functools.partial(scan_kernel, len(pieces)),
        out_shape=(
            shaped((rows, channels), F32),
            shaped((rows, channels), F32),
            shaped((STATE, DT_RANK), F32),
            shaped((STATE, channels), F32),
            shaped(experts.shape[2:], BF16),
        ),
        in_specs=[whole()] * (len(pieces) + 5) + [hbm()],
        out_specs=[whole()] * 5,
        scratch_shapes=[
            pltpu.VMEM((rows, channels), F32),
            pltpu.VMEM((rows, channels), F32),
            pltpu.VMEM((8, 8, channels), F32),
            pltpu.SemaphoreType.DMA,
        ],
        compiler_params=params(),
        cost_estimate=cost(1e6, 14e6),
        name="scan",
    )(*pieces, xconv, rates, gain, bias, weight, experts)


def mix_kernel(parts, *refs):
    maps_ref, y_ref, elapsed_ref, rates_ref, state_ref, silu_ref, quarter_ref, weight_ref, expert_hbm = refs[:9]
    own_ref, sent, third_ref = refs[9], refs[10 : 9 + parts], refs[9 + parts]
    sum_ref, gated_ref, expert_sem = refs[10 + parts :]
    expert_copy = pltpu.make_async_copy(expert_hbm.at[0, 2], third_ref, expert_sem)
    expert_copy.start()
    rows = y_ref.shape[0]

    def block(i, out):
        begin = pl.multiple_of(i * 16, 16)
        for r in range(16):
            decay = jnp.exp2(elapsed_ref[pl.ds(begin + r, 1), :] * rates_ref[...])
            seen = decay * (state_ref[...] * out[:, r : r + 1])
            sum_ref[r] = seen[:8] + seen[8:]
        cut = pl.ds(begin, 16)
        gated_ref[cut, :] = ((y_ref[cut, :] + over_states(sum_ref)) * silu_ref[cut, :]).astype(BF16)
        return pltpu.roll(out, rows - 16, 1)

    lax.fori_loop(0, rows // 16, block, maps_ref[:, rows:])
    own = lax.axis_index("tp")
    width = own_ref.shape[1]
    for k in range(parts):
        start = pl.multiple_of(jnp.bitwise_xor(own, k) * width, 128)
        product = jnp.dot(
            gated_ref[...], weight_ref[:, pl.ds(start, width)], preferred_element_type=F32
        )
        if k == 0:
            own_ref[...] = product + quarter_ref[...]
        else:
            sent[k - 1][...] = product.astype(BF16)
    expert_copy.wait()


def mix(parts, maps, y, elapsed, rates, state, silu, quarter, weight, experts):
    rows, channels = y.shape
    width = weight.shape[1] // parts
    return pl.pallas_call(
        functools.partial(mix_kernel, parts),
        out_shape=[shaped((rows, width), F32)]
        + [shaped((rows, width), BF16)] * (parts - 1)
        + [shaped(experts.shape[2:], BF16)],
        in_specs=[whole()] * 8 + [hbm()],
        out_specs=[whole()] * (parts + 1),
        scratch_shapes=[
            pltpu.VMEM((16, 8, channels), F32),
            pltpu.VMEM((rows, channels), BF16),
            pltpu.SemaphoreType.DMA,
        ],
        compiler_params=params(),
        cost_estimate=cost(1e6, 12e6),
        name="mix",
    )(maps, y, elapsed, rates, state, silu, quarter, weight, experts)


def pick_kernel(parts, *refs):
    own_ref, arrived, chooser_ref = refs[0], refs[1:parts], refs[parts]
    stream_ref, out_refs = refs[parts + 1], refs[parts + 2 :]
    total = own_ref[...]
    for ref in arrived:
        total = total + ref[...].astype(F32)
    stream = total.astype(BF16)
    stream_ref[...] = stream
    picked = jnp.dot(chooser_ref[...], stream, preferred_element_type=F32).astype(BF16)
    for j, ref in enumerate(out_refs):
        ref[...] = picked[j * CAP : (j + 1) * CAP, :]


def pick(own, arrived, chooser):
    rows, width = own.shape
    experts = chooser.shape[0] // CAP
    return pl.pallas_call(
        functools.partial(pick_kernel, 1 + len(arrived)),
        out_shape=[shaped((rows, width), BF16)] + [shaped((CAP, width), BF16)] * experts,
        in_specs=[whole()] * (2 + len(arrived)),
        out_specs=[whole()] * (1 + experts),
        compiler_params=params(),
        cost_estimate=cost(1e6, 1e6),
        name="pick",
    )(own, *arrived, chooser)


def norm_kernel(parts, count, *refs):
    gain_ref, out_ref = refs[parts * count], refs[-1]
    own = lax.axis_index("tp")
    begin = 0
    for i in range(count):
        pieces = [ref[...].astype(F32) for ref in refs[i * parts : (i + 1) * parts]]
        rows, width = pieces[0].shape
        total = sum(jnp.sum(piece * piece, axis=1, keepdims=True) for piece in pieces)
        scale = lax.rsqrt(total / (width * parts) + 1e-6)
        for k, piece in enumerate(pieces):
            start = pl.multiple_of(jnp.bitwise_xor(own, k) * width, 128)
            out_ref[begin : begin + rows, pl.ds(start, width)] = (
                piece * scale * gain_ref[:, pl.ds(start, width)]
            ).astype(BF16)
        begin += rows


def norm(sets, gain, after):
    parts = len(sets[0])
    rows, width = sum(pieces[0].shape[0] for pieces in sets), sets[0][0].shape[1]
    return pl.pallas_call(
        functools.partial(norm_kernel, parts, len(sets)),
        out_shape=shaped((rows, width * parts), BF16),
        in_specs=[whole()] * (parts * len(sets) + 1) + unread(after),
        out_specs=whole(),
        compiler_params=params(),
        cost_estimate=cost(1e6, 1e6),
        name="norm",
    )(*sum(sets, []), gain, *after)


def hidden_kernel(x_ref, gate_ref, up_ref, *refs):
    hidden_ref = refs[-1]
    width = gate_ref.shape[1]
    size = 256 if width % 256 == 0 else width
    for i in range(width // size):
        cut = slice(i * size, (i + 1) * size)
        gate = jnp.dot(x_ref[...], gate_ref[:, cut], preferred_element_type=F32)
        up = jnp.dot(x_ref[...], up_ref[:, cut], preferred_element_type=F32)
        hidden_ref[:, cut] = (gate * sigmoid(gate) * up).astype(BF16)


def hidden_units(x, gate, up, after):
    rows, width = x.shape[0], gate.shape[1]
    return pl.pallas_call(
        hidden_kernel,
        out_shape=shaped((rows, width), BF16),
        in_specs=[whole()] * 3 + unread(after),
        out_specs=whole(),
        compiler_params=params(),
        cost_estimate=cost(1e6, 0),
        name="hidden",
    )(x, gate, up, *after)


def down_kernel(hidden_own_ref, hidden_other_ref, down_ref, *refs):
    own_ref, other_ref, hidden_ref = refs[-3:]
    rows = hidden_own_ref.shape[0]
    hidden_ref[:rows, :] = hidden_own_ref[...]
    hidden_ref[rows:, :] = hidden_other_ref[...]
    size = 256
    for i in range(down_ref.shape[0] // size):
        cut = slice(i * size, (i + 1) * size)
        product = lax.dot_general(
            hidden_ref[...], down_ref[cut, :], (((1,), (1,)), ((), ())), preferred_element_type=F32
        )
        own_ref[:, cut] = product[:rows]
        other_ref[:, cut] = product[rows:].astype(BF16)


def down_sums(hidden_own, hidden_other, down, after):
    rows, width = hidden_own.shape
    model = down.shape[0]
    return pl.pallas_call(
        down_kernel,
        out_shape=(shaped((rows, model), F32), shaped((rows, model), BF16)),
        in_specs=[whole()] * 3 + unread(after),
        out_specs=[whole()] * 2,
        scratch_shapes=[pltpu.VMEM((2 * rows, width), BF16)],
        compiler_params=params(),
        cost_estimate=cost(1e6, 0),
        name="down",
    )(hidden_own, hidden_other, down, *after)


def join_kernel(parts, own_ref, other_ref, *refs):
    out_refs = refs[-parts:]
    width = out_refs[0].shape[1]
    own = lax.axis_index("tp")
    for k, ref in enumerate(out_refs):
        cut = pl.ds(pl.multiple_of(jnp.bitwise_xor(own, k) * width, 128), width)
        ref[...] = (own_ref[:, cut] + other_ref[:, cut].astype(F32)).astype(ref.dtype)


def join(parts, own, other, after):
    rows, model = own.shape
    return pl.pallas_call(
        functools.partial(join_kernel, parts),
        out_shape=[shaped((rows, model // parts), BF16 if k else F32) for k in range(parts)],
        in_specs=[whole()] * 2 + unread(after),
        out_specs=[whole()] * parts,
        compiler_params=params(),
        cost_estimate=cost(1e6, 1e6),
        name="join",
    )(own, other, *after)


def total_kernel(parts, *refs):
    total = refs[0][...].astype(F32)
    for ref in refs[1:parts]:
        total = total + ref[...].astype(F32)
    total = total.astype(BF16)
    for j, ref in enumerate(refs[parts:]):
        ref[...] = total[j * CAP : (j + 1) * CAP, :]


def totals(pieces):
    rows, width = pieces[0].shape
    count = rows // CAP
    return pl.pallas_call(
        functools.partial(total_kernel, len(pieces)),
        out_shape=[shaped((CAP, width), BF16)] * count,
        in_specs=[whole()] * len(pieces),
        out_specs=[whole()] * count,
        compiler_params=params(),
        cost_estimate=cost(1e6, 1e6),
        name="totals",
    )(*pieces)


def blend_kernel(begin, count, *refs):
    back = refs[:count]
    base_ref, first_ref, second_ref, gates_ref, out_ref, rows_ref = refs[count:]
    for j, ref in enumerate(back):
        rows_ref[j * CAP : (j + 1) * CAP, :] = ref[...]
    rows = rows_ref[...]
    gates = jnp.transpose(gates_ref[...])
    cut = slice(begin, begin + count * CAP)
    moe = gates[:, 0:1] * jnp.dot(first_ref[:, cut], rows, preferred_element_type=F32)
    moe = moe + gates[:, 1:2] * jnp.dot(second_ref[:, cut], rows, preferred_element_type=F32)
    out_ref[...] = (base_ref[...].astype(F32) + moe).astype(out_ref.dtype)


def blend(begin, back, base, first, second, gates, dtype):
    count, width = len(back), base.shape[1]
    return pl.pallas_call(
        functools.partial(blend_kernel, begin, count),
        out_shape=shaped(base.shape, dtype),
        in_specs=[whole()] * (count + 4),
        out_specs=whole(),
        scratch_shapes=[pltpu.VMEM((count * CAP, width), BF16)],
        compiler_params=params(),
        cost_estimate=cost(1e6, 1e6),
        name="blend",
    )(*back, base, first, second, gates)


def expert(tp, x_own, gate, up, down, after_start, after_sums):
    x_other = swap(x_own, "ctx", 1)
    hidden_own = hidden_units(x_own, gate, up, after_start)
    hidden_other = hidden_units(x_other, gate, up, [hidden_own])
    sum_own, sum_other = down_sums(hidden_own, hidden_other, down, [])
    after_sums = [order([sum_other, *after_sums])] if after_sums else []
    joined = join(tp, sum_own, swap(sum_other, "ctx", 1), after_sums)
    return sum_own, joined


def body(
    conv_in,
    gate_in,
    residual,
    conv_weight,
    conv_bias,
    proj_weight,
    step_weight,
    step_bias,
    decay_log,
    skip_gain,
    out_weight,
    norm_gain,
    expert_ids,
    route_gates,
    expert_weight,
):
    tp, experts = lax.axis_size("tp"), lax.axis_size("exp")
    local = conv_in[0]
    before = lax.ppermute(local, "ctx", [(0, 1)])
    expert_weight = stay(expert_weight)
    near = load(stay(local), stay(conv_weight), stay(conv_bias[None]), stay(proj_weight.T))
    xconv, part = conv(before, *near)
    parts = [part] + swaps([part] * (tp - 1))
    silu, rates, skip, bias, step_w, out_w, quarter, gain = prepare(
        tp, stay(gate_in[0]), stay(decay_log), stay(residual[0]), stay(skip_gain[None]),
        stay(step_bias[None]), stay(step_weight), stay(out_weight), stay(norm_gain[None]),
    )
    y, elapsed, maps, state, up_w = scan(parts, xconv, rates, skip, bias, step_w, expert_weight)
    before = lax.ppermute(state, "ctx", [(0, 1)])
    own, *sent, down_w = mix(
        tp, maps, y, elapsed, rates, before, silu, quarter, out_w, expert_weight
    )
    arrived = swaps(sent)
    first, second, chooser, gate_w = route(expert_ids[0].T, experts, expert_weight)
    stream, *picked = pick(own, arrived, chooser)
    half = experts // 2
    rows = {j: swap(picked[j], "exp", j) for j in range(experts - 1, 0, -1)}
    piece_a = stack([rows[j] for j in range(half, experts)], [])
    piece_b = stack([picked[0]] + [rows[j] for j in range(1, half)], [piece_a])
    both = order([piece_a, piece_b])
    rows_a = [piece_a] + swaps([piece_a] * (tp - 1))
    rows_b = [piece_b] + swaps([piece_b] * (tp - 1))
    x_a = norm([rows_a], gain, [both])
    own_a, joined_a = expert(tp, x_a, gate_w, up_w, down_w, [], [])
    made_a = totals([joined_a[0]] + swaps(joined_a[1:]))
    x_b = norm([rows_b], gain, [own_a])
    _, joined_b = expert(tp, x_b, gate_w, up_w, down_w, [joined_a[0]], [made_a[0]])
    made_b = totals([joined_b[0]] + swaps(joined_b[1:]))
    back_a = [swap(piece, "exp", j) for j, piece in enumerate(made_a, half)]
    back_b = [made_b[0]] + [swap(made_b[j], "exp", j) for j in range(1, half)]
    gates = route_gates[0].T
    partial = blend(half * CAP, back_a, stream, first, second, gates, F32)
    return blend(0, back_b, partial, first, second, gates, BF16)[None]


def solution(mesh):
    placed = (
        P("exp", "ctx", "tp"),
        P("exp", "ctx", "tp"),
        P("exp", "ctx", None),
        P(None, "tp"),
        P("tp"),
        P("tp", None),
        P(None, "tp"),
        P("tp"),
        P(None, "tp"),
        P("tp"),
        P("tp", None),
        P(),
        P("exp", "ctx", None),
        P("exp", "ctx", None),
        P("exp", None, None, ("ctx", "tp")),
    )
    return jax.shard_map(
        body, mesh=mesh, in_specs=placed, out_specs=P("exp", "ctx", "tp"), check_vma=False
    )
```

```python
import functools
import math

import jax
import jax.numpy as jnp
from jax import lax
from jax.experimental import pallas as pl
from jax.experimental.pallas import tpu as pltpu
from jax.sharding import PartitionSpec as P

STATE = 16
DT_RANK = 256
CAP = 64
LOG2E = math.log2(math.e)
VMEM_LIMIT = 20 * 1024 * 1024
F32 = jnp.float32
BF16 = jnp.bfloat16


def params():
    return pltpu.CompilerParams(vmem_limit_bytes=VMEM_LIMIT)


def whole():
    return pl.BlockSpec(memory_space=pltpu.VMEM)


def shaped(shape, dtype):
    return jax.ShapeDtypeStruct(shape, dtype)


def swap(block, axis, k):
    return lax.ppermute(block, axis, [(i, i ^ k) for i in range(lax.axis_size(axis))])


def swaps(blocks):
    got = {k: swap(blocks[k - 1], "tp", k) for k in range(len(blocks), 0, -1)}
    return [got[k] for k in sorted(got)]


def sigmoid(x):
    return 1.0 / (1.0 + jnp.exp2(x * -LOG2E))


def stay(array):
    return pltpu.with_memory_space_constraint(array, pltpu.HBM)


def hbm():
    return pl.BlockSpec(memory_space=pltpu.HBM)


def unread(arrays):
    return [pl.BlockSpec(memory_space=pl.ANY)] * len(arrays)


def stack_kernel(count, *refs):
    for j, ref in enumerate(refs[:count]):
        rows = ref.shape[0]
        refs[-1][j * rows : (j + 1) * rows, :] = ref[...]


def stack(pieces, after):
    rows, width = pieces[0].shape
    return pl.pallas_call(
        functools.partial(stack_kernel, len(pieces)),
        out_shape=shaped((rows * len(pieces), width), pieces[0].dtype),
        in_specs=[whole()] * len(pieces) + unread(after),
        out_specs=whole(),
        compiler_params=params(),
        cost_estimate=cost(1e6, 0),
        name="stack",
    )(*pieces, *after)


def last_weight_kernel(expert_hbm, *refs):
    weight_ref, token_ref, sem = refs[-3:]
    copy = pltpu.make_async_copy(expert_hbm.at[0, 2], weight_ref, sem)
    copy.start()
    token_ref[...] = jnp.zeros_like(token_ref)
    copy.wait()


def last_weight(experts, after):
    return pl.pallas_call(
        last_weight_kernel,
        out_shape=(shaped(experts.shape[2:], BF16), shaped((8, 128), F32)),
        in_specs=[hbm()] + unread(after),
        out_specs=[whole()] * 2,
        scratch_shapes=[pltpu.SemaphoreType.DMA],
        compiler_params=params(),
        cost_estimate=cost(2e10, 0),
        name="weight",
    )(experts, *after)


def order_kernel(*refs):
    refs[-1][...] = jnp.zeros_like(refs[-1])


def order(after):
    return pl.pallas_call(
        order_kernel,
        out_shape=shaped((8, 128), F32),
        in_specs=unread(after),
        out_specs=whole(),
        compiler_params=params(),
        cost_estimate=cost(2e10, 0),
        name="order",
    )(*after)


def cost(flops, loaded=0):
    return pl.CostEstimate(flops=int(flops), bytes_accessed=int(loaded), transcendentals=0)


def route_kernel(ids_ref, expert_hbm, first_ref, second_ref, chooser_ref, weight_ref, sem):
    copy = pltpu.make_async_copy(expert_hbm.at[0, 0], weight_ref, sem)
    copy.start()
    rows, slots = first_ref.shape
    own = lax.axis_index("exp")
    ids = jnp.transpose(ids_ref[...].astype(F32)).astype(jnp.int32)
    lanes = lax.broadcasted_iota(jnp.int32, (rows, 128), 1)
    hot = [(ids[:, i : i + 1] == lanes).astype(F32) for i in range(2)]
    earlier = lax.broadcasted_iota(jnp.int32, (rows, rows), 1) < lax.broadcasted_iota(
        jnp.int32, (rows, rows), 0
    )
    ranks = jnp.dot(
        earlier.astype(F32).astype(BF16), (hot[0] + hot[1]).astype(BF16), preferred_element_type=F32
    )
    places = lax.broadcasted_iota(jnp.int32, (rows, slots), 1)
    tables = []
    for i in range(2):
        slot = jnp.sum(ranks * hot[i], axis=1, keepdims=True).astype(jnp.int32)
        place = jnp.bitwise_xor(ids[:, i : i + 1], own) * CAP + slot
        tables.append((place == places).astype(F32))
    first_ref[...] = tables[0].astype(BF16)
    second_ref[...] = tables[1].astype(BF16)
    chooser_ref[...] = jnp.transpose(tables[0] + tables[1]).astype(BF16)
    copy.wait()


def route(ids, expert_count, experts):
    rows, slots = ids.shape[1], expert_count * CAP
    return pl.pallas_call(
        route_kernel,
        out_shape=(
            shaped((rows, slots), BF16),
            shaped((rows, slots), BF16),
            shaped((slots, rows), BF16),
            shaped(experts.shape[2:], BF16),
        ),
        in_specs=[whole(), hbm()],
        out_specs=[whole()] * 4,
        scratch_shapes=[pltpu.SemaphoreType.DMA],
        compiler_params=params(),
        cost_estimate=cost(1e6, 8e6),
        name="route",
    )(ids, experts)


def conv_kernel(before_ref, x_ref, taps_ref, bias_ref, weight_ref, xconv_ref, part_ref, ext_ref):
    rows = x_ref.shape[0]
    halo = 16
    count = taps_ref.shape[0]
    ext_ref[:halo, :] = before_ref[rows - halo :, :].astype(F32)
    ext_ref[halo:, :] = x_ref[...].astype(F32)
    total = bias_ref[...] + taps_ref[count - 1 : count, :] * ext_ref[halo:, :]
    for k in range(count - 1):
        start = halo - (count - 1) + k
        total = total + taps_ref[k : k + 1, :] * ext_ref[start : start + rows, :]
    xconv = (total * sigmoid(total)).astype(BF16)
    xconv_ref[...] = xconv
    across = (((1,), (1,)), ((), ()))
    part_ref[:rows, :] = lax.dot_general(
        xconv, weight_ref[:DT_RANK, :], across, preferred_element_type=F32
    ).astype(BF16)
    maps = lax.dot_general(
        weight_ref[DT_RANK:, :], xconv, across, preferred_element_type=F32
    ).astype(BF16)
    part_ref[rows:, :rows] = maps[:STATE]
    part_ref[rows:, rows:] = maps[STATE:]


def conv(before, x, taps, bias, weight):
    rows, channels = x.shape
    return pl.pallas_call(
        conv_kernel,
        out_shape=(shaped((rows, channels), BF16), shaped((rows + STATE, DT_RANK), BF16)),
        in_specs=[whole()] * 5,
        out_specs=[whole()] * 2,
        scratch_shapes=[pltpu.VMEM((16 + rows, channels), F32)],
        compiler_params=params(),
        cost_estimate=cost(1e6, 1e6),
        name="conv",
    )(before, x, taps, bias, weight)


def load_kernel(count, *refs):
    copies = [
        pltpu.make_async_copy(refs[i], refs[count + i], refs[-1].at[i]) for i in range(count)
    ]
    for copy in copies:
        copy.start()
    for copy in copies:
        copy.wait()


def load(*arrays):
    count = len(arrays)
    return pl.pallas_call(
        functools.partial(load_kernel, count),
        out_shape=[shaped(array.shape, array.dtype) for array in arrays],
        in_specs=[hbm()] * count,
        out_specs=[whole()] * count,
        scratch_shapes=[pltpu.SemaphoreType.DMA((count,))],
        compiler_params=params(),
        cost_estimate=cost(1e6, 2e6),
        name="load",
    )(*arrays)


def prepare_kernel(
    xconv_ref, gate_hbm, decay_hbm, residual_hbm, skip_hbm, bias_hbm, step_hbm, out_hbm, gain_hbm,
    silu_ref, rates_ref, skipped_ref, bias_ref, step_ref, out_ref, quarter_ref, gain_ref,
    gate_ref, decay_ref, residual_ref, skip_ref, sems,
):
    copies = [
        pltpu.make_async_copy(source, target, sems.at[i])
        for i, (source, target) in enumerate(
            (
                (gate_hbm, gate_ref),
                (decay_hbm, decay_ref),
                (residual_hbm, residual_ref),
                (skip_hbm, skip_ref),
                (bias_hbm, bias_ref),
                (gain_hbm, gain_ref),
                (step_hbm, step_ref),
                (out_hbm, out_ref),
            )
        )
    ]
    for copy in copies:
        copy.start()
    for copy in copies[:4]:
        copy.wait()
    gate = gate_ref[...].astype(F32)
    silu_ref[...] = gate * sigmoid(gate)
    skipped_ref[...] = skip_ref[...] * xconv_ref[...].astype(F32)
    rates = -LOG2E * jnp.exp(decay_ref[...])
    for j in range(rates_ref.shape[1]):
        rates_ref[:, j, :] = rates[:, j * 128 : (j + 1) * 128]
    width = quarter_ref.shape[1]
    start = pl.multiple_of(lax.axis_index("tp") * width, 128)
    quarter_ref[...] = residual_ref[:, pl.ds(start, width)].astype(F32)
    for copy in copies[4:]:
        copy.wait()


def prepare(parts, xconv, gate, decay_log, residual, skip, bias, step_weight, out_weight, gain):
    rows, channels = gate.shape
    return pl.pallas_call(
        prepare_kernel,
        out_shape=(
            shaped((rows, channels), F32),
            shaped((STATE, channels // 128, 128), F32),
            shaped((rows, channels), F32),
            shaped(bias.shape, F32),
            shaped(step_weight.shape, BF16),
            shaped(out_weight.shape, BF16),
            shaped((rows, residual.shape[1] // parts), F32),
            shaped(gain.shape, F32),
        ),
        in_specs=[whole()] + [hbm()] * 8,
        out_specs=[whole()] * 8,
        scratch_shapes=[
            pltpu.VMEM((rows, channels), BF16),
            pltpu.VMEM(decay_log.shape, F32),
            pltpu.VMEM(residual.shape, BF16),
            pltpu.VMEM(skip.shape, F32),
            pltpu.SemaphoreType.DMA((8,)),
        ],
        compiler_params=params(),
        cost_estimate=cost(1e6, 6e6),
        name="prepare",
    )(xconv, gate, decay_log, residual, skip, bias, step_weight, out_weight, gain)


def scan_kernel(parts, *refs):
    part_refs = refs[:parts]
    xconv_ref, rates_ref, bias_ref, weight_ref, expert_hbm = refs[parts : parts + 5]
    y_ref, elapsed_ref, seen_ref, state_ref, second_ref = refs[parts + 5 : parts + 10]
    steps_ref, driven_ref, spread_ref, expert_sem = refs[parts + 10 :]
    rows = xconv_ref.shape[0]
    tiles = rates_ref.shape[1]
    expert_copy = pltpu.make_async_copy(expert_hbm.at[0, 1], second_ref, expert_sem)
    expert_copy.start()
    proj = part_refs[0][...].astype(F32)
    for ref in part_refs[1:]:
        proj = proj + ref[...].astype(F32)
    maps = proj[rows:]

    for t in range(rows):
        spread_ref[t] = jnp.broadcast_to(maps[:, t : t + 1], (STATE, 128))
        seen_ref[t] = jnp.broadcast_to(maps[:, rows + t : rows + t + 1], (STATE, 128))
    rank = proj[:rows].astype(BF16)
    raw = jnp.dot(rank, weight_ref[...], preferred_element_type=F32) + bias_ref[...]
    steps = jnp.maximum(raw, 0.0) + jnp.log1p(jnp.exp(-jnp.abs(raw)))
    driven = steps * xconv_ref[...].astype(F32)
    for j in range(tiles):
        cut = slice(j * 128, (j + 1) * 128)
        steps_ref[:, j, :] = steps[:, cut]
        driven_ref[:, j, :] = driven[:, cut]

    def step(t, carry):
        elapsed, states = carry
        now, driven = steps_ref[t], driven_ref[t]
        sums = [None, None]
        new = []
        for n in range(STATE):
            state = jnp.exp2(now * rates_ref[n]) * states[n] + driven * spread_ref[t, n : n + 1, :]
            new.append(state)
            term = state * seen_ref[t, n : n + 1, :]
            sums[n % 2] = term if sums[n % 2] is None else sums[n % 2] + term
        elapsed = elapsed + now
        y_ref[t] = sums[0] + sums[1]
        elapsed_ref[t] = elapsed
        return elapsed, tuple(new)

    zero = jnp.zeros((tiles, 128), F32)
    _, states = lax.fori_loop(0, rows, step, (zero, (zero,) * STATE), unroll=16)
    for n in range(STATE):
        state_ref[n] = states[n]
    expert_copy.wait()


def scan(pieces, xconv, rates, bias, weight, experts):
    rows = xconv.shape[0]
    tall = (rows, *rates.shape[1:])
    return pl.pallas_call(
        functools.partial(scan_kernel, len(pieces)),
        out_shape=(
            shaped(tall, F32),
            shaped(tall, F32),
            shaped((rows, STATE, 128), F32),
            shaped(rates.shape, F32),
            shaped(experts.shape[2:], BF16),
        ),
        in_specs=[whole()] * (len(pieces) + 4) + [hbm()],
        out_specs=[whole()] * 5,
        scratch_shapes=[
            pltpu.VMEM(tall, F32),
            pltpu.VMEM(tall, F32),
            pltpu.VMEM((rows, STATE, 128), F32),
            pltpu.SemaphoreType.DMA,
        ],
        compiler_params=params(),
        cost_estimate=cost(1e6, 14e6),
        name="scan",
    )(*pieces, xconv, rates, bias, weight, experts)


def mix_kernel(parts, *refs):
    seen_ref, y_ref, elapsed_ref, rates_ref, state_ref, skipped_ref, silu_ref, quarter_ref, weight_ref = refs[:9]
    own_ref, sent = refs[9], refs[10 : 9 + parts]
    sum_ref, gated_ref = refs[9 + parts :]
    rows, tiles, _ = y_ref.shape

    def step(t, carry):
        elapsed = elapsed_ref[t]
        sums = [y_ref[t], None]
        for n in range(STATE):
            term = jnp.exp2(elapsed * rates_ref[n]) * (state_ref[n] * seen_ref[t, n : n + 1, :])
            sums[n % 2] = term if sums[n % 2] is None else sums[n % 2] + term
        sum_ref[t] = sums[0] + sums[1]
        return carry

    first = lax.axis_index("ctx") == 0

    @pl.when(first)
    def _():
        sum_ref[...] = y_ref[...]

    @pl.when(jnp.logical_not(first))
    def _():
        lax.fori_loop(0, rows, step, 0, unroll=8)

    for j in range(tiles):
        cut = slice(j * 128, (j + 1) * 128)
        total = sum_ref[:, j, :] + skipped_ref[:, cut]
        gated_ref[:, cut] = (total * silu_ref[:, cut]).astype(BF16)
    own = lax.axis_index("tp")
    width = own_ref.shape[1]
    for k in range(parts):
        start = pl.multiple_of(jnp.bitwise_xor(own, k) * width, 128)
        product = jnp.dot(
            gated_ref[...], weight_ref[:, pl.ds(start, width)], preferred_element_type=F32
        )
        if k == 0:
            own_ref[...] = product + quarter_ref[...]
        else:
            sent[k - 1][...] = product.astype(BF16)


def mix(parts, seen, y, elapsed, rates, state, skipped, silu, quarter, weight):
    rows, tiles, _ = y.shape
    width = weight.shape[1] // parts
    return pl.pallas_call(
        functools.partial(mix_kernel, parts),
        out_shape=[shaped((rows, width), F32)]
        + [shaped((rows, width), BF16)] * (parts - 1),
        in_specs=[whole()] * 9,
        out_specs=[whole()] * parts,
        scratch_shapes=[
            pltpu.VMEM((rows, tiles, 128), F32),
            pltpu.VMEM((rows, tiles * 128), BF16),
        ],
        compiler_params=params(),
        cost_estimate=cost(1e6, 12e6),
        name="mix",
    )(seen, y, elapsed, rates, state, skipped, silu, quarter, weight)


def pick_kernel(parts, *refs):
    own_ref, arrived, chooser_ref = refs[0], refs[1:parts], refs[parts]
    stream_ref, out_refs = refs[parts + 1], refs[parts + 2 :]
    total = own_ref[...]
    for ref in arrived:
        total = total + ref[...].astype(F32)
    stream = total.astype(BF16)
    stream_ref[...] = stream
    picked = jnp.dot(chooser_ref[...], stream, preferred_element_type=F32).astype(BF16)
    for j, ref in enumerate(out_refs):
        ref[...] = picked[j * CAP : (j + 1) * CAP, :]


def pick(own, arrived, chooser):
    rows, width = own.shape
    experts = chooser.shape[0] // CAP
    return pl.pallas_call(
        functools.partial(pick_kernel, 1 + len(arrived)),
        out_shape=[shaped((rows, width), BF16)] + [shaped((CAP, width), BF16)] * experts,
        in_specs=[whole()] * (2 + len(arrived)),
        out_specs=[whole()] * (1 + experts),
        compiler_params=params(),
        cost_estimate=cost(1e6, 1e6),
        name="pick",
    )(own, *arrived, chooser)


def norm_kernel(parts, count, *refs):
    gain_ref, out_ref = refs[parts * count], refs[-1]
    own = lax.axis_index("tp")
    begin = 0
    for i in range(count):
        pieces = [ref[...].astype(F32) for ref in refs[i * parts : (i + 1) * parts]]
        rows, width = pieces[0].shape
        total = sum(jnp.sum(piece * piece, axis=1, keepdims=True) for piece in pieces)
        scale = lax.rsqrt(total / (width * parts) + 1e-6)
        for k, piece in enumerate(pieces):
            start = pl.multiple_of(jnp.bitwise_xor(own, k) * width, 128)
            out_ref[begin : begin + rows, pl.ds(start, width)] = (
                piece * scale * gain_ref[:, pl.ds(start, width)]
            ).astype(BF16)
        begin += rows


def norm(sets, gain, after):
    parts = len(sets[0])
    rows, width = sum(pieces[0].shape[0] for pieces in sets), sets[0][0].shape[1]
    return pl.pallas_call(
        functools.partial(norm_kernel, parts, len(sets)),
        out_shape=shaped((rows, width * parts), BF16),
        in_specs=[whole()] * (parts * len(sets) + 1) + unread(after),
        out_specs=whole(),
        compiler_params=params(),
        cost_estimate=cost(1e6, 1e6),
        name="norm",
    )(*sum(sets, []), gain, *after)


def hidden_kernel(x_ref, gate_ref, up_ref, *refs):
    hidden_ref = refs[-1]
    width = gate_ref.shape[1]
    size = 256 if width % 256 == 0 else width
    for i in range(width // size):
        cut = slice(i * size, (i + 1) * size)
        gate = jnp.dot(x_ref[...], gate_ref[:, cut], preferred_element_type=F32)
        up = jnp.dot(x_ref[...], up_ref[:, cut], preferred_element_type=F32)
        hidden_ref[:, cut] = (gate * sigmoid(gate) * up).astype(BF16)


def hidden_units(x, gate, up, after):
    rows, width = x.shape[0], gate.shape[1]
    return pl.pallas_call(
        hidden_kernel,
        out_shape=shaped((rows, width), BF16),
        in_specs=[whole()] * 3 + unread(after),
        out_specs=whole(),
        compiler_params=params(),
        cost_estimate=cost(1e6, 0),
        name="hidden",
    )(x, gate, up, *after)


def down_kernel(hidden_own_ref, hidden_other_ref, down_ref, *refs):
    own_ref, other_ref, hidden_ref = refs[-3:]
    rows = hidden_own_ref.shape[0]
    hidden_ref[:rows, :] = hidden_own_ref[...]
    hidden_ref[rows:, :] = hidden_other_ref[...]
    size = 256
    for i in range(down_ref.shape[0] // size):
        cut = slice(i * size, (i + 1) * size)
        product = lax.dot_general(
            hidden_ref[...], down_ref[cut, :], (((1,), (1,)), ((), ())), preferred_element_type=F32
        )
        own_ref[:, cut] = product[:rows]
        other_ref[:, cut] = product[rows:].astype(BF16)


def down_sums(hidden_own, hidden_other, down, after):
    rows, width = hidden_own.shape
    model = down.shape[0]
    return pl.pallas_call(
        down_kernel,
        out_shape=(shaped((rows, model), F32), shaped((rows, model), BF16)),
        in_specs=[whole()] * 3 + unread(after),
        out_specs=[whole()] * 2,
        scratch_shapes=[pltpu.VMEM((2 * rows, width), BF16)],
        compiler_params=params(),
        cost_estimate=cost(1e6, 0),
        name="down",
    )(hidden_own, hidden_other, down, *after)


def join_kernel(parts, own_ref, other_ref, *refs):
    out_refs = refs[-parts:]
    width = out_refs[0].shape[1]
    own = lax.axis_index("tp")
    for k, ref in enumerate(out_refs):
        cut = pl.ds(pl.multiple_of(jnp.bitwise_xor(own, k) * width, 128), width)
        ref[...] = (own_ref[:, cut] + other_ref[:, cut].astype(F32)).astype(ref.dtype)


def join(parts, own, other, after):
    rows, model = own.shape
    return pl.pallas_call(
        functools.partial(join_kernel, parts),
        out_shape=[shaped((rows, model // parts), BF16 if k else F32) for k in range(parts)],
        in_specs=[whole()] * 2 + unread(after),
        out_specs=[whole()] * parts,
        compiler_params=params(),
        cost_estimate=cost(1e6, 1e6),
        name="join",
    )(own, other, *after)


def total_kernel(parts, *refs):
    total = refs[0][...].astype(F32)
    for ref in refs[1:parts]:
        total = total + ref[...].astype(F32)
    total = total.astype(BF16)
    for j, ref in enumerate(refs[parts:]):
        ref[...] = total[j * CAP : (j + 1) * CAP, :]


def totals(pieces):
    rows, width = pieces[0].shape
    count = rows // CAP
    return pl.pallas_call(
        functools.partial(total_kernel, len(pieces)),
        out_shape=[shaped((CAP, width), BF16)] * count,
        in_specs=[whole()] * len(pieces),
        out_specs=[whole()] * count,
        compiler_params=params(),
        cost_estimate=cost(1e6, 1e6),
        name="totals",
    )(*pieces)


def blend_kernel(begin, count, *refs):
    back = refs[:count]
    base_ref, first_ref, second_ref, gates_ref, out_ref, rows_ref = refs[count:]
    for j, ref in enumerate(back):
        rows_ref[j * CAP : (j + 1) * CAP, :] = ref[...]
    rows = rows_ref[...]
    gates = jnp.transpose(gates_ref[...])
    cut = slice(begin, begin + count * CAP)
    moe = gates[:, 0:1] * jnp.dot(first_ref[:, cut], rows, preferred_element_type=F32)
    moe = moe + gates[:, 1:2] * jnp.dot(second_ref[:, cut], rows, preferred_element_type=F32)
    out_ref[...] = (base_ref[...].astype(F32) + moe).astype(out_ref.dtype)


def blend(begin, back, base, first, second, gates, dtype):
    count, width = len(back), base.shape[1]
    return pl.pallas_call(
        functools.partial(blend_kernel, begin, count),
        out_shape=shaped(base.shape, dtype),
        in_specs=[whole()] * (count + 4),
        out_specs=whole(),
        scratch_shapes=[pltpu.VMEM((count * CAP, width), BF16)],
        compiler_params=params(),
        cost_estimate=cost(1e6, 1e6),
        name="blend",
    )(*back, base, first, second, gates)


def expert(tp, x_own, gate, up, down, after_start, after_sums):
    x_other = swap(x_own, "ctx", 1)
    hidden_own = hidden_units(x_own, gate, up, after_start)
    hidden_other = hidden_units(x_other, gate, up, [hidden_own])
    sum_own, sum_other = down_sums(hidden_own, hidden_other, down, [])
    after_sums = [order([sum_other, *after_sums])] if after_sums else []
    joined = join(tp, sum_own, swap(sum_other, "ctx", 1), after_sums)
    return sum_own, joined


def body(
    conv_in,
    gate_in,
    residual,
    conv_weight,
    conv_bias,
    proj_weight,
    step_weight,
    step_bias,
    decay_log,
    skip_gain,
    out_weight,
    norm_gain,
    expert_ids,
    route_gates,
    expert_weight,
):
    tp, experts = lax.axis_size("tp"), lax.axis_size("exp")
    local = conv_in[0]
    before = lax.ppermute(local, "ctx", [(0, 1)])
    expert_weight = stay(expert_weight)
    near = load(stay(local), stay(conv_weight), stay(conv_bias[None]), stay(proj_weight.T))
    xconv, part = conv(before, *near)
    parts = [part] + swaps([part] * (tp - 1))
    silu, rates, skipped, bias, step_w, out_w, quarter, gain = prepare(
        tp, xconv, stay(gate_in[0]), stay(decay_log), stay(residual[0]), stay(skip_gain[None]),
        stay(step_bias[None]), stay(step_weight), stay(out_weight), stay(norm_gain[None]),
    )
    y, elapsed, seen, state, up_w = scan(parts, xconv, rates, bias, step_w, expert_weight)
    before = lax.ppermute(state, "ctx", [(0, 1)])
    own, *sent = mix(tp, seen, y, elapsed, rates, before, skipped, silu, quarter, out_w)
    arrived = swaps(sent)
    first, second, chooser, gate_w = route(expert_ids[0].T, experts, expert_weight)
    stream, *picked = pick(own, arrived, chooser)
    half = experts // 2
    rows = {j: swap(picked[j], "exp", j) for j in range(experts - 1, 0, -1)}
    piece_a = stack([rows[j] for j in range(half, experts)], [])
    piece_b = stack([picked[0]] + [rows[j] for j in range(1, half)], [piece_a])
    down_w, both = last_weight(expert_weight, [piece_a, piece_b])
    rows_a = [piece_a] + swaps([piece_a] * (tp - 1))
    rows_b = [piece_b] + swaps([piece_b] * (tp - 1))
    x_a = norm([rows_a], gain, [both])
    own_a, joined_a = expert(tp, x_a, gate_w, up_w, down_w, [], [])
    made_a = totals([joined_a[0]] + swaps(joined_a[1:]))
    x_b = norm([rows_b], gain, [own_a])
    _, joined_b = expert(tp, x_b, gate_w, up_w, down_w, [joined_a[0]], [made_a[0]])
    made_b = totals([joined_b[0]] + swaps(joined_b[1:]))
    back_a = [swap(piece, "exp", j) for j, piece in enumerate(made_a, half)]
    back_b = [made_b[0]] + [swap(made_b[j], "exp", j) for j in range(1, half)]
    gates = route_gates[0].T
    partial = blend(half * CAP, back_a, stream, first, second, gates, F32)
    return blend(0, back_b, partial, first, second, gates, BF16)[None]


def solution(mesh):
    placed = (
        P("exp", "ctx", "tp"),
        P("exp", "ctx", "tp"),
        P("exp", "ctx", None),
        P(None, "tp"),
        P("tp"),
        P("tp", None),
        P(None, "tp"),
        P("tp"),
        P(None, "tp"),
        P("tp"),
        P("tp", None),
        P(),
        P("exp", "ctx", None),
        P("exp", "ctx", None),
        P("exp", None, None, ("ctx", "tp")),
    )
    return jax.shard_map(
        body, mesh=mesh, in_specs=placed, out_specs=P("exp", "ctx", "tp"), check_vma=False
    )
```

```python
import functools
import math

import jax
import jax.numpy as jnp
from jax import lax
from jax.experimental import pallas as pl
from jax.experimental.pallas import tpu as pltpu
from jax.sharding import PartitionSpec as P

STATE = 16
DT_RANK = 256
CAP = 64
LOG2E = math.log2(math.e)
VMEM_LIMIT = 20 * 1024 * 1024
F32 = jnp.float32
BF16 = jnp.bfloat16


def params():
    return pltpu.CompilerParams(vmem_limit_bytes=VMEM_LIMIT)


def whole():
    return pl.BlockSpec(memory_space=pltpu.VMEM)


def shaped(shape, dtype):
    return jax.ShapeDtypeStruct(shape, dtype)


def swap(block, axis, k):
    return lax.ppermute(block, axis, [(i, i ^ k) for i in range(lax.axis_size(axis))])


def swaps(blocks):
    got = {k: swap(blocks[k - 1], "tp", k) for k in range(len(blocks), 0, -1)}
    return [got[k] for k in sorted(got)]


def sigmoid(x):
    return 1.0 / (1.0 + jnp.exp2(x * -LOG2E))


def stay(array):
    return pltpu.with_memory_space_constraint(array, pltpu.HBM)


def hbm():
    return pl.BlockSpec(memory_space=pltpu.HBM)


def unread(arrays):
    return [pl.BlockSpec(memory_space=pl.ANY)] * len(arrays)


def stack_kernel(count, *refs):
    for j, ref in enumerate(refs[:count]):
        rows = ref.shape[0]
        refs[-1][j * rows : (j + 1) * rows, :] = ref[...]


def stack(pieces, after):
    rows, width = pieces[0].shape
    return pl.pallas_call(
        functools.partial(stack_kernel, len(pieces)),
        out_shape=shaped((rows * len(pieces), width), pieces[0].dtype),
        in_specs=[whole()] * len(pieces) + unread(after),
        out_specs=whole(),
        compiler_params=params(),
        cost_estimate=cost(1e6, 0),
        name="stack",
    )(*pieces, *after)


def order_kernel(*refs):
    refs[-1][...] = jnp.zeros_like(refs[-1])


def order(after):
    return pl.pallas_call(
        order_kernel,
        out_shape=shaped((8, 128), F32),
        in_specs=unread(after),
        out_specs=whole(),
        compiler_params=params(),
        cost_estimate=cost(2e10, 0),
        name="order",
    )(*after)


def cost(flops, loaded=0):
    return pl.CostEstimate(flops=int(flops), bytes_accessed=int(loaded), transcendentals=0)


def route_kernel(ids_ref, expert_hbm, first_ref, second_ref, chooser_ref, weight_ref, sem):
    copy = pltpu.make_async_copy(expert_hbm.at[0, 0], weight_ref, sem)
    copy.start()
    rows, slots = first_ref.shape
    own = lax.axis_index("exp")
    ids = jnp.transpose(ids_ref[...].astype(F32)).astype(jnp.int32)
    lanes = lax.broadcasted_iota(jnp.int32, (rows, 128), 1)
    hot = [(ids[:, i : i + 1] == lanes).astype(F32) for i in range(2)]
    earlier = lax.broadcasted_iota(jnp.int32, (rows, rows), 1) < lax.broadcasted_iota(
        jnp.int32, (rows, rows), 0
    )
    ranks = jnp.dot(
        earlier.astype(F32).astype(BF16), (hot[0] + hot[1]).astype(BF16), preferred_element_type=F32
    )
    places = lax.broadcasted_iota(jnp.int32, (rows, slots), 1)
    tables = []
    for i in range(2):
        slot = jnp.sum(ranks * hot[i], axis=1, keepdims=True).astype(jnp.int32)
        place = jnp.bitwise_xor(ids[:, i : i + 1], own) * CAP + slot
        tables.append((place == places).astype(F32))
    first_ref[...] = tables[0].astype(BF16)
    second_ref[...] = tables[1].astype(BF16)
    chooser_ref[...] = jnp.transpose(tables[0] + tables[1]).astype(BF16)
    copy.wait()


def route(ids, expert_count, experts):
    rows, slots = ids.shape[1], expert_count * CAP
    return pl.pallas_call(
        route_kernel,
        out_shape=(
            shaped((rows, slots), BF16),
            shaped((rows, slots), BF16),
            shaped((slots, rows), BF16),
            shaped(experts.shape[2:], BF16),
        ),
        in_specs=[whole(), hbm()],
        out_specs=[whole()] * 4,
        scratch_shapes=[pltpu.SemaphoreType.DMA],
        compiler_params=params(),
        cost_estimate=cost(1e6, 8e6),
        name="route",
    )(ids, experts)


def conv_kernel(before_ref, x_ref, taps_ref, bias_ref, weight_ref, xconv_ref, part_ref, ext_ref):
    rows = x_ref.shape[0]
    halo = 16
    count = taps_ref.shape[0]
    ext_ref[:halo, :] = before_ref[rows - halo :, :].astype(F32)
    ext_ref[halo:, :] = x_ref[...].astype(F32)
    total = bias_ref[...] + taps_ref[count - 1 : count, :] * ext_ref[halo:, :]
    for k in range(count - 1):
        start = halo - (count - 1) + k
        total = total + taps_ref[k : k + 1, :] * ext_ref[start : start + rows, :]
    xconv = (total * sigmoid(total)).astype(BF16)
    xconv_ref[...] = xconv
    across = (((1,), (1,)), ((), ()))
    part_ref[:rows, :] = lax.dot_general(
        xconv, weight_ref[:DT_RANK, :], across, preferred_element_type=F32
    ).astype(BF16)
    maps = lax.dot_general(
        weight_ref[DT_RANK:, :], xconv, across, preferred_element_type=F32
    ).astype(BF16)
    part_ref[rows:, :rows] = maps[:STATE]
    part_ref[rows:, rows:] = maps[STATE:]


def conv(before, x, taps, bias, weight):
    rows, channels = x.shape
    return pl.pallas_call(
        conv_kernel,
        out_shape=(shaped((rows, channels), BF16), shaped((rows + STATE, DT_RANK), BF16)),
        in_specs=[whole()] * 5,
        out_specs=[whole()] * 2,
        scratch_shapes=[pltpu.VMEM((16 + rows, channels), F32)],
        compiler_params=params(),
        cost_estimate=cost(1e6, 1e6),
        name="conv",
    )(before, x, taps, bias, weight)


def load_kernel(count, *refs):
    copies = [
        pltpu.make_async_copy(refs[i], refs[count + i], refs[-1].at[i]) for i in range(count)
    ]
    for copy in copies:
        copy.start()
    for copy in copies:
        copy.wait()


def load(*arrays):
    count = len(arrays)
    return pl.pallas_call(
        functools.partial(load_kernel, count),
        out_shape=[shaped(array.shape, array.dtype) for array in arrays],
        in_specs=[hbm()] * count,
        out_specs=[whole()] * count,
        scratch_shapes=[pltpu.SemaphoreType.DMA((count,))],
        compiler_params=params(),
        cost_estimate=cost(1e6, 2e6),
        name="load",
    )(*arrays)


def prepare_kernel(
    xconv_ref, gate_hbm, decay_hbm, residual_hbm, skip_hbm, bias_hbm, step_hbm, out_hbm, gain_hbm,
    silu_ref, rates_ref, skipped_ref, bias_ref, step_ref, out_ref, quarter_ref, gain_ref,
    gate_ref, decay_ref, residual_ref, skip_ref, sems,
):
    copies = [
        pltpu.make_async_copy(source, target, sems.at[i])
        for i, (source, target) in enumerate(
            (
                (gate_hbm, gate_ref),
                (decay_hbm, decay_ref),
                (residual_hbm, residual_ref),
                (skip_hbm, skip_ref),
                (bias_hbm, bias_ref),
                (gain_hbm, gain_ref),
                (step_hbm, step_ref),
                (out_hbm, out_ref),
            )
        )
    ]
    for copy in copies:
        copy.start()
    for copy in copies[:4]:
        copy.wait()
    gate = gate_ref[...].astype(F32)
    silu_ref[...] = gate * sigmoid(gate)
    skipped_ref[...] = skip_ref[...] * xconv_ref[...].astype(F32)
    rates = -LOG2E * jnp.exp(decay_ref[...])
    for j in range(rates_ref.shape[1]):
        rates_ref[:, j, :] = rates[:, j * 128 : (j + 1) * 128]
    width = quarter_ref.shape[1]
    start = pl.multiple_of(lax.axis_index("tp") * width, 128)
    quarter_ref[...] = residual_ref[:, pl.ds(start, width)].astype(F32)
    for copy in copies[4:]:
        copy.wait()


def prepare(parts, xconv, gate, decay_log, residual, skip, bias, step_weight, out_weight, gain):
    rows, channels = gate.shape
    return pl.pallas_call(
        prepare_kernel,
        out_shape=(
            shaped((rows, channels), F32),
            shaped((STATE, channels // 128, 128), F32),
            shaped((rows, channels), F32),
            shaped(bias.shape, F32),
            shaped(step_weight.shape, BF16),
            shaped(out_weight.shape, BF16),
            shaped((rows, residual.shape[1] // parts), F32),
            shaped(gain.shape, F32),
        ),
        in_specs=[whole()] + [hbm()] * 8,
        out_specs=[whole()] * 8,
        scratch_shapes=[
            pltpu.VMEM((rows, channels), BF16),
            pltpu.VMEM(decay_log.shape, F32),
            pltpu.VMEM(residual.shape, BF16),
            pltpu.VMEM(skip.shape, F32),
            pltpu.SemaphoreType.DMA((8,)),
        ],
        compiler_params=params(),
        cost_estimate=cost(1e6, 6e6),
        name="prepare",
    )(xconv, gate, decay_log, residual, skip, bias, step_weight, out_weight, gain)


def scan_kernel(parts, *refs):
    part_refs = refs[:parts]
    xconv_ref, rates_ref, bias_ref, weight_ref, expert_hbm = refs[parts : parts + 5]
    y_ref, elapsed_ref, seen_ref, state_ref, second_ref = refs[parts + 5 : parts + 10]
    steps_ref, driven_ref, spread_ref, expert_sem = refs[parts + 10 :]
    rows = xconv_ref.shape[0]
    tiles = rates_ref.shape[1]
    expert_copy = pltpu.make_async_copy(expert_hbm.at[0, 1], second_ref, expert_sem)
    expert_copy.start()
    proj = part_refs[0][...].astype(F32)
    for ref in part_refs[1:]:
        proj = proj + ref[...].astype(F32)
    maps = proj[rows:]

    for t in range(rows):
        spread_ref[t] = jnp.broadcast_to(maps[:, t : t + 1], (STATE, 128))
        seen_ref[t] = jnp.broadcast_to(maps[:, rows + t : rows + t + 1], (STATE, 128))
    rank = proj[:rows].astype(BF16)
    raw = jnp.dot(rank, weight_ref[...], preferred_element_type=F32) + bias_ref[...]
    steps = jnp.maximum(raw, 0.0) + jnp.log1p(jnp.exp(-jnp.abs(raw)))
    driven = steps * xconv_ref[...].astype(F32)
    for j in range(tiles):
        cut = slice(j * 128, (j + 1) * 128)
        steps_ref[:, j, :] = steps[:, cut]
        driven_ref[:, j, :] = driven[:, cut]

    def step(t, carry):
        elapsed, states = carry
        now, driven = steps_ref[t], driven_ref[t]
        sums = [None, None]
        new = []
        for n in range(STATE):
            state = jnp.exp2(now * rates_ref[n]) * states[n] + driven * spread_ref[t, n : n + 1, :]
            new.append(state)
            term = state * seen_ref[t, n : n + 1, :]
            sums[n % 2] = term if sums[n % 2] is None else sums[n % 2] + term
        elapsed = elapsed + now
        y_ref[t] = sums[0] + sums[1]
        elapsed_ref[t] = elapsed
        return elapsed, tuple(new)

    zero = jnp.zeros((tiles, 128), F32)
    _, states = lax.fori_loop(0, rows, step, (zero, (zero,) * STATE), unroll=16)
    for n in range(STATE):
        state_ref[n] = states[n]
    expert_copy.wait()


def scan(pieces, xconv, rates, bias, weight, experts):
    rows = xconv.shape[0]
    tall = (rows, *rates.shape[1:])
    return pl.pallas_call(
        functools.partial(scan_kernel, len(pieces)),
        out_shape=(
            shaped(tall, F32),
            shaped(tall, F32),
            shaped((rows, STATE, 128), F32),
            shaped(rates.shape, F32),
            shaped(experts.shape[2:], BF16),
        ),
        in_specs=[whole()] * (len(pieces) + 4) + [hbm()],
        out_specs=[whole()] * 5,
        scratch_shapes=[
            pltpu.VMEM(tall, F32),
            pltpu.VMEM(tall, F32),
            pltpu.VMEM((rows, STATE, 128), F32),
            pltpu.SemaphoreType.DMA,
        ],
        compiler_params=params(),
        cost_estimate=cost(1e6, 14e6),
        name="scan",
    )(*pieces, xconv, rates, bias, weight, experts)


def mix_kernel(parts, *refs):
    seen_ref, y_ref, elapsed_ref, rates_ref, state_ref, skipped_ref, silu_ref, quarter_ref, weight_ref = refs[:9]
    own_ref, sent = refs[9], refs[10 : 9 + parts]
    sum_ref, gated_ref = refs[9 + parts :]
    rows, tiles, _ = y_ref.shape

    def step(t, carry):
        elapsed = elapsed_ref[t]
        sums = [y_ref[t], None]
        for n in range(STATE):
            term = jnp.exp2(elapsed * rates_ref[n]) * (state_ref[n] * seen_ref[t, n : n + 1, :])
            sums[n % 2] = term if sums[n % 2] is None else sums[n % 2] + term
        sum_ref[t] = sums[0] + sums[1]
        return carry

    first = lax.axis_index("ctx") == 0

    @pl.when(first)
    def _():
        sum_ref[...] = y_ref[...]

    @pl.when(jnp.logical_not(first))
    def _():
        lax.fori_loop(0, rows, step, 0, unroll=8)

    for j in range(tiles):
        cut = slice(j * 128, (j + 1) * 128)
        total = sum_ref[:, j, :] + skipped_ref[:, cut]
        gated_ref[:, cut] = (total * silu_ref[:, cut]).astype(BF16)
    own = lax.axis_index("tp")
    width = own_ref.shape[1]
    for k in range(parts):
        start = pl.multiple_of(jnp.bitwise_xor(own, k) * width, 128)
        product = jnp.dot(
            gated_ref[...], weight_ref[:, pl.ds(start, width)], preferred_element_type=F32
        )
        if k == 0:
            own_ref[...] = product + quarter_ref[...]
        else:
            sent[k - 1][...] = product.astype(BF16)


def mix(parts, seen, y, elapsed, rates, state, skipped, silu, quarter, weight):
    rows, tiles, _ = y.shape
    width = weight.shape[1] // parts
    return pl.pallas_call(
        functools.partial(mix_kernel, parts),
        out_shape=[shaped((rows, width), F32)]
        + [shaped((rows, width), BF16)] * (parts - 1),
        in_specs=[whole()] * 9,
        out_specs=[whole()] * parts,
        scratch_shapes=[
            pltpu.VMEM((rows, tiles, 128), F32),
            pltpu.VMEM((rows, tiles * 128), BF16),
        ],
        compiler_params=params(),
        cost_estimate=cost(1e6, 12e6),
        name="mix",
    )(seen, y, elapsed, rates, state, skipped, silu, quarter, weight)


def pick_kernel(parts, *refs):
    own_ref, arrived, chooser_ref = refs[0], refs[1:parts], refs[parts]
    stream_ref, out_refs = refs[parts + 1], refs[parts + 2 :]
    total = own_ref[...]
    for ref in arrived:
        total = total + ref[...].astype(F32)
    stream = total.astype(BF16)
    stream_ref[...] = stream
    picked = jnp.dot(chooser_ref[...], stream, preferred_element_type=F32).astype(BF16)
    for j, ref in enumerate(out_refs):
        ref[...] = picked[j * CAP : (j + 1) * CAP, :]


def pick(own, arrived, chooser):
    rows, width = own.shape
    experts = chooser.shape[0] // CAP
    return pl.pallas_call(
        functools.partial(pick_kernel, 1 + len(arrived)),
        out_shape=[shaped((rows, width), BF16)] + [shaped((CAP, width), BF16)] * experts,
        in_specs=[whole()] * (2 + len(arrived)),
        out_specs=[whole()] * (1 + experts),
        compiler_params=params(),
        cost_estimate=cost(1e6, 1e6),
        name="pick",
    )(own, *arrived, chooser)


def norm_kernel(parts, count, *refs):
    gain_ref, out_ref = refs[parts * count], refs[-1]
    own = lax.axis_index("tp")
    begin = 0
    for i in range(count):
        pieces = [ref[...].astype(F32) for ref in refs[i * parts : (i + 1) * parts]]
        rows, width = pieces[0].shape
        total = sum(jnp.sum(piece * piece, axis=1, keepdims=True) for piece in pieces)
        scale = lax.rsqrt(total / (width * parts) + 1e-6)
        for k, piece in enumerate(pieces):
            start = pl.multiple_of(jnp.bitwise_xor(own, k) * width, 128)
            out_ref[begin : begin + rows, pl.ds(start, width)] = (
                piece * scale * gain_ref[:, pl.ds(start, width)]
            ).astype(BF16)
        begin += rows


def norm(sets, gain, after):
    parts = len(sets[0])
    rows, width = sum(pieces[0].shape[0] for pieces in sets), sets[0][0].shape[1]
    return pl.pallas_call(
        functools.partial(norm_kernel, parts, len(sets)),
        out_shape=shaped((rows, width * parts), BF16),
        in_specs=[whole()] * (parts * len(sets) + 1) + unread(after),
        out_specs=whole(),
        compiler_params=params(),
        cost_estimate=cost(1e6, 1e6),
        name="norm",
    )(*sum(sets, []), gain, *after)


def hidden_kernel(part, x_ref, gate_ref, up_ref, *refs):
    if part is None:
        hidden_ref = refs[-1]
    else:
        hidden_ref, weight_ref, sem = refs[-3:]
        count = weight_ref.shape[0]
        copy = pltpu.make_async_copy(refs[0].at[0, 2, pl.ds(part * count, count)], weight_ref, sem)
        copy.start()
    width = gate_ref.shape[1]
    size = 256 if width % 256 == 0 else width
    for i in range(width // size):
        cut = slice(i * size, (i + 1) * size)
        gate = jnp.dot(x_ref[...], gate_ref[:, cut], preferred_element_type=F32)
        up = jnp.dot(x_ref[...], up_ref[:, cut], preferred_element_type=F32)
        hidden_ref[:, cut] = (gate * sigmoid(gate) * up).astype(BF16)
    if part is not None:
        copy.wait()


def hidden_units(x, gate, up, after, experts=None, part=None):
    rows, width = x.shape[0], gate.shape[1]
    made = [shaped((rows, width), BF16)]
    extra = []
    if part is not None:
        made.append(shaped((gate.shape[0] // 2, width), BF16))
        extra = [experts]
    return pl.pallas_call(
        functools.partial(hidden_kernel, part),
        out_shape=made,
        in_specs=[whole()] * 3 + [hbm()] * len(extra) + unread(after),
        out_specs=[whole()] * len(made),
        scratch_shapes=[pltpu.SemaphoreType.DMA] * len(extra),
        compiler_params=params(),
        cost_estimate=cost(1e6, 0),
        name="hidden",
    )(x, gate, up, *extra, *after)


def down_kernel(hidden_own_ref, hidden_other_ref, low_ref, high_ref, *refs):
    own_ref, other_ref, hidden_ref = refs[-3:]
    rows = hidden_own_ref.shape[0]
    hidden_ref[:rows, :] = hidden_own_ref[...]
    hidden_ref[rows:, :] = hidden_other_ref[...]
    size = 256
    half = low_ref.shape[0]
    for i in range(2 * half // size):
        cut = slice(i * size, (i + 1) * size)
        down_ref, begin = (low_ref, i * size) if i * size < half else (high_ref, i * size - half)
        product = lax.dot_general(
            hidden_ref[...],
            down_ref[begin : begin + size, :],
            (((1,), (1,)), ((), ())),
            preferred_element_type=F32,
        )
        own_ref[:, cut] = product[:rows]
        other_ref[:, cut] = product[rows:].astype(BF16)


def down_sums(hidden_own, hidden_other, down, after):
    rows, width = hidden_own.shape
    model = 2 * down[0].shape[0]
    return pl.pallas_call(
        down_kernel,
        out_shape=(shaped((rows, model), F32), shaped((rows, model), BF16)),
        in_specs=[whole()] * 4 + unread(after),
        out_specs=[whole()] * 2,
        scratch_shapes=[pltpu.VMEM((2 * rows, width), BF16)],
        compiler_params=params(),
        cost_estimate=cost(1e6, 0),
        name="down",
    )(hidden_own, hidden_other, *down, *after)


def join_kernel(parts, own_ref, other_ref, *refs):
    out_refs = refs[-parts:]
    width = out_refs[0].shape[1]
    own = lax.axis_index("tp")
    for k, ref in enumerate(out_refs):
        cut = pl.ds(pl.multiple_of(jnp.bitwise_xor(own, k) * width, 128), width)
        ref[...] = (own_ref[:, cut] + other_ref[:, cut].astype(F32)).astype(ref.dtype)


def join(parts, own, other, after):
    rows, model = own.shape
    return pl.pallas_call(
        functools.partial(join_kernel, parts),
        out_shape=[shaped((rows, model // parts), BF16 if k else F32) for k in range(parts)],
        in_specs=[whole()] * 2 + unread(after),
        out_specs=[whole()] * parts,
        compiler_params=params(),
        cost_estimate=cost(1e6, 1e6),
        name="join",
    )(own, other, *after)


def total_kernel(parts, *refs):
    total = refs[0][...].astype(F32)
    for ref in refs[1:parts]:
        total = total + ref[...].astype(F32)
    total = total.astype(BF16)
    for j, ref in enumerate(refs[parts:]):
        ref[...] = total[j * CAP : (j + 1) * CAP, :]


def totals(pieces):
    rows, width = pieces[0].shape
    count = rows // CAP
    return pl.pallas_call(
        functools.partial(total_kernel, len(pieces)),
        out_shape=[shaped((CAP, width), BF16)] * count,
        in_specs=[whole()] * len(pieces),
        out_specs=[whole()] * count,
        compiler_params=params(),
        cost_estimate=cost(1e6, 1e6),
        name="totals",
    )(*pieces)


def blend_kernel(begin, count, *refs):
    back = refs[:count]
    base_ref, first_ref, second_ref, gates_ref, out_ref, rows_ref = refs[count:]
    for j, ref in enumerate(back):
        rows_ref[j * CAP : (j + 1) * CAP, :] = ref[...]
    rows = rows_ref[...]
    gates = jnp.transpose(gates_ref[...])
    cut = slice(begin, begin + count * CAP)
    moe = gates[:, 0:1] * jnp.dot(first_ref[:, cut], rows, preferred_element_type=F32)
    moe = moe + gates[:, 1:2] * jnp.dot(second_ref[:, cut], rows, preferred_element_type=F32)
    out_ref[...] = (base_ref[...].astype(F32) + moe).astype(out_ref.dtype)


def blend(begin, back, base, first, second, gates, dtype):
    count, width = len(back), base.shape[1]
    return pl.pallas_call(
        functools.partial(blend_kernel, begin, count),
        out_shape=shaped(base.shape, dtype),
        in_specs=[whole()] * (count + 4),
        out_specs=whole(),
        scratch_shapes=[pltpu.VMEM((count * CAP, width), BF16)],
        compiler_params=params(),
        cost_estimate=cost(1e6, 1e6),
        name="blend",
    )(*back, base, first, second, gates)


def body(
    conv_in,
    gate_in,
    residual,
    conv_weight,
    conv_bias,
    proj_weight,
    step_weight,
    step_bias,
    decay_log,
    skip_gain,
    out_weight,
    norm_gain,
    expert_ids,
    route_gates,
    expert_weight,
):
    tp, experts = lax.axis_size("tp"), lax.axis_size("exp")
    local = conv_in[0]
    before = lax.ppermute(local, "ctx", [(0, 1)])
    expert_weight = stay(expert_weight)
    near = load(stay(local), stay(conv_weight), stay(conv_bias[None]), stay(proj_weight.T))
    xconv, part = conv(before, *near)
    parts = [part] + swaps([part] * (tp - 1))
    silu, rates, skipped, bias, step_w, out_w, quarter, gain = prepare(
        tp, xconv, stay(gate_in[0]), stay(decay_log), stay(residual[0]), stay(skip_gain[None]),
        stay(step_bias[None]), stay(step_weight), stay(out_weight), stay(norm_gain[None]),
    )
    y, elapsed, seen, state, up_w = scan(parts, xconv, rates, bias, step_w, expert_weight)
    before = lax.ppermute(state, "ctx", [(0, 1)])
    own, *sent = mix(tp, seen, y, elapsed, rates, before, skipped, silu, quarter, out_w)
    arrived = swaps(sent)
    first, second, chooser, gate_w = route(expert_ids[0].T, experts, expert_weight)
    stream, *picked = pick(own, arrived, chooser)
    half = experts // 2
    rows = [picked[0]] + [swap(picked[j], "exp", j) for j in range(1, experts)]
    piece_b = stack(rows[:half], [])
    both = order([rows[half], piece_b])
    first_a = rows[experts - 1]
    second_a = rows[half] if half == 2 else stack(rows[half : experts - 1], [])
    sets = [[piece] + swaps([piece] * (tp - 1)) for piece in (first_a, second_a, piece_b)]
    x_a = norm(sets[:2], gain, [both])
    own_a, low = hidden_units(x_a, gate_w, up_w, [], expert_weight, 0)
    other_a, high = hidden_units(swap(x_a, "ctx", 1), gate_w, up_w, [own_a, order([x_a])], expert_weight, 1)
    down_w = (low, high)
    sum_a, sent_a = down_sums(own_a, other_a, down_w, [])
    joined_a = join(tp, sum_a, swap(sent_a, "ctx", 1), [])
    made_a = totals([joined_a[0]] + swaps(joined_a[1:]))
    x_b = norm(sets[2:], gain, [sum_a])
    own_b, = hidden_units(x_b, gate_w, up_w, [joined_a[0]])
    other_b, = hidden_units(swap(x_b, "ctx", 1), gate_w, up_w, [own_b])
    sum_b, sent_b = down_sums(own_b, other_b, down_w, [])
    joined_b = join(tp, sum_b, swap(sent_b, "ctx", 1), [order([sent_b, made_a[0]])])
    made_b = totals([joined_b[0]] + swaps(joined_b[1:]))
    made_a = made_a[1:] + made_a[:1]
    back_a = [swap(piece, "exp", j) for j, piece in enumerate(made_a, half)]
    back_b = [made_b[0]] + [swap(made_b[j], "exp", j) for j in range(1, half)]
    gates = route_gates[0].T
    partial = blend(half * CAP, back_a, stream, first, second, gates, F32)
    return blend(0, back_b, partial, first, second, gates, BF16)[None]


def solution(mesh):
    placed = (
        P("exp", "ctx", "tp"),
        P("exp", "ctx", "tp"),
        P("exp", "ctx", None),
        P(None, "tp"),
        P("tp"),
        P("tp", None),
        P(None, "tp"),
        P("tp"),
        P(None, "tp"),
        P("tp"),
        P("tp", None),
        P(),
        P("exp", "ctx", None),
        P("exp", "ctx", None),
        P("exp", None, None, ("ctx", "tp")),
    )
    return jax.shard_map(
        body, mesh=mesh, in_specs=placed, out_specs=P("exp", "ctx", "tp"), check_vma=False
    )
```

```python
import functools
import math

import jax
import jax.numpy as jnp
from jax import lax
from jax.experimental import pallas as pl
from jax.experimental.pallas import tpu as pltpu
from jax.sharding import PartitionSpec as P

STATE = 16
DT_RANK = 256
CAP = 64
LOG2E = math.log2(math.e)
VMEM_LIMIT = 20 * 1024 * 1024
F32 = jnp.float32
BF16 = jnp.bfloat16


def params():
    return pltpu.CompilerParams(vmem_limit_bytes=VMEM_LIMIT)


def whole():
    return pl.BlockSpec(memory_space=pltpu.VMEM)


def shaped(shape, dtype):
    return jax.ShapeDtypeStruct(shape, dtype)


def swap(block, axis, k):
    return lax.ppermute(block, axis, [(i, i ^ k) for i in range(lax.axis_size(axis))])


def swaps(blocks):
    return [swap(block, "tp", k) for k, block in enumerate(blocks, 1)]


def sigmoid(x):
    return 1.0 / (1.0 + jnp.exp2(x * -LOG2E))


def stay(array):
    return pltpu.with_memory_space_constraint(array, pltpu.HBM)


def hbm():
    return pl.BlockSpec(memory_space=pltpu.HBM)


def unread(arrays):
    return [pl.BlockSpec(memory_space=pl.ANY)] * len(arrays)


def stack_kernel(count, *refs):
    for j, ref in enumerate(refs[:count]):
        rows = ref.shape[0]
        refs[-1][j * rows : (j + 1) * rows, :] = ref[...]


def stack(pieces, after):
    rows, width = pieces[0].shape
    return pl.pallas_call(
        functools.partial(stack_kernel, len(pieces)),
        out_shape=shaped((rows * len(pieces), width), pieces[0].dtype),
        in_specs=[whole()] * len(pieces) + unread(after),
        out_specs=whole(),
        compiler_params=params(),
        cost_estimate=cost(1e6, 0),
        name="stack",
    )(*pieces, *after)


def order_kernel(*refs):
    refs[-1][...] = jnp.zeros_like(refs[-1])


def order(after):
    return pl.pallas_call(
        order_kernel,
        out_shape=shaped((8, 128), F32),
        in_specs=unread(after),
        out_specs=whole(),
        compiler_params=params(),
        cost_estimate=cost(2e10, 0),
        name="order",
    )(*after)


def cost(flops, loaded=0):
    return pl.CostEstimate(flops=int(flops), bytes_accessed=int(loaded), transcendentals=0)


def route_kernel(ids_ref, expert_hbm, first_ref, second_ref, chooser_ref, weight_ref, sem):
    copy = pltpu.make_async_copy(expert_hbm.at[0, 0], weight_ref, sem)
    copy.start()
    rows, slots = first_ref.shape
    own = lax.axis_index("exp")
    ids = jnp.transpose(ids_ref[...].astype(F32)).astype(jnp.int32)
    lanes = lax.broadcasted_iota(jnp.int32, (rows, 128), 1)
    hot = [(ids[:, i : i + 1] == lanes).astype(F32) for i in range(2)]
    earlier = lax.broadcasted_iota(jnp.int32, (rows, rows), 1) < lax.broadcasted_iota(
        jnp.int32, (rows, rows), 0
    )
    ranks = jnp.dot(
        earlier.astype(F32).astype(BF16), (hot[0] + hot[1]).astype(BF16), preferred_element_type=F32
    )
    places = lax.broadcasted_iota(jnp.int32, (rows, slots), 1)
    tables = []
    for i in range(2):
        slot = jnp.sum(ranks * hot[i], axis=1, keepdims=True).astype(jnp.int32)
        place = jnp.bitwise_xor(ids[:, i : i + 1], own) * CAP + slot
        tables.append((place == places).astype(F32))
    first_ref[...] = tables[0].astype(BF16)
    second_ref[...] = tables[1].astype(BF16)
    chooser_ref[...] = jnp.transpose(tables[0] + tables[1]).astype(BF16)
    copy.wait()


def route(ids, expert_count, experts):
    rows, slots = ids.shape[1], expert_count * CAP
    return pl.pallas_call(
        route_kernel,
        out_shape=(
            shaped((rows, slots), BF16),
            shaped((rows, slots), BF16),
            shaped((slots, rows), BF16),
            shaped(experts.shape[2:], BF16),
        ),
        in_specs=[whole(), hbm()],
        out_specs=[whole()] * 4,
        scratch_shapes=[pltpu.SemaphoreType.DMA],
        compiler_params=params(),
        cost_estimate=cost(1e6, 8e6),
        name="route",
    )(ids, experts)


def conv_kernel(before_ref, x_ref, taps_ref, bias_ref, weight_ref, xconv_ref, part_ref, ext_ref):
    rows = x_ref.shape[0]
    halo = 16
    count = taps_ref.shape[0]
    ext_ref[:halo, :] = before_ref[rows - halo :, :].astype(F32)
    ext_ref[halo:, :] = x_ref[...].astype(F32)
    total = bias_ref[...] + taps_ref[count - 1 : count, :] * ext_ref[halo:, :]
    for k in range(count - 1):
        start = halo - (count - 1) + k
        total = total + taps_ref[k : k + 1, :] * ext_ref[start : start + rows, :]
    xconv = (total * sigmoid(total)).astype(BF16)
    xconv_ref[...] = xconv
    across = (((1,), (1,)), ((), ()))
    part_ref[:rows, :] = lax.dot_general(
        xconv, weight_ref[:DT_RANK, :], across, preferred_element_type=F32
    ).astype(BF16)
    maps = lax.dot_general(
        weight_ref[DT_RANK:, :], xconv, across, preferred_element_type=F32
    ).astype(BF16)
    part_ref[rows:, :rows] = maps[:STATE]
    part_ref[rows:, rows:] = maps[STATE:]


def conv(before, x, taps, bias, weight):
    rows, channels = x.shape
    return pl.pallas_call(
        conv_kernel,
        out_shape=(shaped((rows, channels), BF16), shaped((rows + STATE, DT_RANK), BF16)),
        in_specs=[whole()] * 5,
        out_specs=[whole()] * 2,
        scratch_shapes=[pltpu.VMEM((16 + rows, channels), F32)],
        compiler_params=params(),
        cost_estimate=cost(1e6, 1e6),
        name="conv",
    )(before, x, taps, bias, weight)


def load_kernel(count, *refs):
    copies = [
        pltpu.make_async_copy(refs[i], refs[count + i], refs[-1].at[i]) for i in range(count)
    ]
    for copy in copies:
        copy.start()
    for copy in copies:
        copy.wait()


def load(*arrays):
    count = len(arrays)
    return pl.pallas_call(
        functools.partial(load_kernel, count),
        out_shape=[shaped(array.shape, array.dtype) for array in arrays],
        in_specs=[hbm()] * count,
        out_specs=[whole()] * count,
        scratch_shapes=[pltpu.SemaphoreType.DMA((count,))],
        compiler_params=params(),
        cost_estimate=cost(1e6, 2e6),
        name="load",
    )(*arrays)


def prepare_kernel(
    xconv_ref, gate_hbm, decay_hbm, residual_hbm, skip_hbm, bias_hbm, step_hbm, out_hbm, gain_hbm,
    silu_ref, rates_ref, skipped_ref, bias_ref, step_ref, out_ref, quarter_ref, gain_ref,
    gate_ref, decay_ref, residual_ref, skip_ref, sems,
):
    copies = [
        pltpu.make_async_copy(source, target, sems.at[i])
        for i, (source, target) in enumerate(
            (
                (gate_hbm, gate_ref),
                (decay_hbm, decay_ref),
                (residual_hbm, residual_ref),
                (skip_hbm, skip_ref),
                (bias_hbm, bias_ref),
                (gain_hbm, gain_ref),
                (step_hbm, step_ref),
                (out_hbm, out_ref),
            )
        )
    ]
    for copy in copies:
        copy.start()
    for copy in copies[:4]:
        copy.wait()
    gate = gate_ref[...].astype(F32)
    silu_ref[...] = gate * sigmoid(gate)
    skipped_ref[...] = skip_ref[...] * xconv_ref[...].astype(F32)
    rates = -LOG2E * jnp.exp(decay_ref[...])
    for j in range(rates_ref.shape[1]):
        rates_ref[:, j, :] = rates[:, j * 128 : (j + 1) * 128]
    width = quarter_ref.shape[1]
    start = pl.multiple_of(lax.axis_index("tp") * width, 128)
    quarter_ref[...] = residual_ref[:, pl.ds(start, width)].astype(F32)
    for copy in copies[4:]:
        copy.wait()


def prepare(parts, xconv, gate, decay_log, residual, skip, bias, step_weight, out_weight, gain):
    rows, channels = gate.shape
    return pl.pallas_call(
        prepare_kernel,
        out_shape=(
            shaped((rows, channels), F32),
            shaped((STATE, channels // 128, 128), F32),
            shaped((rows, channels), F32),
            shaped(bias.shape, F32),
            shaped(step_weight.shape, BF16),
            shaped(out_weight.shape, BF16),
            shaped((rows, residual.shape[1] // parts), F32),
            shaped(gain.shape, F32),
        ),
        in_specs=[whole()] + [hbm()] * 8,
        out_specs=[whole()] * 8,
        scratch_shapes=[
            pltpu.VMEM((rows, channels), BF16),
            pltpu.VMEM(decay_log.shape, F32),
            pltpu.VMEM(residual.shape, BF16),
            pltpu.VMEM(skip.shape, F32),
            pltpu.SemaphoreType.DMA((8,)),
        ],
        compiler_params=params(),
        cost_estimate=cost(1e6, 6e6),
        name="prepare",
    )(xconv, gate, decay_log, residual, skip, bias, step_weight, out_weight, gain)


def scan_kernel(parts, *refs):
    part_refs = refs[:parts]
    xconv_ref, rates_ref, bias_ref, weight_ref, expert_hbm = refs[parts : parts + 5]
    y_ref, elapsed_ref, seen_ref, state_ref, second_ref = refs[parts + 5 : parts + 10]
    steps_ref, driven_ref, spread_ref, expert_sem = refs[parts + 10 :]
    rows = xconv_ref.shape[0]
    tiles = rates_ref.shape[1]
    expert_copy = pltpu.make_async_copy(expert_hbm.at[0, 1], second_ref, expert_sem)
    expert_copy.start()
    proj = part_refs[0][...].astype(F32)
    for ref in part_refs[1:]:
        proj = proj + ref[...].astype(F32)
    maps = proj[rows:]

    for t in range(rows):
        spread_ref[t] = jnp.broadcast_to(maps[:, t : t + 1], (STATE, 128))
        seen_ref[t] = jnp.broadcast_to(maps[:, rows + t : rows + t + 1], (STATE, 128))
    rank = proj[:rows].astype(BF16)
    raw = jnp.dot(rank, weight_ref[...], preferred_element_type=F32) + bias_ref[...]
    steps = jnp.maximum(raw, 0.0) + jnp.log1p(jnp.exp(-jnp.abs(raw)))
    driven = steps * xconv_ref[...].astype(F32)
    for j in range(tiles):
        cut = slice(j * 128, (j + 1) * 128)
        steps_ref[:, j, :] = steps[:, cut]
        driven_ref[:, j, :] = driven[:, cut]

    def step(t, carry):
        elapsed, states = carry
        now, driven = steps_ref[t], driven_ref[t]
        sums = [None, None]
        new = []
        for n in range(STATE):
            state = jnp.exp2(now * rates_ref[n]) * states[n] + driven * spread_ref[t, n : n + 1, :]
            new.append(state)
            term = state * seen_ref[t, n : n + 1, :]
            sums[n % 2] = term if sums[n % 2] is None else sums[n % 2] + term
        elapsed = elapsed + now
        y_ref[t] = sums[0] + sums[1]
        elapsed_ref[t] = elapsed
        return elapsed, tuple(new)

    zero = jnp.zeros((tiles, 128), F32)
    _, states = lax.fori_loop(0, rows, step, (zero, (zero,) * STATE), unroll=16)
    for n in range(STATE):
        state_ref[n] = states[n]
    expert_copy.wait()


def scan(pieces, xconv, rates, bias, weight, experts):
    rows = xconv.shape[0]
    tall = (rows, *rates.shape[1:])
    return pl.pallas_call(
        functools.partial(scan_kernel, len(pieces)),
        out_shape=(
            shaped(tall, F32),
            shaped(tall, F32),
            shaped((rows, STATE, 128), F32),
            shaped(rates.shape, F32),
            shaped(experts.shape[2:], BF16),
        ),
        in_specs=[whole()] * (len(pieces) + 4) + [hbm()],
        out_specs=[whole()] * 5,
        scratch_shapes=[
            pltpu.VMEM(tall, F32),
            pltpu.VMEM(tall, F32),
            pltpu.VMEM((rows, STATE, 128), F32),
            pltpu.SemaphoreType.DMA,
        ],
        compiler_params=params(),
        cost_estimate=cost(1e6, 14e6),
        name="scan",
    )(*pieces, xconv, rates, bias, weight, experts)


def mix_kernel(parts, *refs):
    seen_ref, y_ref, elapsed_ref, rates_ref, state_ref, skipped_ref, silu_ref, quarter_ref, weight_ref = refs[:9]
    own_ref, sent = refs[9], refs[10 : 9 + parts]
    sum_ref, gated_ref = refs[9 + parts :]
    rows, tiles, _ = y_ref.shape

    def step(t, carry):
        elapsed = elapsed_ref[t]
        sums = [y_ref[t], None]
        for n in range(STATE):
            term = jnp.exp2(elapsed * rates_ref[n]) * (state_ref[n] * seen_ref[t, n : n + 1, :])
            sums[n % 2] = term if sums[n % 2] is None else sums[n % 2] + term
        sum_ref[t] = sums[0] + sums[1]
        return carry

    first = lax.axis_index("ctx") == 0

    @pl.when(first)
    def _():
        sum_ref[...] = y_ref[...]

    @pl.when(jnp.logical_not(first))
    def _():
        lax.fori_loop(0, rows, step, 0, unroll=8)

    for j in range(tiles):
        cut = slice(j * 128, (j + 1) * 128)
        total = sum_ref[:, j, :] + skipped_ref[:, cut]
        gated_ref[:, cut] = (total * silu_ref[:, cut]).astype(BF16)
    own = lax.axis_index("tp")
    width = own_ref.shape[1]
    for k in range(parts):
        start = pl.multiple_of(jnp.bitwise_xor(own, k) * width, 128)
        product = jnp.dot(
            gated_ref[...], weight_ref[:, pl.ds(start, width)], preferred_element_type=F32
        )
        if k == 0:
            own_ref[...] = product + quarter_ref[...]
        else:
            sent[k - 1][...] = product.astype(BF16)


def mix(parts, seen, y, elapsed, rates, state, skipped, silu, quarter, weight):
    rows, tiles, _ = y.shape
    width = weight.shape[1] // parts
    return pl.pallas_call(
        functools.partial(mix_kernel, parts),
        out_shape=[shaped((rows, width), F32)]
        + [shaped((rows, width), BF16)] * (parts - 1),
        in_specs=[whole()] * 9,
        out_specs=[whole()] * parts,
        scratch_shapes=[
            pltpu.VMEM((rows, tiles, 128), F32),
            pltpu.VMEM((rows, tiles * 128), BF16),
        ],
        compiler_params=params(),
        cost_estimate=cost(1e6, 12e6),
        name="mix",
    )(seen, y, elapsed, rates, state, skipped, silu, quarter, weight)


def pick_kernel(parts, *refs):
    own_ref, arrived, chooser_ref = refs[0], refs[1:parts], refs[parts]
    stream_ref, out_refs = refs[parts + 1], refs[parts + 2 :]
    total = own_ref[...]
    for ref in arrived:
        total = total + ref[...].astype(F32)
    stream = total.astype(BF16)
    stream_ref[...] = stream
    picked = jnp.dot(chooser_ref[...], stream, preferred_element_type=F32).astype(BF16)
    for j, ref in enumerate(out_refs):
        ref[...] = picked[j * CAP : (j + 1) * CAP, :]


def pick(own, arrived, chooser):
    rows, width = own.shape
    experts = chooser.shape[0] // CAP
    return pl.pallas_call(
        functools.partial(pick_kernel, 1 + len(arrived)),
        out_shape=[shaped((rows, width), BF16)] + [shaped((CAP, width), BF16)] * experts,
        in_specs=[whole()] * (2 + len(arrived)),
        out_specs=[whole()] * (1 + experts),
        compiler_params=params(),
        cost_estimate=cost(1e6, 1e6),
        name="pick",
    )(own, *arrived, chooser)


def norm_kernel(parts, count, *refs):
    gain_ref, out_ref = refs[parts * count], refs[-1]
    own = lax.axis_index("tp")
    begin = 0
    for i in range(count):
        pieces = [ref[...].astype(F32) for ref in refs[i * parts : (i + 1) * parts]]
        rows, width = pieces[0].shape
        total = sum(jnp.sum(piece * piece, axis=1, keepdims=True) for piece in pieces)
        scale = lax.rsqrt(total / (width * parts) + 1e-6)
        for k, piece in enumerate(pieces):
            start = pl.multiple_of(jnp.bitwise_xor(own, k) * width, 128)
            out_ref[begin : begin + rows, pl.ds(start, width)] = (
                piece * scale * gain_ref[:, pl.ds(start, width)]
            ).astype(BF16)
        begin += rows


def norm(sets, gain, after):
    parts = len(sets[0])
    rows, width = sum(pieces[0].shape[0] for pieces in sets), sets[0][0].shape[1]
    return pl.pallas_call(
        functools.partial(norm_kernel, parts, len(sets)),
        out_shape=shaped((rows, width * parts), BF16),
        in_specs=[whole()] * (parts * len(sets) + 1) + unread(after),
        out_specs=whole(),
        compiler_params=params(),
        cost_estimate=cost(1e6, 1e6),
        name="norm",
    )(*sum(sets, []), gain, *after)


def hidden_kernel(part, x_ref, gate_ref, up_ref, *refs):
    if part is None:
        hidden_ref = refs[-1]
    else:
        hidden_ref, weight_ref, sem = refs[-3:]
        count = weight_ref.shape[0]
        copy = pltpu.make_async_copy(refs[0].at[0, 2, pl.ds(part * count, count)], weight_ref, sem)
        copy.start()
    width = gate_ref.shape[1]
    size = 256 if width % 256 == 0 else width
    for i in range(width // size):
        cut = slice(i * size, (i + 1) * size)
        gate = jnp.dot(x_ref[...], gate_ref[:, cut], preferred_element_type=F32)
        up = jnp.dot(x_ref[...], up_ref[:, cut], preferred_element_type=F32)
        hidden_ref[:, cut] = (gate * sigmoid(gate) * up).astype(BF16)
    if part is not None:
        copy.wait()


def hidden_units(x, gate, up, after, experts=None, part=None):
    rows, width = x.shape[0], gate.shape[1]
    made = [shaped((rows, width), BF16)]
    extra = []
    if part is not None:
        made.append(shaped((gate.shape[0] // 2, width), BF16))
        extra = [experts]
    return pl.pallas_call(
        functools.partial(hidden_kernel, part),
        out_shape=made,
        in_specs=[whole()] * 3 + [hbm()] * len(extra) + unread(after),
        out_specs=[whole()] * len(made),
        scratch_shapes=[pltpu.SemaphoreType.DMA] * len(extra),
        compiler_params=params(),
        cost_estimate=cost(1e6, 0),
        name="hidden",
    )(x, gate, up, *extra, *after)


def down_kernel(hidden_own_ref, hidden_other_ref, low_ref, high_ref, *refs):
    own_ref, other_ref, hidden_ref = refs[-3:]
    rows = hidden_own_ref.shape[0]
    hidden_ref[:rows, :] = hidden_own_ref[...]
    hidden_ref[rows:, :] = hidden_other_ref[...]
    size = 256
    half = low_ref.shape[0]
    for i in range(2 * half // size):
        cut = slice(i * size, (i + 1) * size)
        down_ref, begin = (low_ref, i * size) if i * size < half else (high_ref, i * size - half)
        product = lax.dot_general(
            hidden_ref[...],
            down_ref[begin : begin + size, :],
            (((1,), (1,)), ((), ())),
            preferred_element_type=F32,
        )
        own_ref[:, cut] = product[:rows]
        other_ref[:, cut] = product[rows:].astype(BF16)


def down_sums(hidden_own, hidden_other, down, after):
    rows, width = hidden_own.shape
    model = 2 * down[0].shape[0]
    return pl.pallas_call(
        down_kernel,
        out_shape=(shaped((rows, model), F32), shaped((rows, model), BF16)),
        in_specs=[whole()] * 4 + unread(after),
        out_specs=[whole()] * 2,
        scratch_shapes=[pltpu.VMEM((2 * rows, width), BF16)],
        compiler_params=params(),
        cost_estimate=cost(1e6, 0),
        name="down",
    )(hidden_own, hidden_other, *down, *after)


def join_kernel(parts, own_ref, other_ref, *refs):
    out_refs = refs[-parts:]
    width = out_refs[0].shape[1]
    own = lax.axis_index("tp")
    for k, ref in enumerate(out_refs):
        cut = pl.ds(pl.multiple_of(jnp.bitwise_xor(own, k) * width, 128), width)
        ref[...] = (own_ref[:, cut] + other_ref[:, cut].astype(F32)).astype(ref.dtype)


def join(parts, own, other, after):
    rows, model = own.shape
    return pl.pallas_call(
        functools.partial(join_kernel, parts),
        out_shape=[shaped((rows, model // parts), BF16 if k else F32) for k in range(parts)],
        in_specs=[whole()] * 2 + unread(after),
        out_specs=[whole()] * parts,
        compiler_params=params(),
        cost_estimate=cost(1e6, 1e6),
        name="join",
    )(own, other, *after)


def total_kernel(parts, *refs):
    total = refs[0][...].astype(F32)
    for ref in refs[1:parts]:
        total = total + ref[...].astype(F32)
    total = total.astype(BF16)
    for j, ref in enumerate(refs[parts:]):
        ref[...] = total[j * CAP : (j + 1) * CAP, :]


def totals(pieces):
    rows, width = pieces[0].shape
    count = rows // CAP
    return pl.pallas_call(
        functools.partial(total_kernel, len(pieces)),
        out_shape=[shaped((CAP, width), BF16)] * count,
        in_specs=[whole()] * len(pieces),
        out_specs=[whole()] * count,
        compiler_params=params(),
        cost_estimate=cost(1e6, 1e6),
        name="totals",
    )(*pieces)


def blend_kernel(begin, count, *refs):
    back = refs[:count]
    base_ref, first_ref, second_ref, gates_ref, out_ref, rows_ref = refs[count:]
    for j, ref in enumerate(back):
        rows_ref[j * CAP : (j + 1) * CAP, :] = ref[...]
    rows = rows_ref[...]
    gates = jnp.transpose(gates_ref[...])
    cut = slice(begin, begin + count * CAP)
    moe = gates[:, 0:1] * jnp.dot(first_ref[:, cut], rows, preferred_element_type=F32)
    moe = moe + gates[:, 1:2] * jnp.dot(second_ref[:, cut], rows, preferred_element_type=F32)
    out_ref[...] = (base_ref[...].astype(F32) + moe).astype(out_ref.dtype)


def blend(begin, back, base, first, second, gates, dtype):
    count, width = len(back), base.shape[1]
    return pl.pallas_call(
        functools.partial(blend_kernel, begin, count),
        out_shape=shaped(base.shape, dtype),
        in_specs=[whole()] * (count + 4),
        out_specs=whole(),
        scratch_shapes=[pltpu.VMEM((count * CAP, width), BF16)],
        compiler_params=params(),
        cost_estimate=cost(1e6, 1e6),
        name="blend",
    )(*back, base, first, second, gates)


def body(
    conv_in,
    gate_in,
    residual,
    conv_weight,
    conv_bias,
    proj_weight,
    step_weight,
    step_bias,
    decay_log,
    skip_gain,
    out_weight,
    norm_gain,
    expert_ids,
    route_gates,
    expert_weight,
):
    tp, experts = lax.axis_size("tp"), lax.axis_size("exp")
    local = conv_in[0]
    before = lax.ppermute(local, "ctx", [(0, 1)])
    expert_weight = stay(expert_weight)
    near = load(stay(local), stay(conv_weight), stay(conv_bias[None]), stay(proj_weight.T))
    xconv, part = conv(before, *near)
    parts = [part] + [swap(part, "tp", k) for k in range(tp - 1, 0, -1)]
    silu, rates, skipped, bias, step_w, out_w, quarter, gain = prepare(
        tp, xconv, stay(gate_in[0]), stay(decay_log), stay(residual[0]), stay(skip_gain[None]),
        stay(step_bias[None]), stay(step_weight), stay(out_weight), stay(norm_gain[None]),
    )
    y, elapsed, seen, state, up_w = scan(parts, xconv, rates, bias, step_w, expert_weight)
    before = lax.ppermute(state, "ctx", [(0, 1)])
    own, *sent = mix(tp, seen, y, elapsed, rates, before, skipped, silu, quarter, out_w)
    arrived = swaps(sent)
    first, second, chooser, gate_w = route(expert_ids[0].T, experts, expert_weight)
    stream, *picked = pick(own, arrived, chooser)
    half = experts // 2
    rows = [picked[0]] + [swap(picked[j], "exp", j) for j in range(1, experts)]
    piece_b = stack(rows[:half], [])
    both = order([rows[experts - 1], piece_b])
    first_a = rows[half]
    second_a = rows[experts - 1] if half == 2 else stack(rows[half + 1 :], [])
    sets = [[piece] + swaps([piece] * (tp - 1)) for piece in (first_a, second_a, piece_b)]
    x_a = norm(sets[:2], gain, [both])
    own_a, low = hidden_units(x_a, gate_w, up_w, [], expert_weight, 0)
    other_a, high = hidden_units(swap(x_a, "ctx", 1), gate_w, up_w, [own_a, order([x_a])], expert_weight, 1)
    down_w = (low, high)
    sum_a, sent_a = down_sums(own_a, other_a, down_w, [])
    sent_a = swap(sent_a, "ctx", 1)
    x_b = norm(sets[2:], gain, [sum_a])
    own_b, = hidden_units(x_b, gate_w, up_w, [])
    joined_a = join(tp, sum_a, sent_a, [own_b])
    made_a = totals([joined_a[0]] + swaps(joined_a[1:]))
    other_b, = hidden_units(swap(x_b, "ctx", 1), gate_w, up_w, [joined_a[0]])
    sum_b, sent_b = down_sums(own_b, other_b, down_w, [])
    joined_b = join(tp, sum_b, swap(sent_b, "ctx", 1), [order([sent_b, made_a[0]])])
    made_b = totals([joined_b[0]] + swaps(joined_b[1:]))
    back_a = [swap(piece, "exp", j) for j, piece in enumerate(made_a, half)]
    back_b = [made_b[0]] + [swap(made_b[j], "exp", j) for j in range(1, half)]
    gates = route_gates[0].T
    partial = blend(half * CAP, back_a, stream, first, second, gates, F32)
    return blend(0, back_b, partial, first, second, gates, BF16)[None]


def solution(mesh):
    placed = (
        P("exp", "ctx", "tp"),
        P("exp", "ctx", "tp"),
        P("exp", "ctx", None),
        P(None, "tp"),
        P("tp"),
        P("tp", None),
        P(None, "tp"),
        P("tp"),
        P(None, "tp"),
        P("tp"),
        P("tp", None),
        P(),
        P("exp", "ctx", None),
        P("exp", "ctx", None),
        P("exp", None, None, ("ctx", "tp")),
    )
    return jax.shard_map(
        body, mesh=mesh, in_specs=placed, out_specs=P("exp", "ctx", "tp"), check_vma=False
    )
```

```python
import functools
import math

import jax
import jax.numpy as jnp
from jax import lax
from jax.experimental import pallas as pl
from jax.experimental.pallas import tpu as pltpu
from jax.sharding import PartitionSpec as P

STATE = 16
DT_RANK = 256
CAP = 64
LOG2E = math.log2(math.e)
VMEM_LIMIT = 20 * 1024 * 1024
F32 = jnp.float32
BF16 = jnp.bfloat16


def params():
    return pltpu.CompilerParams(vmem_limit_bytes=VMEM_LIMIT)


def whole():
    return pl.BlockSpec(memory_space=pltpu.VMEM)


def shaped(shape, dtype):
    return jax.ShapeDtypeStruct(shape, dtype)


def swap(block, axis, k):
    return lax.ppermute(block, axis, [(i, i ^ k) for i in range(lax.axis_size(axis))])


def swaps(blocks):
    return [swap(block, "tp", k) for k, block in enumerate(blocks, 1)]


def sigmoid(x):
    return 1.0 / (1.0 + jnp.exp2(x * -LOG2E))


def stay(array):
    return pltpu.with_memory_space_constraint(array, pltpu.HBM)


def hbm():
    return pl.BlockSpec(memory_space=pltpu.HBM)


def unread(arrays):
    return [pl.BlockSpec(memory_space=pl.ANY)] * len(arrays)


def stack_kernel(count, *refs):
    for j, ref in enumerate(refs[:count]):
        rows = ref.shape[0]
        refs[-1][j * rows : (j + 1) * rows, :] = ref[...]


def stack(pieces, after):
    rows, width = pieces[0].shape
    return pl.pallas_call(
        functools.partial(stack_kernel, len(pieces)),
        out_shape=shaped((rows * len(pieces), width), pieces[0].dtype),
        in_specs=[whole()] * len(pieces) + unread(after),
        out_specs=whole(),
        compiler_params=params(),
        cost_estimate=cost(1e6, 0),
        name="stack",
    )(*pieces, *after)


def order_kernel(*refs):
    refs[-1][...] = jnp.zeros_like(refs[-1])


def order(after):
    return pl.pallas_call(
        order_kernel,
        out_shape=shaped((8, 128), F32),
        in_specs=unread(after),
        out_specs=whole(),
        compiler_params=params(),
        cost_estimate=cost(2e10, 0),
        name="order",
    )(*after)


def cost(flops, loaded=0):
    return pl.CostEstimate(flops=int(flops), bytes_accessed=int(loaded), transcendentals=0)


def route_kernel(ids_ref, expert_hbm, first_ref, second_ref, chooser_ref, weight_ref, sem):
    copy = pltpu.make_async_copy(expert_hbm.at[0, 0], weight_ref, sem)
    copy.start()
    rows, slots = first_ref.shape
    own = lax.axis_index("exp")
    ids = jnp.transpose(ids_ref[...].astype(F32)).astype(jnp.int32)
    lanes = lax.broadcasted_iota(jnp.int32, (rows, 128), 1)
    hot = [(ids[:, i : i + 1] == lanes).astype(F32) for i in range(2)]
    earlier = lax.broadcasted_iota(jnp.int32, (rows, rows), 1) < lax.broadcasted_iota(
        jnp.int32, (rows, rows), 0
    )
    ranks = jnp.dot(
        earlier.astype(F32).astype(BF16), (hot[0] + hot[1]).astype(BF16), preferred_element_type=F32
    )
    places = lax.broadcasted_iota(jnp.int32, (rows, slots), 1)
    tables = []
    for i in range(2):
        slot = jnp.sum(ranks * hot[i], axis=1, keepdims=True).astype(jnp.int32)
        place = jnp.bitwise_xor(ids[:, i : i + 1], own) * CAP + slot
        tables.append((place == places).astype(F32))
    first_ref[...] = tables[0].astype(BF16)
    second_ref[...] = tables[1].astype(BF16)
    chooser_ref[...] = jnp.transpose(tables[0] + tables[1]).astype(BF16)
    copy.wait()


def route(ids, expert_count, experts):
    rows, slots = ids.shape[1], expert_count * CAP
    return pl.pallas_call(
        route_kernel,
        out_shape=(
            shaped((rows, slots), BF16),
            shaped((rows, slots), BF16),
            shaped((slots, rows), BF16),
            shaped(experts.shape[2:], BF16),
        ),
        in_specs=[whole(), hbm()],
        out_specs=[whole()] * 4,
        scratch_shapes=[pltpu.SemaphoreType.DMA],
        compiler_params=params(),
        cost_estimate=cost(1e6, 8e6),
        name="route",
    )(ids, experts)


def conv_kernel(before_ref, x_ref, taps_ref, bias_ref, weight_ref, xconv_ref, part_ref, ext_ref):
    rows = x_ref.shape[0]
    halo = 16
    count = taps_ref.shape[0]
    ext_ref[:halo, :] = before_ref[rows - halo :, :].astype(F32)
    ext_ref[halo:, :] = x_ref[...].astype(F32)
    total = bias_ref[...] + taps_ref[count - 1 : count, :] * ext_ref[halo:, :]
    for k in range(count - 1):
        start = halo - (count - 1) + k
        total = total + taps_ref[k : k + 1, :] * ext_ref[start : start + rows, :]
    xconv = (total * sigmoid(total)).astype(BF16)
    xconv_ref[...] = xconv
    across = (((1,), (1,)), ((), ()))
    part_ref[:rows, :] = lax.dot_general(
        xconv, weight_ref[:DT_RANK, :], across, preferred_element_type=F32
    ).astype(BF16)
    maps = lax.dot_general(
        weight_ref[DT_RANK:, :], xconv, across, preferred_element_type=F32
    ).astype(BF16)
    part_ref[rows:, :rows] = maps[:STATE]
    part_ref[rows:, rows:] = maps[STATE:]


def conv(before, x, taps, bias, weight):
    rows, channels = x.shape
    return pl.pallas_call(
        conv_kernel,
        out_shape=(shaped((rows, channels), BF16), shaped((rows + STATE, DT_RANK), BF16)),
        in_specs=[whole()] * 5,
        out_specs=[whole()] * 2,
        scratch_shapes=[pltpu.VMEM((16 + rows, channels), F32)],
        compiler_params=params(),
        cost_estimate=cost(1e6, 1e6),
        name="conv",
    )(before, x, taps, bias, weight)


def load_kernel(count, *refs):
    copies = [
        pltpu.make_async_copy(refs[i], refs[count + i], refs[-1].at[i]) for i in range(count)
    ]
    for copy in copies:
        copy.start()
    for copy in copies:
        copy.wait()


def load(*arrays):
    count = len(arrays)
    return pl.pallas_call(
        functools.partial(load_kernel, count),
        out_shape=[shaped(array.shape, array.dtype) for array in arrays],
        in_specs=[hbm()] * count,
        out_specs=[whole()] * count,
        scratch_shapes=[pltpu.SemaphoreType.DMA((count,))],
        compiler_params=params(),
        cost_estimate=cost(1e6, 2e6),
        name="load",
    )(*arrays)


def prepare_kernel(
    xconv_ref, gate_hbm, decay_hbm, residual_hbm, skip_hbm, bias_hbm, step_hbm, out_hbm, gain_hbm,
    silu_ref, rates_ref, skipped_ref, bias_ref, step_ref, out_ref, quarter_ref, gain_ref,
    gate_ref, decay_ref, residual_ref, skip_ref, sems,
):
    copies = [
        pltpu.make_async_copy(source, target, sems.at[i])
        for i, (source, target) in enumerate(
            (
                (gate_hbm, gate_ref),
                (decay_hbm, decay_ref),
                (residual_hbm, residual_ref),
                (skip_hbm, skip_ref),
                (bias_hbm, bias_ref),
                (gain_hbm, gain_ref),
                (step_hbm, step_ref),
                (out_hbm, out_ref),
            )
        )
    ]
    for copy in copies:
        copy.start()
    for copy in copies[:4]:
        copy.wait()
    gate = gate_ref[...].astype(F32)
    silu_ref[...] = gate * sigmoid(gate)
    skipped_ref[...] = skip_ref[...] * xconv_ref[...].astype(F32)
    rates = -LOG2E * jnp.exp(decay_ref[...])
    for j in range(rates_ref.shape[1]):
        rates_ref[:, j, :] = rates[:, j * 128 : (j + 1) * 128]
    width = quarter_ref.shape[1]
    start = pl.multiple_of(lax.axis_index("tp") * width, 128)
    quarter_ref[...] = residual_ref[:, pl.ds(start, width)].astype(F32)
    for copy in copies[4:]:
        copy.wait()


def prepare(parts, xconv, gate, decay_log, residual, skip, bias, step_weight, out_weight, gain):
    rows, channels = gate.shape
    return pl.pallas_call(
        prepare_kernel,
        out_shape=(
            shaped((rows, channels), F32),
            shaped((STATE, channels // 128, 128), F32),
            shaped((rows, channels), F32),
            shaped(bias.shape, F32),
            shaped(step_weight.shape, BF16),
            shaped(out_weight.shape, BF16),
            shaped((rows, residual.shape[1] // parts), F32),
            shaped(gain.shape, F32),
        ),
        in_specs=[whole()] + [hbm()] * 8,
        out_specs=[whole()] * 8,
        scratch_shapes=[
            pltpu.VMEM((rows, channels), BF16),
            pltpu.VMEM(decay_log.shape, F32),
            pltpu.VMEM(residual.shape, BF16),
            pltpu.VMEM(skip.shape, F32),
            pltpu.SemaphoreType.DMA((8,)),
        ],
        compiler_params=params(),
        cost_estimate=cost(1e6, 6e6),
        name="prepare",
    )(xconv, gate, decay_log, residual, skip, bias, step_weight, out_weight, gain)


def scan_kernel(parts, *refs):
    part_refs = refs[:parts]
    xconv_ref, rates_ref, bias_ref, weight_ref, expert_hbm = refs[parts : parts + 5]
    y_ref, elapsed_ref, seen_ref, state_ref, second_ref = refs[parts + 5 : parts + 10]
    steps_ref, driven_ref, spread_ref, expert_sem = refs[parts + 10 :]
    rows = xconv_ref.shape[0]
    tiles = rates_ref.shape[1]
    expert_copy = pltpu.make_async_copy(expert_hbm.at[0, 1], second_ref, expert_sem)
    expert_copy.start()
    proj = part_refs[0][...].astype(F32)
    for ref in part_refs[1:]:
        proj = proj + ref[...].astype(F32)
    maps = proj[rows:]

    for t in range(rows):
        spread_ref[t] = jnp.broadcast_to(maps[:, t : t + 1], (STATE, 128))
        seen_ref[t] = jnp.broadcast_to(maps[:, rows + t : rows + t + 1], (STATE, 128))
    rank = proj[:rows].astype(BF16)
    raw = jnp.dot(rank, weight_ref[...], preferred_element_type=F32) + bias_ref[...]
    steps = jnp.maximum(raw, 0.0) + jnp.log1p(jnp.exp(-jnp.abs(raw)))
    driven = steps * xconv_ref[...].astype(F32)
    for j in range(tiles):
        cut = slice(j * 128, (j + 1) * 128)
        steps_ref[:, j, :] = steps[:, cut]
        driven_ref[:, j, :] = driven[:, cut]

    def step(t, carry):
        elapsed, states = carry
        now, driven = steps_ref[t], driven_ref[t]
        sums = [None, None]
        new = []
        for n in range(STATE):
            state = jnp.exp2(now * rates_ref[n]) * states[n] + driven * spread_ref[t, n : n + 1, :]
            new.append(state)
            term = state * seen_ref[t, n : n + 1, :]
            sums[n % 2] = term if sums[n % 2] is None else sums[n % 2] + term
        elapsed = elapsed + now
        y_ref[t] = sums[0] + sums[1]
        elapsed_ref[t] = elapsed
        return elapsed, tuple(new)

    zero = jnp.zeros((tiles, 128), F32)
    _, states = lax.fori_loop(0, rows, step, (zero, (zero,) * STATE), unroll=16)
    for n in range(STATE):
        state_ref[n] = states[n]
    expert_copy.wait()


def scan(pieces, xconv, rates, bias, weight, experts):
    rows = xconv.shape[0]
    tall = (rows, *rates.shape[1:])
    return pl.pallas_call(
        functools.partial(scan_kernel, len(pieces)),
        out_shape=(
            shaped(tall, F32),
            shaped(tall, F32),
            shaped((rows, STATE, 128), F32),
            shaped(rates.shape, F32),
            shaped(experts.shape[2:], BF16),
        ),
        in_specs=[whole()] * (len(pieces) + 4) + [hbm()],
        out_specs=[whole()] * 5,
        scratch_shapes=[
            pltpu.VMEM(tall, F32),
            pltpu.VMEM(tall, F32),
            pltpu.VMEM((rows, STATE, 128), F32),
            pltpu.SemaphoreType.DMA,
        ],
        compiler_params=params(),
        cost_estimate=cost(1e6, 14e6),
        name="scan",
    )(*pieces, xconv, rates, bias, weight, experts)


def project(total_ref, skipped_ref, silu_ref, quarter_ref, weight_ref, own_ref, sent, gated_ref):
    for j in range(total_ref.shape[1]):
        cut = slice(j * 128, (j + 1) * 128)
        total = total_ref[:, j, :] + skipped_ref[:, cut]
        gated_ref[:, cut] = (total * silu_ref[:, cut]).astype(BF16)
    own = lax.axis_index("tp")
    width = own_ref.shape[1]
    for k in range(len(sent) + 1):
        start = pl.multiple_of(jnp.bitwise_xor(own, k) * width, 128)
        product = jnp.dot(
            gated_ref[...], weight_ref[:, pl.ds(start, width)], preferred_element_type=F32
        )
        if k == 0:
            own_ref[...] = product + quarter_ref[...]
        else:
            sent[k - 1][...] = product.astype(BF16)


def mix_first_kernel(parts, y_ref, skipped_ref, silu_ref, quarter_ref, weight_ref, *refs):
    @pl.when(lax.axis_index("ctx") == 0)
    def _():
        project(y_ref, skipped_ref, silu_ref, quarter_ref, weight_ref, refs[0], refs[1:parts], refs[parts])


def mix_kernel(parts, *refs):
    seen_ref, y_ref, elapsed_ref, rates_ref, state_ref, skipped_ref, silu_ref, quarter_ref, weight_ref = refs[:9]
    own_ref, sent = refs[9 + parts], refs[10 + parts : 9 + 2 * parts]
    sum_ref, gated_ref = refs[9 + 2 * parts :]
    rows = y_ref.shape[0]

    def step(t, carry):
        elapsed = elapsed_ref[t]
        sums = [y_ref[t], None]
        for n in range(STATE):
            term = jnp.exp2(elapsed * rates_ref[n]) * (state_ref[n] * seen_ref[t, n : n + 1, :])
            sums[n % 2] = term if sums[n % 2] is None else sums[n % 2] + term
        sum_ref[t] = sums[0] + sums[1]
        return carry

    @pl.when(lax.axis_index("ctx") > 0)
    def _():
        lax.fori_loop(0, rows, step, 0, unroll=8)
        project(sum_ref, skipped_ref, silu_ref, quarter_ref, weight_ref, own_ref, sent, gated_ref)


def mix(parts, seen, y, elapsed, rates, state, skipped, silu, quarter, weight):
    rows, tiles, _ = y.shape
    width = weight.shape[1] // parts
    made = [shaped((rows, width), F32)] + [shaped((rows, width), BF16)] * (parts - 1)
    started = pl.pallas_call(
        functools.partial(mix_first_kernel, parts),
        out_shape=made,
        in_specs=[whole()] * 5,
        out_specs=[whole()] * parts,
        scratch_shapes=[pltpu.VMEM((rows, tiles * 128), BF16)],
        compiler_params=params(),
        cost_estimate=cost(3e9, 0),
        name="mix_first",
    )(y, skipped, silu, quarter, weight)
    return pl.pallas_call(
        functools.partial(mix_kernel, parts),
        out_shape=made,
        in_specs=[whole()] * (9 + parts),
        out_specs=[whole()] * parts,
        input_output_aliases={9 + i: i for i in range(parts)},
        scratch_shapes=[
            pltpu.VMEM((rows, tiles, 128), F32),
            pltpu.VMEM((rows, tiles * 128), BF16),
        ],
        compiler_params=params(),
        cost_estimate=cost(1e6, 12e6),
        name="mix",
    )(seen, y, elapsed, rates, state, skipped, silu, quarter, weight, *started)


def pick_kernel(parts, *refs):
    own_ref, arrived, chooser_ref = refs[0], refs[1:parts], refs[parts]
    stream_ref, out_refs = refs[parts + 1], refs[parts + 2 :]
    total = own_ref[...]
    for ref in arrived:
        total = total + ref[...].astype(F32)
    stream = total.astype(BF16)
    stream_ref[...] = stream
    picked = jnp.dot(chooser_ref[...], stream, preferred_element_type=F32).astype(BF16)
    for j, ref in enumerate(out_refs):
        ref[...] = picked[j * CAP : (j + 1) * CAP, :]


def pick(own, arrived, chooser):
    rows, width = own.shape
    experts = chooser.shape[0] // CAP
    return pl.pallas_call(
        functools.partial(pick_kernel, 1 + len(arrived)),
        out_shape=[shaped((rows, width), BF16)] + [shaped((CAP, width), BF16)] * experts,
        in_specs=[whole()] * (2 + len(arrived)),
        out_specs=[whole()] * (1 + experts),
        compiler_params=params(),
        cost_estimate=cost(1e6, 1e6),
        name="pick",
    )(own, *arrived, chooser)


def norm_kernel(parts, count, *refs):
    gain_ref, out_ref = refs[parts * count], refs[-1]
    own = lax.axis_index("tp")
    begin = 0
    for i in range(count):
        pieces = [ref[...].astype(F32) for ref in refs[i * parts : (i + 1) * parts]]
        rows, width = pieces[0].shape
        total = sum(jnp.sum(piece * piece, axis=1, keepdims=True) for piece in pieces)
        scale = lax.rsqrt(total / (width * parts) + 1e-6)
        for k, piece in enumerate(pieces):
            start = pl.multiple_of(jnp.bitwise_xor(own, k) * width, 128)
            out_ref[begin : begin + rows, pl.ds(start, width)] = (
                piece * scale * gain_ref[:, pl.ds(start, width)]
            ).astype(BF16)
        begin += rows


def norm(sets, gain, after):
    parts = len(sets[0])
    rows, width = sum(pieces[0].shape[0] for pieces in sets), sets[0][0].shape[1]
    return pl.pallas_call(
        functools.partial(norm_kernel, parts, len(sets)),
        out_shape=shaped((rows, width * parts), BF16),
        in_specs=[whole()] * (parts * len(sets) + 1) + unread(after),
        out_specs=whole(),
        compiler_params=params(),
        cost_estimate=cost(1e6, 1e6),
        name="norm",
    )(*sum(sets, []), gain, *after)


def hidden_kernel(part, x_ref, gate_ref, up_ref, *refs):
    if part is None:
        hidden_ref = refs[-1]
    else:
        hidden_ref, weight_ref, sem = refs[-3:]
        count = weight_ref.shape[0]
        copy = pltpu.make_async_copy(refs[0].at[0, 2, pl.ds(part * count, count)], weight_ref, sem)
        copy.start()
    width = gate_ref.shape[1]
    size = 256 if width % 256 == 0 else width
    for i in range(width // size):
        cut = slice(i * size, (i + 1) * size)
        gate = jnp.dot(x_ref[...], gate_ref[:, cut], preferred_element_type=F32)
        up = jnp.dot(x_ref[...], up_ref[:, cut], preferred_element_type=F32)
        hidden_ref[:, cut] = (gate * sigmoid(gate) * up).astype(BF16)
    if part is not None:
        copy.wait()


def hidden_units(x, gate, up, after, experts=None, part=None):
    rows, width = x.shape[0], gate.shape[1]
    made = [shaped((rows, width), BF16)]
    extra = []
    if part is not None:
        made.append(shaped((gate.shape[0] // 2, width), BF16))
        extra = [experts]
    return pl.pallas_call(
        functools.partial(hidden_kernel, part),
        out_shape=made,
        in_specs=[whole()] * 3 + [hbm()] * len(extra) + unread(after),
        out_specs=[whole()] * len(made),
        scratch_shapes=[pltpu.SemaphoreType.DMA] * len(extra),
        compiler_params=params(),
        cost_estimate=cost(1e6, 0),
        name="hidden",
    )(x, gate, up, *extra, *after)


def down_kernel(hidden_own_ref, hidden_other_ref, low_ref, high_ref, *refs):
    own_ref, other_ref, hidden_ref = refs[-3:]
    rows = hidden_own_ref.shape[0]
    hidden_ref[:rows, :] = hidden_own_ref[...]
    hidden_ref[rows:, :] = hidden_other_ref[...]
    size = 256
    half = low_ref.shape[0]
    for i in range(2 * half // size):
        cut = slice(i * size, (i + 1) * size)
        down_ref, begin = (low_ref, i * size) if i * size < half else (high_ref, i * size - half)
        product = lax.dot_general(
            hidden_ref[...],
            down_ref[begin : begin + size, :],
            (((1,), (1,)), ((), ())),
            preferred_element_type=F32,
        )
        own_ref[:, cut] = product[:rows]
        other_ref[:, cut] = product[rows:].astype(BF16)


def down_sums(hidden_own, hidden_other, down, after):
    rows, width = hidden_own.shape
    model = 2 * down[0].shape[0]
    return pl.pallas_call(
        down_kernel,
        out_shape=(shaped((rows, model), F32), shaped((rows, model), BF16)),
        in_specs=[whole()] * 4 + unread(after),
        out_specs=[whole()] * 2,
        scratch_shapes=[pltpu.VMEM((2 * rows, width), BF16)],
        compiler_params=params(),
        cost_estimate=cost(1e6, 0),
        name="down",
    )(hidden_own, hidden_other, *down, *after)


def join_kernel(parts, own_ref, other_ref, *refs):
    out_refs = refs[-parts:]
    width = out_refs[0].shape[1]
    own = lax.axis_index("tp")
    for k, ref in enumerate(out_refs):
        cut = pl.ds(pl.multiple_of(jnp.bitwise_xor(own, k) * width, 128), width)
        ref[...] = (own_ref[:, cut] + other_ref[:, cut].astype(F32)).astype(ref.dtype)


def join(parts, own, other, after):
    rows, model = own.shape
    return pl.pallas_call(
        functools.partial(join_kernel, parts),
        out_shape=[shaped((rows, model // parts), BF16 if k else F32) for k in range(parts)],
        in_specs=[whole()] * 2 + unread(after),
        out_specs=[whole()] * parts,
        compiler_params=params(),
        cost_estimate=cost(1e6, 1e6),
        name="join",
    )(own, other, *after)


def total_kernel(parts, *refs):
    total = refs[0][...].astype(F32)
    for ref in refs[1:parts]:
        total = total + ref[...].astype(F32)
    total = total.astype(BF16)
    for j, ref in enumerate(refs[parts:]):
        ref[...] = total[j * CAP : (j + 1) * CAP, :]


def totals(pieces):
    rows, width = pieces[0].shape
    count = rows // CAP
    return pl.pallas_call(
        functools.partial(total_kernel, len(pieces)),
        out_shape=[shaped((CAP, width), BF16)] * count,
        in_specs=[whole()] * len(pieces),
        out_specs=[whole()] * count,
        compiler_params=params(),
        cost_estimate=cost(1e6, 1e6),
        name="totals",
    )(*pieces)


def blend_kernel(begin, count, *refs):
    back = refs[:count]
    base_ref, first_ref, second_ref, gates_ref, out_ref, rows_ref = refs[count:]
    for j, ref in enumerate(back):
        rows_ref[j * CAP : (j + 1) * CAP, :] = ref[...]
    rows = rows_ref[...]
    gates = jnp.transpose(gates_ref[...])
    cut = slice(begin, begin + count * CAP)
    moe = gates[:, 0:1] * jnp.dot(first_ref[:, cut], rows, preferred_element_type=F32)
    moe = moe + gates[:, 1:2] * jnp.dot(second_ref[:, cut], rows, preferred_element_type=F32)
    out_ref[...] = (base_ref[...].astype(F32) + moe).astype(out_ref.dtype)


def blend(begin, back, base, first, second, gates, dtype):
    count, width = len(back), base.shape[1]
    return pl.pallas_call(
        functools.partial(blend_kernel, begin, count),
        out_shape=shaped(base.shape, dtype),
        in_specs=[whole()] * (count + 4),
        out_specs=whole(),
        scratch_shapes=[pltpu.VMEM((count * CAP, width), BF16)],
        compiler_params=params(),
        cost_estimate=cost(1e6, 1e6),
        name="blend",
    )(*back, base, first, second, gates)


def body(
    conv_in,
    gate_in,
    residual,
    conv_weight,
    conv_bias,
    proj_weight,
    step_weight,
    step_bias,
    decay_log,
    skip_gain,
    out_weight,
    norm_gain,
    expert_ids,
    route_gates,
    expert_weight,
):
    tp, experts = lax.axis_size("tp"), lax.axis_size("exp")
    local = conv_in[0]
    before = lax.ppermute(local, "ctx", [(0, 1)])
    expert_weight = stay(expert_weight)
    near = load(stay(local), stay(conv_weight), stay(conv_bias[None]), stay(proj_weight.T))
    xconv, part = conv(before, *near)
    parts = [part] + [swap(part, "tp", k) for k in range(tp - 1, 0, -1)]
    silu, rates, skipped, bias, step_w, out_w, quarter, gain = prepare(
        tp, xconv, stay(gate_in[0]), stay(decay_log), stay(residual[0]), stay(skip_gain[None]),
        stay(step_bias[None]), stay(step_weight), stay(out_weight), stay(norm_gain[None]),
    )
    y, elapsed, seen, state, up_w = scan(parts, xconv, rates, bias, step_w, expert_weight)
    before = lax.ppermute(state, "ctx", [(0, 1)])
    own, *sent = mix(tp, seen, y, elapsed, rates, before, skipped, silu, quarter, out_w)
    arrived = swaps(sent)
    first, second, chooser, gate_w = route(expert_ids[0].T, experts, expert_weight)
    stream, *picked = pick(own, arrived, chooser)
    half = experts // 2
    rows = [picked[0]] + [swap(picked[j], "exp", j) for j in range(1, experts)]
    piece_b = stack(rows[:half], [])
    both = order([rows[experts - 1], piece_b])
    first_a = rows[half]
    second_a = rows[experts - 1] if half == 2 else stack(rows[half + 1 :], [])
    sets = [[piece] + swaps([piece] * (tp - 1)) for piece in (first_a, second_a, piece_b)]
    x_a = norm(sets[:2], gain, [both])
    own_a, low = hidden_units(x_a, gate_w, up_w, [], expert_weight, 0)
    other_a, high = hidden_units(swap(x_a, "ctx", 1), gate_w, up_w, [own_a, order([x_a])], expert_weight, 1)
    down_w = (low, high)
    sum_a, sent_a = down_sums(own_a, other_a, down_w, [])
    sent_a = swap(sent_a, "ctx", 1)
    x_b = norm(sets[2:], gain, [sum_a])
    own_b, = hidden_units(x_b, gate_w, up_w, [])
    joined_a = join(tp, sum_a, sent_a, [own_b])
    made_a = totals([joined_a[0]] + swaps(joined_a[1:]))
    other_b, = hidden_units(swap(x_b, "ctx", 1), gate_w, up_w, [joined_a[0]])
    sum_b, sent_b = down_sums(own_b, other_b, down_w, [])
    joined_b = join(tp, sum_b, swap(sent_b, "ctx", 1), [order([sent_b, made_a[0]])])
    made_b = totals([joined_b[0]] + swaps(joined_b[1:]))
    back_a = [swap(piece, "exp", j) for j, piece in enumerate(made_a, half)]
    back_b = [made_b[0]] + [swap(made_b[j], "exp", j) for j in range(1, half)]
    gates = route_gates[0].T
    partial = blend(half * CAP, back_a, stream, first, second, gates, F32)
    return blend(0, back_b, partial, first, second, gates, BF16)[None]


def solution(mesh):
    placed = (
        P("exp", "ctx", "tp"),
        P("exp", "ctx", "tp"),
        P("exp", "ctx", None),
        P(None, "tp"),
        P("tp"),
        P("tp", None),
        P(None, "tp"),
        P("tp"),
        P(None, "tp"),
        P("tp"),
        P("tp", None),
        P(),
        P("exp", "ctx", None),
        P("exp", "ctx", None),
        P("exp", None, None, ("ctx", "tp")),
    )
    return jax.shard_map(
        body, mesh=mesh, in_specs=placed, out_specs=P("exp", "ctx", "tp"), check_vma=False
    )
```

```python
import functools
import math

import jax
import jax.numpy as jnp
from jax import lax
from jax.experimental import pallas as pl
from jax.experimental.pallas import tpu as pltpu
from jax.sharding import PartitionSpec as P

STATE = 16
DT_RANK = 256
CAP = 64
LOG2E = math.log2(math.e)
VMEM_LIMIT = 20 * 1024 * 1024
F32 = jnp.float32
BF16 = jnp.bfloat16


def params():
    return pltpu.CompilerParams(vmem_limit_bytes=VMEM_LIMIT)


def whole():
    return pl.BlockSpec(memory_space=pltpu.VMEM)


def shaped(shape, dtype):
    return jax.ShapeDtypeStruct(shape, dtype)


def swap(block, axis, k):
    return lax.ppermute(block, axis, [(i, i ^ k) for i in range(lax.axis_size(axis))])


def swaps(blocks):
    return [swap(block, "tp", k) for k, block in enumerate(blocks, 1)]


def sigmoid(x):
    return 1.0 / (1.0 + jnp.exp2(x * -LOG2E))


def stay(array):
    return pltpu.with_memory_space_constraint(array, pltpu.HBM)


def hbm():
    return pl.BlockSpec(memory_space=pltpu.HBM)


def unread(arrays):
    return [pl.BlockSpec(memory_space=pl.ANY)] * len(arrays)


def stack_kernel(count, *refs):
    for j, ref in enumerate(refs[:count]):
        rows = ref.shape[0]
        refs[-1][j * rows : (j + 1) * rows, :] = ref[...]


def stack(pieces, after):
    rows, width = pieces[0].shape
    return pl.pallas_call(
        functools.partial(stack_kernel, len(pieces)),
        out_shape=shaped((rows * len(pieces), width), pieces[0].dtype),
        in_specs=[whole()] * len(pieces) + unread(after),
        out_specs=whole(),
        compiler_params=params(),
        cost_estimate=cost(1e6, 0),
        name="stack",
    )(*pieces, *after)


def order_kernel(*refs):
    refs[-1][...] = jnp.zeros_like(refs[-1])


def order(after):
    return pl.pallas_call(
        order_kernel,
        out_shape=shaped((8, 128), F32),
        in_specs=unread(after),
        out_specs=whole(),
        compiler_params=params(),
        cost_estimate=cost(2e10, 0),
        name="order",
    )(*after)


def cost(flops, loaded=0):
    return pl.CostEstimate(flops=int(flops), bytes_accessed=int(loaded), transcendentals=0)


def route_kernel(ids_ref, expert_hbm, first_ref, second_ref, chooser_ref, weight_ref, sem):
    copy = pltpu.make_async_copy(expert_hbm.at[0, 0], weight_ref, sem)
    copy.start()
    rows, slots = first_ref.shape
    own = lax.axis_index("exp")
    ids = jnp.transpose(ids_ref[...].astype(F32)).astype(jnp.int32)
    lanes = lax.broadcasted_iota(jnp.int32, (rows, 128), 1)
    hot = [(ids[:, i : i + 1] == lanes).astype(F32) for i in range(2)]
    earlier = lax.broadcasted_iota(jnp.int32, (rows, rows), 1) < lax.broadcasted_iota(
        jnp.int32, (rows, rows), 0
    )
    ranks = jnp.dot(
        earlier.astype(F32).astype(BF16), (hot[0] + hot[1]).astype(BF16), preferred_element_type=F32
    )
    places = lax.broadcasted_iota(jnp.int32, (rows, slots), 1)
    tables = []
    for i in range(2):
        slot = jnp.sum(ranks * hot[i], axis=1, keepdims=True).astype(jnp.int32)
        place = jnp.bitwise_xor(ids[:, i : i + 1], own) * CAP + slot
        tables.append((place == places).astype(F32))
    first_ref[...] = tables[0].astype(BF16)
    second_ref[...] = tables[1].astype(BF16)
    chooser_ref[...] = jnp.transpose(tables[0] + tables[1]).astype(BF16)
    copy.wait()


def route(ids, expert_count, experts):
    rows, slots = ids.shape[1], expert_count * CAP
    return pl.pallas_call(
        route_kernel,
        out_shape=(
            shaped((rows, slots), BF16),
            shaped((rows, slots), BF16),
            shaped((slots, rows), BF16),
            shaped(experts.shape[2:], BF16),
        ),
        in_specs=[whole(), hbm()],
        out_specs=[whole()] * 4,
        scratch_shapes=[pltpu.SemaphoreType.DMA],
        compiler_params=params(),
        cost_estimate=cost(1e6, 8e6),
        name="route",
    )(ids, experts)


def conv_kernel(before_ref, x_ref, taps_ref, bias_ref, weight_ref, xconv_ref, part_ref, ext_ref):
    rows = x_ref.shape[0]
    halo = 16
    count = taps_ref.shape[0]
    ext_ref[:halo, :] = before_ref[rows - halo :, :].astype(F32)
    ext_ref[halo:, :] = x_ref[...].astype(F32)
    total = bias_ref[...] + taps_ref[count - 1 : count, :] * ext_ref[halo:, :]
    for k in range(count - 1):
        start = halo - (count - 1) + k
        total = total + taps_ref[k : k + 1, :] * ext_ref[start : start + rows, :]
    xconv = (total * sigmoid(total)).astype(BF16)
    xconv_ref[...] = xconv
    across = (((1,), (1,)), ((), ()))
    part_ref[:rows, :] = lax.dot_general(
        xconv, weight_ref[:DT_RANK, :], across, preferred_element_type=F32
    ).astype(BF16)
    maps = lax.dot_general(
        weight_ref[DT_RANK:, :], xconv, across, preferred_element_type=F32
    ).astype(BF16)
    part_ref[rows:, :rows] = maps[:STATE]
    part_ref[rows:, rows:] = maps[STATE:]


def conv(before, x, taps, bias, weight):
    rows, channels = x.shape
    return pl.pallas_call(
        conv_kernel,
        out_shape=(shaped((rows, channels), BF16), shaped((rows + STATE, DT_RANK), BF16)),
        in_specs=[whole()] * 5,
        out_specs=[whole()] * 2,
        scratch_shapes=[pltpu.VMEM((16 + rows, channels), F32)],
        compiler_params=params(),
        cost_estimate=cost(1e6, 1e6),
        name="conv",
    )(before, x, taps, bias, weight)


def load_kernel(count, *refs):
    copies = [
        pltpu.make_async_copy(refs[i], refs[count + i], refs[-1].at[i]) for i in range(count)
    ]
    for copy in copies:
        copy.start()
    for copy in copies:
        copy.wait()


def load(*arrays):
    count = len(arrays)
    return pl.pallas_call(
        functools.partial(load_kernel, count),
        out_shape=[shaped(array.shape, array.dtype) for array in arrays],
        in_specs=[hbm()] * count,
        out_specs=[whole()] * count,
        scratch_shapes=[pltpu.SemaphoreType.DMA((count,))],
        compiler_params=params(),
        cost_estimate=cost(1e6, 2e6),
        name="load",
    )(*arrays)


def prepare_kernel(
    xconv_ref, gate_hbm, decay_hbm, residual_hbm, skip_hbm, bias_hbm, step_hbm, out_hbm, gain_hbm,
    silu_ref, rates_ref, skipped_ref, bias_ref, step_ref, out_ref, quarter_ref, gain_ref,
    gate_ref, decay_ref, residual_ref, skip_ref, sems,
):
    copies = [
        pltpu.make_async_copy(source, target, sems.at[i])
        for i, (source, target) in enumerate(
            (
                (gate_hbm, gate_ref),
                (decay_hbm, decay_ref),
                (residual_hbm, residual_ref),
                (skip_hbm, skip_ref),
                (bias_hbm, bias_ref),
                (gain_hbm, gain_ref),
                (step_hbm, step_ref),
                (out_hbm, out_ref),
            )
        )
    ]
    for copy in copies:
        copy.start()
    for copy in copies[:4]:
        copy.wait()
    gate = gate_ref[...].astype(F32)
    silu_ref[...] = gate * sigmoid(gate)
    skipped_ref[...] = skip_ref[...] * xconv_ref[...].astype(F32)
    rates = -LOG2E * jnp.exp(decay_ref[...])
    for j in range(rates_ref.shape[1]):
        rates_ref[:, j, :] = rates[:, j * 128 : (j + 1) * 128]
    width = quarter_ref.shape[1]
    start = pl.multiple_of(lax.axis_index("tp") * width, 128)
    quarter_ref[...] = residual_ref[:, pl.ds(start, width)].astype(F32)
    for copy in copies[4:]:
        copy.wait()


def prepare(parts, xconv, gate, decay_log, residual, skip, bias, step_weight, out_weight, gain):
    rows, channels = gate.shape
    return pl.pallas_call(
        prepare_kernel,
        out_shape=(
            shaped((rows, channels), F32),
            shaped((STATE, channels // 128, 128), F32),
            shaped((rows, channels), F32),
            shaped(bias.shape, F32),
            shaped(step_weight.shape, BF16),
            shaped(out_weight.shape, BF16),
            shaped((rows, residual.shape[1] // parts), F32),
            shaped(gain.shape, F32),
        ),
        in_specs=[whole()] + [hbm()] * 8,
        out_specs=[whole()] * 8,
        scratch_shapes=[
            pltpu.VMEM((rows, channels), BF16),
            pltpu.VMEM(decay_log.shape, F32),
            pltpu.VMEM(residual.shape, BF16),
            pltpu.VMEM(skip.shape, F32),
            pltpu.SemaphoreType.DMA((8,)),
        ],
        compiler_params=params(),
        cost_estimate=cost(1e6, 6e6),
        name="prepare",
    )(xconv, gate, decay_log, residual, skip, bias, step_weight, out_weight, gain)


def scan_kernel(parts, *refs):
    part_refs = refs[:parts]
    xconv_ref, rates_ref, bias_ref, weight_ref, expert_hbm = refs[parts : parts + 5]
    y_ref, elapsed_ref, seen_ref, state_ref, second_ref = refs[parts + 5 : parts + 10]
    steps_ref, driven_ref, spread_ref, expert_sem = refs[parts + 10 :]
    rows = xconv_ref.shape[0]
    tiles = rates_ref.shape[1]
    expert_copy = pltpu.make_async_copy(expert_hbm.at[0, 1], second_ref, expert_sem)
    expert_copy.start()
    proj = part_refs[0][...].astype(F32)
    for ref in part_refs[1:]:
        proj = proj + ref[...].astype(F32)
    maps = proj[rows:]

    for t in range(rows):
        spread_ref[t] = jnp.broadcast_to(maps[:, t : t + 1], (STATE, 128))
        seen_ref[t] = jnp.broadcast_to(maps[:, rows + t : rows + t + 1], (STATE, 128))
    rank = proj[:rows].astype(BF16)
    raw = jnp.dot(rank, weight_ref[...], preferred_element_type=F32) + bias_ref[...]
    steps = jnp.maximum(raw, 0.0) + jnp.log1p(jnp.exp(-jnp.abs(raw)))
    driven = steps * xconv_ref[...].astype(F32)
    for j in range(tiles):
        cut = slice(j * 128, (j + 1) * 128)
        steps_ref[:, j, :] = steps[:, cut]
        driven_ref[:, j, :] = driven[:, cut]

    def step(t, carry):
        elapsed, states = carry
        now, driven = steps_ref[t], driven_ref[t]
        sums = [None, None]
        new = []
        for n in range(STATE):
            state = jnp.exp2(now * rates_ref[n]) * states[n] + driven * spread_ref[t, n : n + 1, :]
            new.append(state)
            term = state * seen_ref[t, n : n + 1, :]
            sums[n % 2] = term if sums[n % 2] is None else sums[n % 2] + term
        elapsed = elapsed + now
        y_ref[t] = sums[0] + sums[1]
        elapsed_ref[t] = elapsed
        return elapsed, tuple(new)

    zero = jnp.zeros((tiles, 128), F32)
    _, states = lax.fori_loop(0, rows, step, (zero, (zero,) * STATE), unroll=16)
    for n in range(STATE):
        state_ref[n] = states[n]
    expert_copy.wait()


def scan(pieces, xconv, rates, bias, weight, experts):
    rows = xconv.shape[0]
    tall = (rows, *rates.shape[1:])
    return pl.pallas_call(
        functools.partial(scan_kernel, len(pieces)),
        out_shape=(
            shaped(tall, F32),
            shaped(tall, F32),
            shaped((rows, STATE, 128), F32),
            shaped(rates.shape, F32),
            shaped(experts.shape[2:], BF16),
        ),
        in_specs=[whole()] * (len(pieces) + 4) + [hbm()],
        out_specs=[whole()] * 5,
        scratch_shapes=[
            pltpu.VMEM(tall, F32),
            pltpu.VMEM(tall, F32),
            pltpu.VMEM((rows, STATE, 128), F32),
            pltpu.SemaphoreType.DMA,
        ],
        compiler_params=params(),
        cost_estimate=cost(1e6, 14e6),
        name="scan",
    )(*pieces, xconv, rates, bias, weight, experts)


def project(total_ref, skipped_ref, silu_ref, quarter_ref, weight_ref, own_ref, sent, gated_ref):
    for j in range(total_ref.shape[1]):
        cut = slice(j * 128, (j + 1) * 128)
        total = total_ref[:, j, :] + skipped_ref[:, cut]
        gated_ref[:, cut] = (total * silu_ref[:, cut]).astype(BF16)
    own = lax.axis_index("tp")
    width = own_ref.shape[1]
    for k in range(len(sent) + 1):
        start = pl.multiple_of(jnp.bitwise_xor(own, k) * width, 128)
        product = jnp.dot(
            gated_ref[...], weight_ref[:, pl.ds(start, width)], preferred_element_type=F32
        )
        if k == 0:
            own_ref[...] = product + quarter_ref[...]
        else:
            sent[k - 1][...] = product.astype(BF16)


def mix_first_kernel(parts, y_ref, skipped_ref, silu_ref, quarter_ref, weight_ref, *refs):
    @pl.when(lax.axis_index("ctx") == 0)
    def _():
        project(y_ref, skipped_ref, silu_ref, quarter_ref, weight_ref, refs[0], refs[1:parts], refs[parts])


def mix_kernel(parts, *refs):
    seen_ref, y_ref, elapsed_ref, rates_ref, state_ref, skipped_ref, silu_ref, quarter_ref, weight_ref = refs[:9]
    own_ref, sent = refs[9 + parts], refs[10 + parts : 9 + 2 * parts]
    sum_ref, gated_ref = refs[9 + 2 * parts :]
    rows = y_ref.shape[0]

    def step(t, carry):
        elapsed = elapsed_ref[t]
        sums = [y_ref[t], None]
        for n in range(STATE):
            term = jnp.exp2(elapsed * rates_ref[n]) * (state_ref[n] * seen_ref[t, n : n + 1, :])
            sums[n % 2] = term if sums[n % 2] is None else sums[n % 2] + term
        sum_ref[t] = sums[0] + sums[1]
        return carry

    @pl.when(lax.axis_index("ctx") > 0)
    def _():
        lax.fori_loop(0, rows, step, 0, unroll=8)
        project(sum_ref, skipped_ref, silu_ref, quarter_ref, weight_ref, own_ref, sent, gated_ref)


def mix(parts, seen, y, elapsed, rates, state, skipped, silu, quarter, weight):
    rows, tiles, _ = y.shape
    width = weight.shape[1] // parts
    made = [shaped((rows, width), F32)] + [shaped((rows, width), BF16)] * (parts - 1)
    started = pl.pallas_call(
        functools.partial(mix_first_kernel, parts),
        out_shape=made,
        in_specs=[whole()] * 5,
        out_specs=[whole()] * parts,
        scratch_shapes=[pltpu.VMEM((rows, tiles * 128), BF16)],
        compiler_params=params(),
        cost_estimate=cost(3e9, 0),
        name="mix_first",
    )(y, skipped, silu, quarter, weight)
    return pl.pallas_call(
        functools.partial(mix_kernel, parts),
        out_shape=made,
        in_specs=[whole()] * (9 + parts),
        out_specs=[whole()] * parts,
        input_output_aliases={9 + i: i for i in range(parts)},
        scratch_shapes=[
            pltpu.VMEM((rows, tiles, 128), F32),
            pltpu.VMEM((rows, tiles * 128), BF16),
        ],
        compiler_params=params(),
        cost_estimate=cost(1e6, 12e6),
        name="mix",
    )(seen, y, elapsed, rates, state, skipped, silu, quarter, weight, *started)


def pick_kernel(parts, *refs):
    own_ref, arrived, chooser_ref = refs[0], refs[1:parts], refs[parts]
    stream_ref, out_refs = refs[parts + 1], refs[parts + 2 :]
    total = own_ref[...]
    for ref in arrived:
        total = total + ref[...].astype(F32)
    stream = total.astype(BF16)
    stream_ref[...] = stream
    picked = jnp.dot(chooser_ref[...], stream, preferred_element_type=F32).astype(BF16)
    for j, ref in enumerate(out_refs):
        ref[...] = picked[j * CAP : (j + 1) * CAP, :]


def pick(own, arrived, chooser):
    rows, width = own.shape
    experts = chooser.shape[0] // CAP
    return pl.pallas_call(
        functools.partial(pick_kernel, 1 + len(arrived)),
        out_shape=[shaped((rows, width), BF16)] + [shaped((CAP, width), BF16)] * experts,
        in_specs=[whole()] * (2 + len(arrived)),
        out_specs=[whole()] * (1 + experts),
        compiler_params=params(),
        cost_estimate=cost(1e6, 1e6),
        name="pick",
    )(own, *arrived, chooser)


def norm_kernel(parts, count, *refs):
    gain_ref, out_ref = refs[parts * count], refs[-1]
    own = lax.axis_index("tp")
    begin = 0
    for i in range(count):
        pieces = [ref[...].astype(F32) for ref in refs[i * parts : (i + 1) * parts]]
        rows, width = pieces[0].shape
        total = sum(jnp.sum(piece * piece, axis=1, keepdims=True) for piece in pieces)
        scale = lax.rsqrt(total / (width * parts) + 1e-6)
        for k, piece in enumerate(pieces):
            start = pl.multiple_of(jnp.bitwise_xor(own, k) * width, 128)
            out_ref[begin : begin + rows, pl.ds(start, width)] = (
                piece * scale * gain_ref[:, pl.ds(start, width)]
            ).astype(BF16)
        begin += rows


def norm(sets, gain, after):
    parts = len(sets[0])
    rows, width = sum(pieces[0].shape[0] for pieces in sets), sets[0][0].shape[1]
    return pl.pallas_call(
        functools.partial(norm_kernel, parts, len(sets)),
        out_shape=shaped((rows, width * parts), BF16),
        in_specs=[whole()] * (parts * len(sets) + 1) + unread(after),
        out_specs=whole(),
        compiler_params=params(),
        cost_estimate=cost(1e6, 1e6),
        name="norm",
    )(*sum(sets, []), gain, *after)


def hidden_kernel(part, x_ref, gate_ref, up_ref, *refs):
    if part is None:
        hidden_ref = refs[-1]
    else:
        hidden_ref, weight_ref, sem = refs[-3:]
        count = weight_ref.shape[0]
        copy = pltpu.make_async_copy(refs[0].at[0, 2, pl.ds(part * count, count)], weight_ref, sem)
        copy.start()
    width = gate_ref.shape[1]
    size = 256 if width % 256 == 0 else width
    for i in range(width // size):
        cut = slice(i * size, (i + 1) * size)
        gate = jnp.dot(x_ref[...], gate_ref[:, cut], preferred_element_type=F32)
        up = jnp.dot(x_ref[...], up_ref[:, cut], preferred_element_type=F32)
        hidden_ref[:, cut] = (gate * sigmoid(gate) * up).astype(BF16)
    if part is not None:
        copy.wait()


def hidden_units(x, gate, up, after, experts=None, part=None):
    rows, width = x.shape[0], gate.shape[1]
    made = [shaped((rows, width), BF16)]
    extra = []
    if part is not None:
        made.append(shaped((gate.shape[0] // 2, width), BF16))
        extra = [experts]
    return pl.pallas_call(
        functools.partial(hidden_kernel, part),
        out_shape=made,
        in_specs=[whole()] * 3 + [hbm()] * len(extra) + unread(after),
        out_specs=[whole()] * len(made),
        scratch_shapes=[pltpu.SemaphoreType.DMA] * len(extra),
        compiler_params=params(),
        cost_estimate=cost(1e6, 0),
        name="hidden",
    )(x, gate, up, *extra, *after)


def down_kernel(hidden_own_ref, hidden_other_ref, low_ref, high_ref, *refs):
    own_ref, other_ref, hidden_ref = refs[-3:]
    rows = hidden_own_ref.shape[0]
    hidden_ref[:rows, :] = hidden_own_ref[...]
    hidden_ref[rows:, :] = hidden_other_ref[...]
    size = 256
    half = low_ref.shape[0]
    for i in range(2 * half // size):
        cut = slice(i * size, (i + 1) * size)
        down_ref, begin = (low_ref, i * size) if i * size < half else (high_ref, i * size - half)
        product = lax.dot_general(
            hidden_ref[...],
            down_ref[begin : begin + size, :],
            (((1,), (1,)), ((), ())),
            preferred_element_type=F32,
        )
        own_ref[:, cut] = product[:rows]
        other_ref[:, cut] = product[rows:].astype(BF16)


def down_sums(hidden_own, hidden_other, down, after):
    rows, width = hidden_own.shape
    model = 2 * down[0].shape[0]
    return pl.pallas_call(
        down_kernel,
        out_shape=(shaped((rows, model), F32), shaped((rows, model), BF16)),
        in_specs=[whole()] * 4 + unread(after),
        out_specs=[whole()] * 2,
        scratch_shapes=[pltpu.VMEM((2 * rows, width), BF16)],
        compiler_params=params(),
        cost_estimate=cost(1e6, 0),
        name="down",
    )(hidden_own, hidden_other, *down, *after)


def join_kernel(parts, own_ref, other_ref, *refs):
    out_refs = refs[-parts:]
    width = out_refs[0].shape[1]
    own = lax.axis_index("tp")
    for k, ref in enumerate(out_refs):
        cut = pl.ds(pl.multiple_of(jnp.bitwise_xor(own, k) * width, 128), width)
        ref[...] = (own_ref[:, cut] + other_ref[:, cut].astype(F32)).astype(ref.dtype)


def join(parts, own, other, after):
    rows, model = own.shape
    return pl.pallas_call(
        functools.partial(join_kernel, parts),
        out_shape=[shaped((rows, model // parts), BF16 if k else F32) for k in range(parts)],
        in_specs=[whole()] * 2 + unread(after),
        out_specs=[whole()] * parts,
        compiler_params=params(),
        cost_estimate=cost(1e6, 1e6),
        name="join",
    )(own, other, *after)


def total_kernel(parts, *refs):
    total = refs[0][...].astype(F32)
    for ref in refs[1:parts]:
        total = total + ref[...].astype(F32)
    total = total.astype(BF16)
    for j, ref in enumerate(refs[parts:]):
        ref[...] = total[j * CAP : (j + 1) * CAP, :]


def totals(pieces):
    rows, width = pieces[0].shape
    count = rows // CAP
    return pl.pallas_call(
        functools.partial(total_kernel, len(pieces)),
        out_shape=[shaped((CAP, width), BF16)] * count,
        in_specs=[whole()] * len(pieces),
        out_specs=[whole()] * count,
        compiler_params=params(),
        cost_estimate=cost(1e6, 1e6),
        name="totals",
    )(*pieces)


def blend_kernel(begin, count, *refs):
    back = refs[:count]
    base_ref, first_ref, second_ref, gates_ref, out_ref, rows_ref = refs[count:]
    for j, ref in enumerate(back):
        rows_ref[j * CAP : (j + 1) * CAP, :] = ref[...]
    rows = rows_ref[...]
    gates = jnp.transpose(gates_ref[...])
    cut = slice(begin, begin + count * CAP)
    moe = gates[:, 0:1] * jnp.dot(first_ref[:, cut], rows, preferred_element_type=F32)
    moe = moe + gates[:, 1:2] * jnp.dot(second_ref[:, cut], rows, preferred_element_type=F32)
    out_ref[...] = (base_ref[...].astype(F32) + moe).astype(out_ref.dtype)


def blend(begin, back, base, first, second, gates, dtype):
    count, width = len(back), base.shape[1]
    return pl.pallas_call(
        functools.partial(blend_kernel, begin, count),
        out_shape=shaped(base.shape, dtype),
        in_specs=[whole()] * (count + 4),
        out_specs=whole(),
        scratch_shapes=[pltpu.VMEM((count * CAP, width), BF16)],
        compiler_params=params(),
        cost_estimate=cost(1e6, 1e6),
        name="blend",
    )(*back, base, first, second, gates)


def body(
    conv_in,
    gate_in,
    residual,
    conv_weight,
    conv_bias,
    proj_weight,
    step_weight,
    step_bias,
    decay_log,
    skip_gain,
    out_weight,
    norm_gain,
    expert_ids,
    route_gates,
    expert_weight,
):
    tp, experts = lax.axis_size("tp"), lax.axis_size("exp")
    local = conv_in[0]
    before = lax.ppermute(local, "ctx", [(0, 1)])
    expert_weight = stay(expert_weight)
    near = load(stay(local), stay(conv_weight), stay(conv_bias[None]), stay(proj_weight.T))
    xconv, part = conv(before, *near)
    parts = [part] + [swap(part, "tp", k) for k in range(tp - 1, 0, -1)]
    silu, rates, skipped, bias, step_w, out_w, quarter, gain = prepare(
        tp, xconv, stay(gate_in[0]), stay(decay_log), stay(residual[0]), stay(skip_gain[None]),
        stay(step_bias[None]), stay(step_weight), stay(out_weight), stay(norm_gain[None]),
    )
    y, elapsed, seen, state, up_w = scan(parts, xconv, rates, bias, step_w, expert_weight)
    before = lax.ppermute(state, "ctx", [(0, 1)])
    own, *sent = mix(tp, seen, y, elapsed, rates, before, skipped, silu, quarter, out_w)
    arrived = swaps(sent)
    first, second, chooser, gate_w = route(expert_ids[0].T, experts, expert_weight)
    stream, *picked = pick(own, arrived, chooser)
    half = experts // 2
    rows = [picked[0]] + [swap(picked[j], "exp", j) for j in range(1, experts)]
    piece_b = stack(rows[:half], [])
    both = order([rows[experts - 1], piece_b])
    first_a = rows[half]
    second_a = rows[experts - 1] if half == 2 else stack(rows[half + 1 :], [])
    sets = [[piece] + swaps([piece] * (tp - 1)) for piece in (first_a, second_a, piece_b)]
    x_a = norm(sets[:2], gain, [both])
    own_a, low = hidden_units(x_a, gate_w, up_w, [], expert_weight, 0)
    other_a, high = hidden_units(swap(x_a, "ctx", 1), gate_w, up_w, [own_a, order([x_a])], expert_weight, 1)
    down_w = (low, high)
    sum_a, sent_a = down_sums(own_a, other_a, down_w, [])
    sent_a = swap(sent_a, "ctx", 1)
    x_b = norm(sets[2:], gain, [sum_a])
    own_b, = hidden_units(x_b, gate_w, up_w, [])
    joined_a = join(tp, sum_a, sent_a, [own_b])
    made_a = totals([joined_a[0]] + swaps(joined_a[1:]))
    other_b, = hidden_units(swap(x_b, "ctx", 1), gate_w, up_w, [joined_a[0]])
    sum_b, sent_b = down_sums(own_b, other_b, down_w, [])
    joined_b = join(tp, sum_b, swap(sent_b, "ctx", 1), [order([sent_b, made_a[0]])])
    made_b = totals([joined_b[0]] + swaps(joined_b[1:]))
    back_a = [swap(piece, "exp", j) for j, piece in enumerate(made_a, half)]
    back_b = [made_b[0]] + [swap(made_b[j], "exp", j) for j in range(1, half)]
    gates = route_gates[0].T
    return blend(0, back_b + back_a, stream, first, second, gates, BF16)[None]


def solution(mesh):
    placed = (
        P("exp", "ctx", "tp"),
        P("exp", "ctx", "tp"),
        P("exp", "ctx", None),
        P(None, "tp"),
        P("tp"),
        P("tp", None),
        P(None, "tp"),
        P("tp"),
        P(None, "tp"),
        P("tp"),
        P("tp", None),
        P(),
        P("exp", "ctx", None),
        P("exp", "ctx", None),
        P("exp", None, None, ("ctx", "tp")),
    )
    return jax.shard_map(
        body, mesh=mesh, in_specs=placed, out_specs=P("exp", "ctx", "tp"), check_vma=False
    )
```

```python
import functools
import math

import jax
import jax.numpy as jnp
from jax import lax
from jax.experimental import pallas as pl
from jax.experimental.pallas import tpu as pltpu
from jax.sharding import PartitionSpec as P

STATE = 16
DT_RANK = 256
CAP = 64
LOG2E = math.log2(math.e)
VMEM_LIMIT = 20 * 1024 * 1024
F32 = jnp.float32
BF16 = jnp.bfloat16


def params():
    return pltpu.CompilerParams(vmem_limit_bytes=VMEM_LIMIT)


def whole():
    return pl.BlockSpec(memory_space=pltpu.VMEM)


def shaped(shape, dtype):
    return jax.ShapeDtypeStruct(shape, dtype)


def swap(block, axis, k):
    return lax.ppermute(block, axis, [(i, i ^ k) for i in range(lax.axis_size(axis))])


def swaps(blocks):
    return [swap(block, "tp", k) for k, block in enumerate(blocks, 1)]


def sigmoid(x):
    return 1.0 / (1.0 + jnp.exp2(x * -LOG2E))


def stay(array):
    return pltpu.with_memory_space_constraint(array, pltpu.HBM)


def hbm():
    return pl.BlockSpec(memory_space=pltpu.HBM)


def unread(arrays):
    return [pl.BlockSpec(memory_space=pl.ANY)] * len(arrays)


def stack_kernel(count, *refs):
    for j, ref in enumerate(refs[:count]):
        rows = ref.shape[0]
        refs[-1][j * rows : (j + 1) * rows, :] = ref[...]


def stack(pieces, after):
    rows, width = pieces[0].shape
    return pl.pallas_call(
        functools.partial(stack_kernel, len(pieces)),
        out_shape=shaped((rows * len(pieces), width), pieces[0].dtype),
        in_specs=[whole()] * len(pieces) + unread(after),
        out_specs=whole(),
        compiler_params=params(),
        cost_estimate=cost(1e6, 0),
        name="stack",
    )(*pieces, *after)


def order_kernel(*refs):
    refs[-1][...] = jnp.zeros_like(refs[-1])


def order(after):
    return pl.pallas_call(
        order_kernel,
        out_shape=shaped((8, 128), F32),
        in_specs=unread(after),
        out_specs=whole(),
        compiler_params=params(),
        cost_estimate=cost(2e10, 0),
        name="order",
    )(*after)


def cost(flops, loaded=0):
    return pl.CostEstimate(flops=int(flops), bytes_accessed=int(loaded), transcendentals=0)


def route_kernel(ids_ref, expert_hbm, first_ref, second_ref, chooser_ref, weight_ref, sem):
    copy = pltpu.make_async_copy(expert_hbm.at[0, 0], weight_ref, sem)
    copy.start()
    rows, slots = first_ref.shape
    own = lax.axis_index("exp")
    ids = jnp.transpose(ids_ref[...].astype(F32)).astype(jnp.int32)
    lanes = lax.broadcasted_iota(jnp.int32, (rows, 128), 1)
    hot = [(ids[:, i : i + 1] == lanes).astype(F32) for i in range(2)]
    earlier = lax.broadcasted_iota(jnp.int32, (rows, rows), 1) < lax.broadcasted_iota(
        jnp.int32, (rows, rows), 0
    )
    ranks = jnp.dot(
        earlier.astype(F32).astype(BF16), (hot[0] + hot[1]).astype(BF16), preferred_element_type=F32
    )
    places = lax.broadcasted_iota(jnp.int32, (rows, slots), 1)
    tables = []
    for i in range(2):
        slot = jnp.sum(ranks * hot[i], axis=1, keepdims=True).astype(jnp.int32)
        place = jnp.bitwise_xor(ids[:, i : i + 1], own) * CAP + slot
        tables.append((place == places).astype(F32))
    first_ref[...] = tables[0].astype(BF16)
    second_ref[...] = tables[1].astype(BF16)
    chooser_ref[...] = jnp.transpose(tables[0] + tables[1]).astype(BF16)
    copy.wait()


def route(ids, expert_count, experts):
    rows, slots = ids.shape[1], expert_count * CAP
    return pl.pallas_call(
        route_kernel,
        out_shape=(
            shaped((rows, slots), BF16),
            shaped((rows, slots), BF16),
            shaped((slots, rows), BF16),
            shaped(experts.shape[2:], BF16),
        ),
        in_specs=[whole(), hbm()],
        out_specs=[whole()] * 4,
        scratch_shapes=[pltpu.SemaphoreType.DMA],
        compiler_params=params(),
        cost_estimate=cost(1e6, 8e6),
        name="route",
    )(ids, experts)


def conv_kernel(before_ref, x_ref, taps_ref, bias_ref, weight_ref, xconv_ref, part_ref, ext_ref):
    rows = x_ref.shape[0]
    halo = 16
    count = taps_ref.shape[0]
    ext_ref[:halo, :] = before_ref[rows - halo :, :].astype(F32)
    ext_ref[halo:, :] = x_ref[...].astype(F32)
    total = bias_ref[...] + taps_ref[count - 1 : count, :] * ext_ref[halo:, :]
    for k in range(count - 1):
        start = halo - (count - 1) + k
        total = total + taps_ref[k : k + 1, :] * ext_ref[start : start + rows, :]
    xconv = (total * sigmoid(total)).astype(BF16)
    xconv_ref[...] = xconv
    across = (((1,), (1,)), ((), ()))
    part_ref[:rows, :] = lax.dot_general(
        xconv, weight_ref[:DT_RANK, :], across, preferred_element_type=F32
    ).astype(BF16)
    maps = lax.dot_general(
        weight_ref[DT_RANK:, :], xconv, across, preferred_element_type=F32
    ).astype(BF16)
    part_ref[rows:, :rows] = maps[:STATE]
    part_ref[rows:, rows:] = maps[STATE:]


def conv(before, x, taps, bias, weight):
    rows, channels = x.shape
    return pl.pallas_call(
        conv_kernel,
        out_shape=(shaped((rows, channels), BF16), shaped((rows + STATE, DT_RANK), BF16)),
        in_specs=[whole()] * 5,
        out_specs=[whole()] * 2,
        scratch_shapes=[pltpu.VMEM((16 + rows, channels), F32)],
        compiler_params=params(),
        cost_estimate=cost(1e6, 1e6),
        name="conv",
    )(before, x, taps, bias, weight)


def load_kernel(count, *refs):
    copies = [
        pltpu.make_async_copy(refs[i], refs[count + i], refs[-1].at[i]) for i in range(count)
    ]
    for copy in copies:
        copy.start()
    for copy in copies:
        copy.wait()


def load(*arrays):
    count = len(arrays)
    return pl.pallas_call(
        functools.partial(load_kernel, count),
        out_shape=[shaped(array.shape, array.dtype) for array in arrays],
        in_specs=[hbm()] * count,
        out_specs=[whole()] * count,
        scratch_shapes=[pltpu.SemaphoreType.DMA((count,))],
        compiler_params=params(),
        cost_estimate=cost(1e6, 2e6),
        name="load",
    )(*arrays)


def prepare_kernel(
    xconv_ref, gate_hbm, decay_hbm, residual_hbm, skip_hbm, bias_hbm, step_hbm, out_hbm, gain_hbm,
    silu_ref, rates_ref, skipped_ref, bias_ref, step_ref, out_ref, quarter_ref, gain_ref,
    gate_ref, decay_ref, residual_ref, skip_ref, sems,
):
    copies = [
        pltpu.make_async_copy(source, target, sems.at[i])
        for i, (source, target) in enumerate(
            (
                (gate_hbm, gate_ref),
                (decay_hbm, decay_ref),
                (residual_hbm, residual_ref),
                (skip_hbm, skip_ref),
                (bias_hbm, bias_ref),
                (gain_hbm, gain_ref),
                (step_hbm, step_ref),
                (out_hbm, out_ref),
            )
        )
    ]
    for copy in copies:
        copy.start()
    for copy in copies[:4]:
        copy.wait()
    gate = gate_ref[...].astype(F32)
    silu_ref[...] = gate * sigmoid(gate)
    skipped_ref[...] = skip_ref[...] * xconv_ref[...].astype(F32)
    rates = -LOG2E * jnp.exp(decay_ref[...])
    for j in range(rates_ref.shape[1]):
        rates_ref[:, j, :] = rates[:, j * 128 : (j + 1) * 128]
    width = quarter_ref.shape[1]
    start = pl.multiple_of(lax.axis_index("tp") * width, 128)
    quarter_ref[...] = residual_ref[:, pl.ds(start, width)].astype(F32)
    for copy in copies[4:]:
        copy.wait()


def prepare(parts, xconv, gate, decay_log, residual, skip, bias, step_weight, out_weight, gain):
    rows, channels = gate.shape
    return pl.pallas_call(
        prepare_kernel,
        out_shape=(
            shaped((rows, channels), F32),
            shaped((STATE, channels // 128, 128), F32),
            shaped((rows, channels), F32),
            shaped(bias.shape, F32),
            shaped(step_weight.shape, BF16),
            shaped(out_weight.shape, BF16),
            shaped((rows, residual.shape[1] // parts), F32),
            shaped(gain.shape, F32),
        ),
        in_specs=[whole()] + [hbm()] * 8,
        out_specs=[whole()] * 8,
        scratch_shapes=[
            pltpu.VMEM((rows, channels), BF16),
            pltpu.VMEM(decay_log.shape, F32),
            pltpu.VMEM(residual.shape, BF16),
            pltpu.VMEM(skip.shape, F32),
            pltpu.SemaphoreType.DMA((8,)),
        ],
        compiler_params=params(),
        cost_estimate=cost(1e6, 6e6),
        name="prepare",
    )(xconv, gate, decay_log, residual, skip, bias, step_weight, out_weight, gain)


def scan_kernel(parts, *refs):
    part_refs = refs[:parts]
    xconv_ref, rates_ref, bias_ref, weight_ref, expert_hbm = refs[parts : parts + 5]
    y_ref, elapsed_ref, seen_ref, state_ref, second_ref = refs[parts + 5 : parts + 10]
    steps_ref, driven_ref, spread_ref, expert_sem = refs[parts + 10 :]
    rows = xconv_ref.shape[0]
    tiles = rates_ref.shape[1]
    expert_copy = pltpu.make_async_copy(expert_hbm.at[0, 1], second_ref, expert_sem)
    expert_copy.start()
    proj = part_refs[0][...].astype(F32)
    for ref in part_refs[1:]:
        proj = proj + ref[...].astype(F32)
    maps = proj[rows:]

    for t in range(rows):
        spread_ref[t] = jnp.broadcast_to(maps[:, t : t + 1], (STATE, 128))
        seen_ref[t] = jnp.broadcast_to(maps[:, rows + t : rows + t + 1], (STATE, 128))
    rank = proj[:rows].astype(BF16)
    raw = jnp.dot(rank, weight_ref[...], preferred_element_type=F32) + bias_ref[...]
    steps = jnp.maximum(raw, 0.0) + jnp.log1p(jnp.exp(-jnp.abs(raw)))
    driven = steps * xconv_ref[...].astype(F32)
    for j in range(tiles):
        cut = slice(j * 128, (j + 1) * 128)
        steps_ref[:, j, :] = steps[:, cut]
        driven_ref[:, j, :] = driven[:, cut]

    def step(t, carry):
        elapsed, states = carry
        now, driven = steps_ref[t], driven_ref[t]
        sums = [None, None]
        new = []
        for n in range(STATE):
            state = jnp.exp2(now * rates_ref[n]) * states[n] + driven * spread_ref[t, n : n + 1, :]
            new.append(state)
            term = state * seen_ref[t, n : n + 1, :]
            sums[n % 2] = term if sums[n % 2] is None else sums[n % 2] + term
        elapsed = elapsed + now
        y_ref[t] = sums[0] + sums[1]
        elapsed_ref[t] = elapsed
        return elapsed, tuple(new)

    zero = jnp.zeros((tiles, 128), F32)
    _, states = lax.fori_loop(0, rows, step, (zero, (zero,) * STATE), unroll=32)
    for n in range(STATE):
        state_ref[n] = states[n]
    expert_copy.wait()


def scan(pieces, xconv, rates, bias, weight, experts):
    rows = xconv.shape[0]
    tall = (rows, *rates.shape[1:])
    return pl.pallas_call(
        functools.partial(scan_kernel, len(pieces)),
        out_shape=(
            shaped(tall, F32),
            shaped(tall, F32),
            shaped((rows, STATE, 128), F32),
            shaped(rates.shape, F32),
            shaped(experts.shape[2:], BF16),
        ),
        in_specs=[whole()] * (len(pieces) + 4) + [hbm()],
        out_specs=[whole()] * 5,
        scratch_shapes=[
            pltpu.VMEM(tall, F32),
            pltpu.VMEM(tall, F32),
            pltpu.VMEM((rows, STATE, 128), F32),
            pltpu.SemaphoreType.DMA,
        ],
        compiler_params=params(),
        cost_estimate=cost(1e6, 14e6),
        name="scan",
    )(*pieces, xconv, rates, bias, weight, experts)


def project(total_ref, skipped_ref, silu_ref, quarter_ref, weight_ref, own_ref, sent, gated_ref):
    for j in range(total_ref.shape[1]):
        cut = slice(j * 128, (j + 1) * 128)
        total = total_ref[:, j, :] + skipped_ref[:, cut]
        gated_ref[:, cut] = (total * silu_ref[:, cut]).astype(BF16)
    own = lax.axis_index("tp")
    width = own_ref.shape[1]
    for k in range(len(sent) + 1):
        start = pl.multiple_of(jnp.bitwise_xor(own, k) * width, 128)
        product = jnp.dot(
            gated_ref[...], weight_ref[:, pl.ds(start, width)], preferred_element_type=F32
        )
        if k == 0:
            own_ref[...] = product + quarter_ref[...]
        else:
            sent[k - 1][...] = product.astype(BF16)


def mix_first_kernel(parts, y_ref, skipped_ref, silu_ref, quarter_ref, weight_ref, *refs):
    @pl.when(lax.axis_index("ctx") == 0)
    def _():
        project(y_ref, skipped_ref, silu_ref, quarter_ref, weight_ref, refs[0], refs[1:parts], refs[parts])


def mix_kernel(parts, *refs):
    seen_ref, y_ref, elapsed_ref, rates_ref, state_ref, skipped_ref, silu_ref, quarter_ref, weight_ref = refs[:9]
    own_ref, sent = refs[9 + parts], refs[10 + parts : 9 + 2 * parts]
    sum_ref, gated_ref = refs[9 + 2 * parts :]
    rows = y_ref.shape[0]

    def step(t, carry):
        elapsed = elapsed_ref[t]
        sums = [y_ref[t], None]
        for n in range(STATE):
            term = jnp.exp2(elapsed * rates_ref[n]) * (state_ref[n] * seen_ref[t, n : n + 1, :])
            sums[n % 2] = term if sums[n % 2] is None else sums[n % 2] + term
        sum_ref[t] = sums[0] + sums[1]
        return carry

    @pl.when(lax.axis_index("ctx") > 0)
    def _():
        lax.fori_loop(0, rows, step, 0, unroll=8)
        project(sum_ref, skipped_ref, silu_ref, quarter_ref, weight_ref, own_ref, sent, gated_ref)


def mix(parts, seen, y, elapsed, rates, state, skipped, silu, quarter, weight):
    rows, tiles, _ = y.shape
    width = weight.shape[1] // parts
    made = [shaped((rows, width), F32)] + [shaped((rows, width), BF16)] * (parts - 1)
    started = pl.pallas_call(
        functools.partial(mix_first_kernel, parts),
        out_shape=made,
        in_specs=[whole()] * 5,
        out_specs=[whole()] * parts,
        scratch_shapes=[pltpu.VMEM((rows, tiles * 128), BF16)],
        compiler_params=params(),
        cost_estimate=cost(3e9, 0),
        name="mix_first",
    )(y, skipped, silu, quarter, weight)
    return pl.pallas_call(
        functools.partial(mix_kernel, parts),
        out_shape=made,
        in_specs=[whole()] * (9 + parts),
        out_specs=[whole()] * parts,
        input_output_aliases={9 + i: i for i in range(parts)},
        scratch_shapes=[
            pltpu.VMEM((rows, tiles, 128), F32),
            pltpu.VMEM((rows, tiles * 128), BF16),
        ],
        compiler_params=params(),
        cost_estimate=cost(1e6, 12e6),
        name="mix",
    )(seen, y, elapsed, rates, state, skipped, silu, quarter, weight, *started)


def pick_kernel(parts, *refs):
    own_ref, arrived, chooser_ref = refs[0], refs[1:parts], refs[parts]
    stream_ref, out_refs = refs[parts + 1], refs[parts + 2 :]
    total = own_ref[...]
    for ref in arrived:
        total = total + ref[...].astype(F32)
    stream = total.astype(BF16)
    stream_ref[...] = stream
    picked = jnp.dot(chooser_ref[...], stream, preferred_element_type=F32).astype(BF16)
    for j, ref in enumerate(out_refs):
        ref[...] = picked[j * CAP : (j + 1) * CAP, :]


def pick(own, arrived, chooser):
    rows, width = own.shape
    experts = chooser.shape[0] // CAP
    return pl.pallas_call(
        functools.partial(pick_kernel, 1 + len(arrived)),
        out_shape=[shaped((rows, width), BF16)] + [shaped((CAP, width), BF16)] * experts,
        in_specs=[whole()] * (2 + len(arrived)),
        out_specs=[whole()] * (1 + experts),
        compiler_params=params(),
        cost_estimate=cost(1e6, 1e6),
        name="pick",
    )(own, *arrived, chooser)


def norm_kernel(parts, count, *refs):
    gain_ref, out_ref = refs[parts * count], refs[-1]
    own = lax.axis_index("tp")
    begin = 0
    for i in range(count):
        pieces = [ref[...].astype(F32) for ref in refs[i * parts : (i + 1) * parts]]
        rows, width = pieces[0].shape
        total = sum(jnp.sum(piece * piece, axis=1, keepdims=True) for piece in pieces)
        scale = lax.rsqrt(total / (width * parts) + 1e-6)
        for k, piece in enumerate(pieces):
            start = pl.multiple_of(jnp.bitwise_xor(own, k) * width, 128)
            out_ref[begin : begin + rows, pl.ds(start, width)] = (
                piece * scale * gain_ref[:, pl.ds(start, width)]
            ).astype(BF16)
        begin += rows


def norm(sets, gain, after):
    parts = len(sets[0])
    rows, width = sum(pieces[0].shape[0] for pieces in sets), sets[0][0].shape[1]
    return pl.pallas_call(
        functools.partial(norm_kernel, parts, len(sets)),
        out_shape=shaped((rows, width * parts), BF16),
        in_specs=[whole()] * (parts * len(sets) + 1) + unread(after),
        out_specs=whole(),
        compiler_params=params(),
        cost_estimate=cost(1e6, 1e6),
        name="norm",
    )(*sum(sets, []), gain, *after)


def hidden_kernel(part, x_ref, gate_ref, up_ref, *refs):
    if part is None:
        hidden_ref = refs[-1]
    else:
        hidden_ref, weight_ref, sem = refs[-3:]
        count = weight_ref.shape[0]
        copy = pltpu.make_async_copy(refs[0].at[0, 2, pl.ds(part * count, count)], weight_ref, sem)
        copy.start()
    width = gate_ref.shape[1]
    size = 256 if width % 256 == 0 else width
    for i in range(width // size):
        cut = slice(i * size, (i + 1) * size)
        gate = jnp.dot(x_ref[...], gate_ref[:, cut], preferred_element_type=F32)
        up = jnp.dot(x_ref[...], up_ref[:, cut], preferred_element_type=F32)
        hidden_ref[:, cut] = (gate * sigmoid(gate) * up).astype(BF16)
    if part is not None:
        copy.wait()


def hidden_units(x, gate, up, after, experts=None, part=None):
    rows, width = x.shape[0], gate.shape[1]
    made = [shaped((rows, width), BF16)]
    extra = []
    if part is not None:
        made.append(shaped((gate.shape[0] // 2, width), BF16))
        extra = [experts]
    return pl.pallas_call(
        functools.partial(hidden_kernel, part),
        out_shape=made,
        in_specs=[whole()] * 3 + [hbm()] * len(extra) + unread(after),
        out_specs=[whole()] * len(made),
        scratch_shapes=[pltpu.SemaphoreType.DMA] * len(extra),
        compiler_params=params(),
        cost_estimate=cost(1e6, 0),
        name="hidden",
    )(x, gate, up, *extra, *after)


def down_kernel(hidden_own_ref, hidden_other_ref, low_ref, high_ref, *refs):
    own_ref, other_ref, hidden_ref = refs[-3:]
    rows = hidden_own_ref.shape[0]
    hidden_ref[:rows, :] = hidden_own_ref[...]
    hidden_ref[rows:, :] = hidden_other_ref[...]
    size = 256
    half = low_ref.shape[0]
    for i in range(2 * half // size):
        cut = slice(i * size, (i + 1) * size)
        down_ref, begin = (low_ref, i * size) if i * size < half else (high_ref, i * size - half)
        product = lax.dot_general(
            hidden_ref[...],
            down_ref[begin : begin + size, :],
            (((1,), (1,)), ((), ())),
            preferred_element_type=F32,
        )
        own_ref[:, cut] = product[:rows]
        other_ref[:, cut] = product[rows:].astype(BF16)


def down_sums(hidden_own, hidden_other, down, after):
    rows, width = hidden_own.shape
    model = 2 * down[0].shape[0]
    return pl.pallas_call(
        down_kernel,
        out_shape=(shaped((rows, model), F32), shaped((rows, model), BF16)),
        in_specs=[whole()] * 4 + unread(after),
        out_specs=[whole()] * 2,
        scratch_shapes=[pltpu.VMEM((2 * rows, width), BF16)],
        compiler_params=params(),
        cost_estimate=cost(1e6, 0),
        name="down",
    )(hidden_own, hidden_other, *down, *after)


def join_kernel(parts, own_ref, other_ref, *refs):
    out_refs = refs[-parts:]
    width = out_refs[0].shape[1]
    own = lax.axis_index("tp")
    for k, ref in enumerate(out_refs):
        cut = pl.ds(pl.multiple_of(jnp.bitwise_xor(own, k) * width, 128), width)
        ref[...] = (own_ref[:, cut] + other_ref[:, cut].astype(F32)).astype(ref.dtype)


def join(parts, own, other, after):
    rows, model = own.shape
    return pl.pallas_call(
        functools.partial(join_kernel, parts),
        out_shape=[shaped((rows, model // parts), BF16 if k else F32) for k in range(parts)],
        in_specs=[whole()] * 2 + unread(after),
        out_specs=[whole()] * parts,
        compiler_params=params(),
        cost_estimate=cost(1e6, 1e6),
        name="join",
    )(own, other, *after)


def total_kernel(parts, *refs):
    total = refs[0][...].astype(F32)
    for ref in refs[1:parts]:
        total = total + ref[...].astype(F32)
    total = total.astype(BF16)
    for j, ref in enumerate(refs[parts:]):
        ref[...] = total[j * CAP : (j + 1) * CAP, :]


def totals(pieces):
    rows, width = pieces[0].shape
    count = rows // CAP
    return pl.pallas_call(
        functools.partial(total_kernel, len(pieces)),
        out_shape=[shaped((CAP, width), BF16)] * count,
        in_specs=[whole()] * len(pieces),
        out_specs=[whole()] * count,
        compiler_params=params(),
        cost_estimate=cost(1e6, 1e6),
        name="totals",
    )(*pieces)


def blend_kernel(begin, count, *refs):
    back = refs[:count]
    base_ref, first_ref, second_ref, gates_ref, out_ref, rows_ref = refs[count:]
    for j, ref in enumerate(back):
        rows_ref[j * CAP : (j + 1) * CAP, :] = ref[...]
    rows = rows_ref[...]
    gates = jnp.transpose(gates_ref[...])
    cut = slice(begin, begin + count * CAP)
    moe = gates[:, 0:1] * jnp.dot(first_ref[:, cut], rows, preferred_element_type=F32)
    moe = moe + gates[:, 1:2] * jnp.dot(second_ref[:, cut], rows, preferred_element_type=F32)
    out_ref[...] = (base_ref[...].astype(F32) + moe).astype(out_ref.dtype)


def blend(begin, back, base, first, second, gates, dtype):
    count, width = len(back), base.shape[1]
    return pl.pallas_call(
        functools.partial(blend_kernel, begin, count),
        out_shape=shaped(base.shape, dtype),
        in_specs=[whole()] * (count + 4),
        out_specs=whole(),
        scratch_shapes=[pltpu.VMEM((count * CAP, width), BF16)],
        compiler_params=params(),
        cost_estimate=cost(1e6, 1e6),
        name="blend",
    )(*back, base, first, second, gates)


def body(
    conv_in,
    gate_in,
    residual,
    conv_weight,
    conv_bias,
    proj_weight,
    step_weight,
    step_bias,
    decay_log,
    skip_gain,
    out_weight,
    norm_gain,
    expert_ids,
    route_gates,
    expert_weight,
):
    tp, experts = lax.axis_size("tp"), lax.axis_size("exp")
    local = conv_in[0]
    before = lax.ppermute(local, "ctx", [(0, 1)])
    expert_weight = stay(expert_weight)
    near = load(stay(local), stay(conv_weight), stay(conv_bias[None]), stay(proj_weight.T))
    xconv, part = conv(before, *near)
    parts = [part] + [swap(part, "tp", k) for k in range(tp - 1, 0, -1)]
    silu, rates, skipped, bias, step_w, out_w, quarter, gain = prepare(
        tp, xconv, stay(gate_in[0]), stay(decay_log), stay(residual[0]), stay(skip_gain[None]),
        stay(step_bias[None]), stay(step_weight), stay(out_weight), stay(norm_gain[None]),
    )
    y, elapsed, seen, state, up_w = scan(parts, xconv, rates, bias, step_w, expert_weight)
    before = lax.ppermute(state, "ctx", [(0, 1)])
    own, *sent = mix(tp, seen, y, elapsed, rates, before, skipped, silu, quarter, out_w)
    arrived = swaps(sent)
    first, second, chooser, gate_w = route(expert_ids[0].T, experts, expert_weight)
    stream, *picked = pick(own, arrived, chooser)
    half = experts // 2
    rows = [picked[0]] + [swap(picked[j], "exp", j) for j in range(1, experts)]
    piece_b = stack(rows[:half], [])
    both = order([rows[experts - 1], piece_b])
    first_a = rows[half]
    second_a = rows[experts - 1] if half == 2 else stack(rows[half + 1 :], [])
    sets = [[piece] + swaps([piece] * (tp - 1)) for piece in (first_a, second_a, piece_b)]
    x_a = norm(sets[:2], gain, [both])
    own_a, low = hidden_units(x_a, gate_w, up_w, [], expert_weight, 0)
    other_a, high = hidden_units(swap(x_a, "ctx", 1), gate_w, up_w, [own_a, order([x_a])], expert_weight, 1)
    down_w = (low, high)
    sum_a, sent_a = down_sums(own_a, other_a, down_w, [])
    sent_a = swap(sent_a, "ctx", 1)
    x_b = norm(sets[2:], gain, [sum_a])
    own_b, = hidden_units(x_b, gate_w, up_w, [])
    joined_a = join(tp, sum_a, sent_a, [own_b])
    made_a = totals([joined_a[0]] + swaps(joined_a[1:]))
    other_b, = hidden_units(swap(x_b, "ctx", 1), gate_w, up_w, [joined_a[0]])
    sum_b, sent_b = down_sums(own_b, other_b, down_w, [])
    joined_b = join(tp, sum_b, swap(sent_b, "ctx", 1), [order([sent_b, made_a[0]])])
    made_b = totals([joined_b[0]] + swaps(joined_b[1:]))
    back_a = [swap(piece, "exp", j) for j, piece in enumerate(made_a, half)]
    back_b = [made_b[0]] + [swap(made_b[j], "exp", j) for j in range(1, half)]
    gates = route_gates[0].T
    return blend(0, back_b + back_a, stream, first, second, gates, BF16)[None]


def solution(mesh):
    placed = (
        P("exp", "ctx", "tp"),
        P("exp", "ctx", "tp"),
        P("exp", "ctx", None),
        P(None, "tp"),
        P("tp"),
        P("tp", None),
        P(None, "tp"),
        P("tp"),
        P(None, "tp"),
        P("tp"),
        P("tp", None),
        P(),
        P("exp", "ctx", None),
        P("exp", "ctx", None),
        P("exp", None, None, ("ctx", "tp")),
    )
    return jax.shard_map(
        body, mesh=mesh, in_specs=placed, out_specs=P("exp", "ctx", "tp"), check_vma=False
    )
```
